32 devices in a mesh: groups: 2 (over y), seq: 4 (over z), res: 2 (over x), sub: 2 (over core).
Axes of the slice: x: 2, y: 2, z: 4, core: 2. Of those that a mesh axis runs over, the one named last changes fastest.
Arguments:
- alignment_input: bfloat16 [64, 512, 64], P(('groups', 'seq'), ('res', 'sub')), parts along dimension 0
- pair_features: bfloat16 [1024, 512, 128], P(('groups', 'seq'), ('res', 'sub')), parts along dimension 0
- update_cotangent: bfloat16 [64, 512, 64], P(('groups', 'seq'), ('res', 'sub')), parts along dimension 0, may hold values from -6 to 6
- alignment_norm_gain: bfloat16 [64], replicated, may hold values from 0.099609375 to 1.8984375
- pair_norm_gain: bfloat16 [128], replicated, may hold values from 0.099609375 to 1.8984375
- value_matrix: bfloat16 [64, 256], replicated, may hold values from -0.75 to 0.75
- gate_matrix: bfloat16 [64, 256], replicated, may hold values from -0.75 to 0.75
- output_matrix: bfloat16 [256, 64], replicated, may hold values from -0.375 to 0.375
- head_bias_matrix: bfloat16 [128, 8], replicated
- sequence_mask: int32 [64], P(('groups', 'seq')), parts along dimension 0, may hold values from 0 to 1, as said below
- token_padding_mask: int32 [1024], P(('groups', 'res', 'sub')), parts along dimension 0, may hold values from 0 to 1, as said below
Outputs:
- alignment_update: bfloat16 [64, 512, 64], P(('groups', 'seq'), ('res', 'sub')), parts along dimension 0
- alignment_gradient: bfloat16 [64, 512, 64], P(('groups', 'seq'), ('res', 'sub')), parts along dimension 0
- pair_gradient: bfloat16 [1024, 512, 128], P(('groups', 'seq'), ('res', 'sub')), parts along dimension 0
The draws below stay inside these ranges and needn't reach their ends.
There are 2 independent parts, one for each index of `groups`. The reference program is written for one: setup_inputs(seed, part) draws one part's arguments, and reference() takes and returns one part's arrays. A program takes and returns all parts, laid end to end along the dimension named above; an argument that names none is the same for every part. Nothing has to cross between parts.
Inputs may be any that keep to these rules, and one draw needn't show every extreme that they name: `sequence_mask`: the first sequence is 1 and the last sequence is 0. `token_padding_mask`: 1 for the first tokens and 0 for all after them; at least the first half is 1 and the last token is 0.
All inputs are finite; a program needn't handle non-finite values.
Results may differ from the reference program's by a relative error of at most 0.014.
Values may be sent and summed in bfloat16 or wider, within the bound.
No kernel may reach another device: no remote copies, remote signals or barrier semaphores. Data moves between devices by JAX's collectives and lax.ppermute only.
A program may use at most 128 MiB of HBM per device.

```python
import math
import jax
import jax.numpy as jnp
from jax import lax

HEAD_TOTAL = 8
HEAD_CHANNELS = 32
ALIGNMENT_WIDTH = 64
PAIR_WIDTH = 128
SEQ_DEV = 8
ALIGNED_SEQUENCES = 32
TOKEN_TOTAL = 512


def shared_layout(key):
    key = jax.random.fold_in(key, 101)
    sign_key, head_key = jax.random.split(key)
    signs = (2 * jax.random.randint(sign_key, (PAIR_WIDTH,), 0, 2) - 1).astype(jnp.float32)
    order = jax.random.permutation(head_key, HEAD_TOTAL)
    chosen_heads = (order < HEAD_TOTAL // 2).astype(jnp.float32)
    owner = jnp.arange(PAIR_WIDTH) // (PAIR_WIDTH // HEAD_TOTAL)
    ownership = (owner[:, None] == jnp.arange(HEAD_TOTAL)[None, :]).astype(jnp.float32)
    return (signs, chosen_heads, ownership)


def draw_alignment_input(key, part):
    key = jax.random.fold_in(key, 15)
    common = jax.random.normal(jax.random.fold_in(key, 1), (ALIGNMENT_WIDTH,), jnp.float32)
    noise = jax.random.normal(jax.random.fold_in(key, 2), (ALIGNED_SEQUENCES, TOKEN_TOTAL, ALIGNMENT_WIDTH), jnp.float32)
    return (common[None, None, :] + noise).astype(jnp.bfloat16)


def draw_pair_features(key, part):
    signs, chosen_heads, ownership = shared_layout(key)
    key = jax.random.fold_in(key, 11)
    array_shape = (TOKEN_TOTAL, TOKEN_TOTAL, PAIR_WIDTH)
    base_key = jax.random.fold_in(key, 0)
    common_key = jax.random.fold_in(key, 3)
    common = jax.random.normal(common_key, (PAIR_WIDTH,), jnp.float32)
    lifted = signs * jnp.dot(ownership, chosen_heads)
    position = jnp.arange(TOKEN_TOTAL)
    same_token = (position[:, None] == position[None, :]).astype(jnp.float32)
    noise = jax.random.normal(base_key, array_shape, jnp.float32)
    field = (common[None, None, :] + 0.03 * noise + 0.27 * same_token[:, :, None] * lifted[None, None, :]) * 0.03
    return field.astype(jnp.bfloat16)


def draw_head_bias_matrix(key, part):
    signs, chosen_heads, ownership = shared_layout(key)
    key = jax.random.fold_in(key, 12)
    noise = jax.random.normal(key, (PAIR_WIDTH, HEAD_TOTAL), jnp.float32)
    field = (noise + 20.0 * ownership * signs[:, None]) / math.sqrt(PAIR_WIDTH)
    return field.astype(jnp.bfloat16)


def draw_sequence_mask(key, part):
    key = jax.random.fold_in(key, 13)
    picks = jax.random.randint(key, (ALIGNED_SEQUENCES,), 0, 4)
    position = jnp.arange(ALIGNED_SEQUENCES)
    used = jnp.where(position == 0, 1, jnp.where(position == ALIGNED_SEQUENCES - 1, 0, (picks > 0).astype(jnp.int32)))
    return used.astype(jnp.int32)


def draw_token_padding_mask(key, part):
    key = jax.random.fold_in(key, 14)
    used_entries = jax.random.randint(key, (), TOKEN_TOTAL // 2, TOKEN_TOTAL)
    return (jnp.arange(TOKEN_TOTAL) < used_entries).astype(jnp.int32)


def shard_levels(rng, shape, shards, low, high):
    loudness = 1.0
    for dim, shards_of in shards:
        steps = jax.random.uniform(jax.random.fold_in(jax.random.fold_in(rng, 6), dim), (shards_of,), jnp.float32, low / len(shards), high / len(shards))
        loudness = loudness * jnp.repeat(jnp.exp(steps), shape[dim] // shards_of).reshape((-1,) + (1,) * (len(shape) - 1 - dim))
    return loudness


def bell_draw(own_key, dims, spread, reach, cuts=(), held_as=jnp.bfloat16):
    entries = spread * jax.random.normal(own_key, dims, jnp.float32)
    if cuts:
        entries = entries * shard_levels(own_key, dims, cuts, -0.22, 0.18)
    return jnp.clip(entries, -reach, reach).astype(held_as)


def setup_inputs(seed: int = 0, part: int = 0) -> dict:
    key_of = jax.random.split(jax.random.key(seed), 12)
    part_splits = jax.random.split(jax.random.fold_in(key_of[11], part), 12)
    return {
        "alignment_input": draw_alignment_input(jax.random.fold_in(jax.random.fold_in(key_of[11], part), 71), part),
        "pair_features": draw_pair_features(jax.random.fold_in(jax.random.fold_in(key_of[11], part), 71), part),
        "update_cotangent": bell_draw(part_splits[2], (ALIGNED_SEQUENCES, TOKEN_TOTAL, ALIGNMENT_WIDTH), 1.0, 6.0, ((0, 4), (1, 4))),
        "alignment_norm_gain": jnp.clip(1.0 + 0.18 * jax.random.normal(key_of[3], (ALIGNMENT_WIDTH,), jnp.float32), 0.099609375, 1.8984375).astype(jnp.bfloat16),
        "pair_norm_gain": jnp.clip(1.0 + 0.18 * jax.random.normal(key_of[4], (PAIR_WIDTH,), jnp.float32), 0.099609375, 1.8984375).astype(jnp.bfloat16),
        "value_matrix": bell_draw(key_of[5], (ALIGNMENT_WIDTH, HEAD_TOTAL * HEAD_CHANNELS), ALIGNMENT_WIDTH ** -0.5, 0.75),
        "gate_matrix": bell_draw(key_of[6], (ALIGNMENT_WIDTH, HEAD_TOTAL * HEAD_CHANNELS), ALIGNMENT_WIDTH ** -0.5, 0.75),
        "output_matrix": bell_draw(key_of[7], (HEAD_TOTAL * HEAD_CHANNELS, ALIGNMENT_WIDTH), (HEAD_TOTAL * HEAD_CHANNELS) ** -0.5, 0.375),
        "head_bias_matrix": draw_head_bias_matrix(jax.random.fold_in(key_of[11], 71), part),
        "sequence_mask": draw_sequence_mask(jax.random.fold_in(jax.random.fold_in(key_of[11], part), 71), part),
        "token_padding_mask": draw_token_padding_mask(jax.random.fold_in(jax.random.fold_in(key_of[11], part), 71), part),
    }


def layer_normalize(inputs, gain):
    center = inputs - lax.optimization_barrier(jnp.mean(inputs, axis=-1, keepdims=True))
    inverse = lax.rsqrt(lax.optimization_barrier(jnp.mean(center * center, axis=-1, keepdims=True)) + 1e-05)
    scaled = center * inverse
    return (scaled * gain, scaled, inverse)

def recover_normalized(scaled, inverse, gain, incoming):
    grads = incoming * gain
    mean_grad = lax.optimization_barrier(jnp.mean(grads, axis=-1, keepdims=True))
    mean_cross = lax.optimization_barrier(jnp.mean(grads * scaled, axis=-1, keepdims=True))
    return inverse * (grads - mean_grad - scaled * mean_cross)

def matrix_multiply(left_side, right_side):
    flat = left_side.reshape(-1, left_side.shape[-1])
    product = jnp.dot(flat, right_side, preferred_element_type=jnp.float32)
    return product.reshape(left_side.shape[:-1] + (right_side.shape[-1],))

def reference(alignment_input, pair_features, update_cotangent, alignment_norm_gain, pair_norm_gain, value_matrix, gate_matrix, output_matrix, head_bias_matrix, sequence_mask, token_padding_mask):
    sequence_total = alignment_input.shape[0]
    token_total = alignment_input.shape[1]
    hidden = HEAD_TOTAL * HEAD_CHANNELS
    normed_complete, alignment_scaled, alignment_inverse_deviation = layer_normalize(alignment_input.astype(jnp.float32), alignment_norm_gain.astype(jnp.float32))
    normed_alignment = normed_complete.astype(jnp.bfloat16)
    value_rows = matrix_multiply(normed_alignment, value_matrix).astype(jnp.bfloat16)
    gate_activation = jax.nn.sigmoid(matrix_multiply(normed_alignment, gate_matrix))
    normed_pair, pair_scaled, pair_inverse = layer_normalize(pair_features.astype(jnp.float32), pair_norm_gain.astype(jnp.float32))
    padding = 1000000000.0 * (token_padding_mask.astype(jnp.float32) - 1.0)
    logits = jnp.einsum('ijk,kh->hij', normed_pair, head_bias_matrix.astype(jnp.float32), precision=lax.Precision.HIGHEST) + padding[None, None, :]
    probs = jax.nn.softmax(logits, axis=-1)
    weights = probs.astype(jnp.bfloat16)
    split_values = value_rows.reshape(sequence_total, token_total, HEAD_TOTAL, HEAD_CHANNELS).astype(jnp.float32)
    mixed = jnp.einsum('hij,sjhc->sihc', weights.astype(jnp.float32), split_values).reshape(sequence_total, token_total, hidden)
    gated_output = (mixed * gate_activation).astype(jnp.bfloat16)
    active_entries = (sequence_mask[:, None] * token_padding_mask[None, :]).astype(jnp.float32)[:, :, None]
    alignment_update = (matrix_multiply(gated_output, output_matrix) * active_entries).astype(jnp.bfloat16)
    upstream = (update_cotangent.astype(jnp.float32) * active_entries).astype(jnp.bfloat16)
    d_gated = matrix_multiply(upstream, output_matrix.T)
    d_mixed = (d_gated * gate_activation).astype(jnp.bfloat16)
    gating_gradient = (d_gated * mixed * gate_activation * (1.0 - gate_activation)).astype(jnp.bfloat16)
    split_grads = d_mixed.reshape(sequence_total, token_total, HEAD_TOTAL, HEAD_CHANNELS).astype(jnp.float32)
    value_gradient = jnp.einsum('hij,sihc->sjhc', weights.astype(jnp.float32), split_grads)
    value_gradient = value_gradient.reshape(sequence_total, token_total, hidden).astype(jnp.bfloat16)
    block_count = sequence_total // SEQ_DEV
    grad_blocks = split_grads.reshape(block_count, SEQ_DEV, token_total, HEAD_TOTAL, HEAD_CHANNELS)
    value_blocks = split_values.reshape(block_count, SEQ_DEV, token_total, HEAD_TOTAL, HEAD_CHANNELS)

    def accumulate(running, operands):
        grad_block, value_block = operands
        partial_sum = jnp.einsum('sihc,sjhc->hij', grad_block, value_block)
        rounded = lax.optimization_barrier(partial_sum.astype(jnp.bfloat16))
        return (running + rounded.astype(jnp.float32), None)
    d_scores, _ = lax.scan(accumulate, jnp.zeros((HEAD_TOTAL, token_total, token_total), jnp.float32), (grad_blocks, value_blocks))
    row_totals = lax.optimization_barrier(jnp.sum(probs * d_scores, axis=-1, keepdims=True))
    d_logits = probs * (d_scores - row_totals)
    d_normed_pair = jnp.einsum('hij,kh->ijk', d_logits, head_bias_matrix.astype(jnp.float32), precision=lax.Precision.HIGHEST)
    pair_gradient = recover_normalized(pair_scaled, pair_inverse, pair_norm_gain.astype(jnp.float32), d_normed_pair).astype(jnp.bfloat16)
    normed_alignment_gradient = matrix_multiply(value_gradient, value_matrix.T) + matrix_multiply(gating_gradient, gate_matrix.T)
    alignment_gradient = recover_normalized(alignment_scaled, alignment_inverse_deviation, alignment_norm_gain.astype(jnp.float32), normed_alignment_gradient).astype(jnp.bfloat16)
    return (alignment_update, alignment_gradient, pair_gradient)
```

```python
import functools

import jax
import jax.numpy as jnp
from jax import lax
from jax.experimental import pallas as pl
from jax.experimental.pallas import tpu as pltpu
from jax.sharding import PartitionSpec as P

F32 = jnp.float32
BF16 = jnp.bfloat16
EPS = 1e-05
QUAD = 4
GROUP = 4
SLOTS = 32
VMEM = 56 * 1024 * 1024


def dot(a, b):
    return jnp.dot(a, b, preferred_element_type=F32)


def dot_nt(a, b):
    return lax.dot_general(a, b, (((1,), (1,)), ((), ())), preferred_element_type=F32)


def dot_tn(a, b):
    return lax.dot_general(a, b, (((0,), (0,)), ((), ())), preferred_element_type=F32)


def iota(shape, dim):
    return lax.broadcasted_iota(jnp.int32, shape, dim)


def split3(value):
    high = value.astype(BF16).astype(F32)
    rest = value - high
    middle = rest.astype(BF16).astype(F32)
    return high, middle, rest - middle


def split2(value):
    high = value.astype(BF16)
    return high, (value - high.astype(F32)).astype(BF16)


def call(kernel, out_shape, name, scratch=(), flops=10_000_000, scalars=0, operands=(), grid=None, in_specs=None, out_specs=None):
    whole = pl.BlockSpec(memory_space=pltpu.VMEM)
    if in_specs is None:
        in_specs = [pl.BlockSpec(memory_space=pltpu.SMEM)] * scalars + [whole] * (len(operands) - scalars)
        out_specs = [whole] * len(out_shape)
    extra = {} if grid is None else {"grid": grid}
    moved = sum(o.size * o.dtype.itemsize for o in operands) + sum(
        o.size * o.dtype.itemsize for o in out_shape
    )
    return pl.pallas_call(
        kernel,
        out_shape=out_shape,
        in_specs=in_specs,
        out_specs=out_specs,
        scratch_shapes=list(scratch),
        compiler_params=pltpu.CompilerParams(vmem_limit_bytes=VMEM),
        cost_estimate=pl.CostEstimate(flops=flops, bytes_accessed=moved, transcendentals=0),
        name=name,
        **extra,
    )(*operands)


def shape(dims, dtype):
    return jax.ShapeDtypeStruct(tuple(dims), dtype)


def spread(matrix, channels, depth):
    hidden = matrix.shape[1]
    wide = hidden * QUAD
    row, col = iota((hidden, wide), 0), iota((hidden, wide), 1)
    pick = (row // depth == col // (depth * QUAD)) & (row % depth == col % depth)
    placed = dot(matrix, pick.astype(F32).astype(BF16))
    tall = jnp.concatenate([placed] * QUAD, axis=0)
    row, col = iota(tall.shape, 0), iota(tall.shape, 1)
    return jnp.where(row // channels == (col // depth) % QUAD, tall, 0.0).astype(BF16)


def weights_kernel(
    depth, value_ref, gate_ref, output_ref, bias_ref, gain_ref,
    spread_value, spread_gate, spread_output, moments, squares, centers, back,
):
    channels = value_ref.shape[0]
    spread_value[...] = spread(value_ref[...], channels, depth)
    spread_gate[...] = spread(gate_ref[...], channels, depth)
    spread_output[...] = spread(output_ref[...], channels, depth)
    scaled = bias_ref[...].astype(F32) * gain_ref[...].astype(F32)
    heads, width = scaled.shape
    total = jnp.sum(scaled, axis=1, keepdims=True)
    centers[...] = jnp.broadcast_to(total, (heads, width))
    high, middle, low = split3(scaled)
    tail = (SLOTS - 3 * heads, width)
    row = iota(tail, 0)
    slots = jnp.concatenate([high, middle, low, jnp.where(row < 4, 1.0, 0.0)], axis=0)
    square_slots = jnp.concatenate(
        [jnp.zeros((3 * heads, width), F32), jnp.where(row >= 4, 1.0, 0.0)], axis=0
    )

    def diagonal(tile):
        tall = jnp.concatenate([tile] * GROUP, axis=0)
        full = jnp.concatenate([tall] * GROUP, axis=1)
        row, col = iota(full.shape, 0), iota(full.shape, 1)
        return jnp.where(row // SLOTS == col // tile.shape[1], full, 0.0).astype(BF16)

    moments[...] = diagonal(slots)
    squares[...] = diagonal(square_slots)
    high, middle, _ = split3(scaled - total * (1.0 / width))
    left = jnp.concatenate([high, middle, high, jnp.where(row < 3, 1.0, 0.0)], axis=0)
    right = jnp.concatenate(
        [jnp.zeros((3 * heads, width), F32), jnp.where((row >= 3) & (row < 6), 1.0, 0.0)], axis=0
    )
    back[...] = diagonal(jnp.concatenate([left, right], axis=1))


def side_by_side(ref, pair, channels):
    col = iota((channels, 2 * channels), 1)
    row = iota((channels, 2 * channels), 0)
    first = (col == row).astype(F32).astype(BF16)
    second = (col == row + channels).astype(F32).astype(BF16)
    return dot(ref[2 * pair], first) + dot(ref[2 * pair + 1], second)


def averaging(channels):
    row, col = iota((2 * channels, 2 * channels), 0), iota((2 * channels, 2 * channels), 1)
    return jnp.where(row // channels == col // channels, 1.0 / channels, 0.0).astype(BF16)


def average(value, mean_matrix):
    high, low = split2(value)
    return dot(high, mean_matrix) + dot(low, mean_matrix)


def normalized(value, mean_matrix):
    center = value - dot(value.astype(BF16), mean_matrix)
    inverse = lax.rsqrt(average(center * center, mean_matrix) + EPS)
    return center * inverse, inverse


def column(row_value, lanes):
    return jnp.transpose(jnp.broadcast_to(row_value, (lanes, row_value.shape[1])))


def first_kernel(dims, place_ref, seq_mask_ref, x_ref, u_ref, gain_ref, token_ref, spread_out, *messages):
    Z, R, rows, ways, width, lanes = dims
    channels = x_ref.shape[2]
    mean_matrix = averaging(channels)
    live = column(token_ref[...].astype(F32), 2 * channels)
    gain = gain_ref[...].astype(F32)
    second_half = iota(live.shape, 1) >= channels
    normed, masked = [], []
    for pair in range(x_ref.shape[0] // 2):
        scaled, _ = normalized(side_by_side(x_ref, pair, channels), mean_matrix)
        normed.append((scaled * gain).astype(BF16))
        keep = jnp.where(second_half, seq_mask_ref[2 * pair + 1], seq_mask_ref[2 * pair]).astype(F32)
        masked.append((side_by_side(u_ref, pair, channels) * keep * live).astype(BF16))
    per = width // (2 * channels)
    normed = [jnp.concatenate(normed[x * per : (x + 1) * per], axis=1) for x in range(R)]
    masked = [jnp.concatenate(masked[x * per : (x + 1) * per], axis=1) for x in range(R)]
    for z in range(Z):
        for x in range(R):
            spread_out[z * R + x] = normed[x]
    turn = place_ref[0]
    for k, message in enumerate(messages):
        for e in range(ways):
            part, x = e // R, e % R

            @pl.when(lax.rem(turn + k, ways) == e)
            def _():
                message[0:rows] = normed[x][part * rows : (part + 1) * rows]
                message[rows : 2 * rows] = masked[x][part * rows : (part + 1) * rows]


def pair_kernel(heads, x_ref, moments, squares, centers, token_ref, e_ref, logit_ref, mean_ref, inverse_ref, scratch, stat):
    count, columns, width = x_ref.shape
    groups = count // GROUP
    x = x_ref[...].reshape(groups, GROUP, columns, width)
    parts, highs, lows = [], [], []
    for g in range(GROUP):
        part = x[:, g].reshape(groups * columns, width)
        value = part.astype(F32)
        high, low = split2(value * value)
        parts.append(part)
        highs.append(high)
        lows.append(low)
    both = squares[...]
    product = (
        dot_nt(jnp.concatenate(parts, axis=1), moments[...])
        + dot_nt(jnp.concatenate(highs, axis=1), both)
        + dot_nt(jnp.concatenate(lows, axis=1), both)
    )
    padding = 1000000000.0 * (token_ref[...].astype(F32) - 1.0)
    center = centers[...]
    for group in range(groups):
        turned = jnp.transpose(product[group * columns : (group + 1) * columns])
        for g in range(GROUP):
            i = group * GROUP + g
            base = g * SLOTS
            raw = (
                turned[base : base + heads]
                + turned[base + heads : base + 2 * heads]
                + turned[base + 2 * heads : base + 3 * heads]
            )
            total = turned[base + 3 * heads : base + 3 * heads + 1]
            square = turned[base + 3 * heads + 4 : base + 3 * heads + 5]
            mean = total * (1.0 / width)
            upper = total.astype(BF16).astype(F32)
            lower = total - upper
            spread_sum = (square - upper * upper * (1.0 / width)) - (
                2.0 * upper * lower + lower * lower
            ) * (1.0 / width)
            inverse = lax.rsqrt(jnp.maximum(spread_sum, 0.0) * (1.0 / width) + EPS)
            scratch[i * heads : (i + 1) * heads] = inverse * (raw - mean * center)
            mean_ref[i : i + 1] = mean
            inverse_ref[i : i + 1] = inverse
    lane = iota((count, columns), 1)
    stats = jnp.zeros((count, columns), F32)
    for h in range(heads):
        logit = scratch[pl.ds(h, count, stride=heads), :]
        logit_ref[h] = logit
        logit = logit + padding
        peak = jnp.max(logit, axis=1, keepdims=True)
        e = jnp.exp(logit - peak).astype(BF16)
        e_ref[h] = e
        total = jnp.sum(e.astype(F32), axis=1, keepdims=True)
        for t, part in enumerate(split3(peak)):
            stats = jnp.where(lane == t * heads + h, part, stats)
        for t, part in enumerate(split3(total)):
            stats = jnp.where(lane == (t + 3) * heads + h, part, stats)
    e_ref[heads] = stats.astype(BF16)


def joined_thirds(stats, heads):
    lanes = stats.shape[1]
    return (
        stats
        + pltpu.roll(stats, lanes - heads, 1)
        + pltpu.roll(stats, lanes - 2 * heads, 1)
    )


def quads_of(dims, place_ref, own, other, scratch):
    Z, R, rows, ways, width, lanes = dims
    core, slot = place_ref[1], place_ref[2]
    for plane in range(Z):
        half, n = plane // ways, plane % ways
        k = lax.rem(slot - n + ways, ways)
        for index in range(ways):
            for mine, refs in ((True, own), (False, other)):

                @pl.when((k == index) & ((core == half) if mine else (core != half)))
                def _():
                    scratch[plane] = refs[index][...]


def quad_rows(dims, scratch, quad, low):
    Z, R, rows, ways, width, lanes = dims
    per = lanes // width
    return jnp.concatenate(
        [scratch[quad * per + g, low : low + rows] for g in range(per)], axis=1
    )


def rows_kernel(dims, heads, place_ref, *refs):
    Z, R, rows, ways, width, lanes = dims
    refs = list(refs)
    own, refs = refs[:ways], refs[ways:]
    other, refs = refs[:ways], refs[ways:]
    exps, refs = refs[:R], refs[R:]
    far, refs = refs[:R], refs[R:]
    value_ref, gate_ref, output_ref = refs[:3]
    partial_out, mixed_grad, probs, scales, gathered, turned = refs[3:]
    columns = exps[0].shape[2]
    quads_of(dims, place_ref, own, other, gathered)
    x_place = place_ref[3]
    near = [joined_thirds(e[heads].astype(F32), heads) for e in exps]
    away = [joined_thirds(s[...].astype(F32), heads) for s in far]
    everything = near + away
    peak = functools.reduce(jnp.maximum, everything)
    total = 0.0
    for s in everything:
        total = total + jnp.exp(s - peak) * pltpu.roll(s, s.shape[1] - 3 * heads, 1)
    for r in range(R):
        scale = jnp.exp(near[r] - peak) / total
        scales[r] = scale
        at = pl.multiple_of(lax.rem(x_place + r, R) * columns, columns)
        for h in range(heads):
            weight = exps[r][h].astype(F32) * scale[:, h : h + 1]
            probs[h, :, pl.ds(at, columns)] = weight.astype(BF16)
    quads = Z * width // lanes
    step = value_ref.shape[1] // heads
    for q in range(quads):
        gate = jax.nn.sigmoid(dot(quad_rows(dims, gathered, q, 0), gate_ref[...]))
        grad = dot(quad_rows(dims, gathered, q, rows), output_ref[...])
        product = (gate * grad).astype(BF16)
        for h in range(heads):
            mixed_grad[h, :, q * step : (q + 1) * step] = product[:, h * step : (h + 1) * step]
    for h in range(heads):
        grads = dot_tn(probs[h], mixed_grad[h]).astype(BF16)
        for q in range(quads):
            turned[q, :, h * step : (h + 1) * step] = grads[:, q * step : (q + 1) * step]
    for q in range(quads):
        partial = dot_nt(turned[q], value_ref[...]).astype(BF16)
        per = lanes // width
        for g in range(per):
            for x in range(R):
                partial_out[(q * per + g) * R + x] = partial[
                    x * columns : (x + 1) * columns, g * width : (g + 1) * width
                ]


def scores_kernel(dims, heads, place_ref, x_ref, value_ref, mixed_grad, scales, *refs):
    Z, R, rows, ways, width, lanes = dims
    exps, refs = refs[:R], refs[R:]
    values, own_scores = refs[:2]
    messages = refs[2 : 1 + R]
    scratch = refs[1 + R]
    columns = exps[0].shape[2]
    x_place = place_ref[3]
    quads, per = Z * width // lanes, lanes // width
    step = value_ref.shape[1] // heads
    for q in range(quads):
        tokens = [
            jnp.concatenate([x_ref[(q * per + g) * R + x] for g in range(per)], axis=1)
            for x in range(R)
        ]
        product = dot(jnp.concatenate(tokens, axis=0), value_ref[...]).astype(BF16)
        for h in range(heads):
            values[h, :, q * step : (q + 1) * step] = product[:, h * step : (h + 1) * step]
    lane = iota((rows, columns), 1)
    sums = jnp.zeros((rows, columns), F32)
    for h in range(heads):
        scratch[...] = dot_nt(mixed_grad[h], values[h])
        total = 0.0
        for r in range(R):
            at = pl.multiple_of(lax.rem(x_place + r, R) * columns, columns)
            part = scratch[:, pl.ds(at, columns)]
            if r == 0:
                own_scores[h] = part
            else:
                part = part.astype(BF16)
                messages[r - 1][h] = part
                part = part.astype(F32)
            weight = exps[r][h].astype(F32) * scales[r][:, h : h + 1]
            total = total + jnp.sum(weight * part, axis=1, keepdims=True)
        for t, part in enumerate(split3(total)):
            sums = jnp.where(lane == t * heads + h, part, sums)
    for message in messages:
        message[heads] = sums.astype(BF16)


def mixed_kernel(dims, heads, place_ref, *refs):
    Z, R, rows, ways, width, lanes = dims
    own, refs = refs[:ways], refs[ways:]
    other, refs = refs[:ways], refs[ways:]
    values, probs, gate_ref, output_ref, keep, send, gathered, turned, sums = refs
    quads_of(dims, place_ref, own, other, gathered)
    quads, per = Z * width // lanes, lanes // width
    step = gate_ref.shape[1] // heads
    for h in range(heads):
        mixed = dot(probs[h], values[h])
        for q in range(quads):
            turned[q, :, h * step : (h + 1) * step] = mixed[:, q * step : (q + 1) * step]
    for q in range(quads):
        mixed = turned[q]
        gate = jax.nn.sigmoid(dot(quad_rows(dims, gathered, q, 0), gate_ref[...]))
        grad = dot(quad_rows(dims, gathered, q, rows), output_ref[...])
        gated = mixed * gate
        update = dot_nt(gated.astype(BF16), output_ref[...])
        gate_grad = (grad * gated * (1.0 - gate)).astype(BF16)
        through_gate = dot_nt(gate_grad, gate_ref[...])
        for g in range(per):
            sums[q * per + g, 0:rows] = update[:, g * width : (g + 1) * width]
            sums[q * per + g, rows : 2 * rows] = through_gate[:, g * width : (g + 1) * width]
    core = place_ref[1]
    keep[...] = sums[pl.ds(core * ways, ways)]
    send[...] = sums[pl.ds((1 - core) * ways, ways)].astype(BF16)


def reply_kernel(dims, place_ref, keep, received, *messages):
    Z, R, rows, ways, width, lanes = dims
    slot = place_ref[2]
    for k, message in enumerate(messages):
        n = lax.rem(slot - k + ways, ways)
        message[...] = (keep[n] + received[n].astype(F32)).astype(BF16)


def pair_back_kernel(R, heads, x_ref, logit_ref, mean_ref, inverse_ref, e_ref, scale_ref, own_ref, back_ref, *refs):
    received, refs = refs[: R - 1], refs[R - 1 :]
    totals, refs = refs[: R + 1], refs[R + 1 :]
    out_ref, scratch = refs
    count, columns, width = x_ref.shape
    total = sum(t[0].astype(F32) for t in totals) + sum(m[heads].astype(F32) for m in received)
    total = joined_thirds(total, heads)
    scale = scale_ref[0]
    inverse = inverse_ref[...]
    cross = 0.0
    for h in range(heads):
        scores = own_ref[h]
        for m in received:
            scores = scores + m[h].astype(F32)
        prob = e_ref[h].astype(F32) * scale[:, h : h + 1]
        grad = prob * (scores - total[:, h : h + 1])
        cross = cross + grad * logit_ref[h]
        scaled = grad * inverse
        high = scaled.astype(BF16).astype(F32)
        scratch[pl.ds(h, count, stride=SLOTS), :] = high
        scratch[pl.ds(heads + h, count, stride=SLOTS), :] = high
        scratch[pl.ds(2 * heads + h, count, stride=SLOTS), :] = scaled - high
    factor = inverse * inverse * cross * (1.0 / width)
    rest = list(split3(factor * mean_ref[...])) + list(split3(factor))
    rest += [jnp.zeros_like(factor)] * (SLOTS - 3 * heads - len(rest))
    for t, part in enumerate(rest):
        scratch[pl.ds(3 * heads + t, count, stride=SLOTS), :] = part
    back = back_ref[...]
    for group in range(count // GROUP):
        tile = scratch[group * GROUP * SLOTS : (group + 1) * GROUP * SLOTS]
        product = dot(jnp.transpose(tile).astype(BF16), back)
        for g in range(GROUP):
            i = group * GROUP + g
            plain = product[:, 2 * g * width : (2 * g + 1) * width]
            slope = product[:, (2 * g + 1) * width : (2 * g + 2) * width]
            out_ref[i] = (plain - slope * x_ref[i].astype(F32)).astype(BF16)


def last_kernel(dims, place_ref, seq_mask_ref, x_ref, gain_ref, token_ref, partial_ref, *refs):
    Z, R, rows, ways, width, lanes = dims
    messages, refs = refs[:ways], refs[ways:]
    update_ref, grad_ref, updates, through = refs
    channels = x_ref.shape[2]
    turn = place_ref[0]
    for k, message in enumerate(messages):
        for e in range(ways):
            part, x = e // R, e % R

            @pl.when(lax.rem(turn + k, ways) == e)
            def _():
                at = slice(part * rows, (part + 1) * rows), slice(x * width, (x + 1) * width)
                updates[at] = message[0:rows].astype(F32)
                through[at] = message[rows : 2 * rows].astype(F32)

    mean_matrix = averaging(channels)
    live = column(token_ref[...].astype(F32), 2 * channels)
    gain = gain_ref[...].astype(F32)
    second_half = iota(live.shape, 1) >= channels
    row, col = iota((2 * channels, channels), 0), iota((2 * channels, channels), 1)
    first = (row == col).astype(F32).astype(BF16)
    second = (row == col + channels).astype(F32).astype(BF16)
    for x in range(R):
        grads = through[:, x * width : (x + 1) * width]
        for z in range(Z):
            grads = grads + partial_ref[z * R + x].astype(F32)
        for p in range(width // (2 * channels)):
            pair = x * (width // (2 * channels)) + p
            at = slice(p * 2 * channels, (p + 1) * 2 * channels)
            scaled, inverse = normalized(side_by_side(x_ref, pair, channels), mean_matrix)
            grad = grads[:, at] * gain
            grad = inverse * (
                grad - average(grad, mean_matrix) - scaled * average(grad * scaled, mean_matrix)
            )
            grad = grad.astype(BF16)
            keep = jnp.where(second_half, seq_mask_ref[2 * pair + 1], seq_mask_ref[2 * pair]).astype(F32)
            update = updates[:, pair * 2 * channels : (pair + 1) * 2 * channels] * keep * live
            update = update.astype(BF16)
            for s, pick in enumerate((first, second)):
                grad_ref[2 * pair + s] = dot(grad, pick).astype(BF16)
                update_ref[2 * pair + s] = dot(update, pick).astype(BF16)


def shards(
    Z, R, C,
    alignment_input, pair_features, update_cotangent, alignment_norm_gain, pair_norm_gain,
    value_matrix, gate_matrix, output_matrix, head_bias_matrix, sequence_mask, token_padding_mask,
):
    sequences, columns, channels = alignment_input.shape
    rows, _, pair_width = pair_features.shape
    heads = head_bias_matrix.shape[1]
    hidden = value_matrix.shape[1]
    depth = hidden // heads
    ways = Z // C
    width = sequences // R * channels
    lanes = QUAD * channels
    step = QUAD * depth
    quads = Z * width // lanes
    dims = (Z, R, rows, ways, width, lanes)
    parts = columns // rows
    z, x, c = lax.axis_index("seq"), lax.axis_index("res"), lax.axis_index("sub")
    place = jnp.stack([z % ways, c, (z % parts) * R + x, x]).astype(jnp.int32)
    everyone = ("seq", "res", "sub")

    def device(z, x, c):
        return (z * R + x) * C + c

    def owner_moves(k):
        moves = []
        for plane in range(Z):
            for block in range(R * C):
                e = (plane % ways + k) % ways
                to = device(block * parts + e // R, e % R, plane // ways)
                moves.append((device(plane, block // C, block % C), to))
        return moves

    swap = [(i, C - 1 - i) for i in range(C)]

    def along_res(value, k):
        return lax.ppermute(value, "res", [((i + k) % R, i) for i in range(R)])

    other_core = lambda value: lax.ppermute(value, "sub", swap)

    gain2 = jnp.concatenate([alignment_norm_gain] * 2).reshape(1, 2 * channels)
    token_row = token_padding_mask.reshape(1, columns)
    message = shape((2 * rows, width), BF16)

    first = call(
        functools.partial(first_kernel, dims),
        [shape((Z * R, columns, width), BF16)] + [message] * ways,
        "first",
        scalars=2,
        operands=(place, sequence_mask, alignment_input, update_cotangent, gain2, token_row),
    )
    outgoing, to_rows = first[0], first[1:]
    own = [lax.ppermute(m, everyone, owner_moves(k)) for k, m in enumerate(to_rows)]
    everywhere = lax.all_to_all(outgoing, ("seq", "res"), 0, 0, tiled=True)
    other = [other_core(m) for m in own]

    spread_value, spread_gate, spread_output, moments, squares, centers, back = call(
        functools.partial(weights_kernel, depth),
        [shape((lanes, hidden * QUAD), BF16)] * 3
        + [shape((GROUP * SLOTS, GROUP * pair_width), BF16)] * 2
        + [shape((heads, pair_width), F32), shape((GROUP * SLOTS, 2 * GROUP * pair_width), BF16)],
        "weights",
        operands=(
            value_matrix, gate_matrix, output_matrix.T, head_bias_matrix.T,
            pair_norm_gain.reshape(1, pair_width),
        ),
    )

    block = min(32, rows)
    steps = rows // block
    whole = pl.BlockSpec(memory_space=pltpu.VMEM)
    by_row = lambda *tail: pl.BlockSpec((block, *tail), lambda i: (i,) + (0,) * len(tail))
    by_middle = lambda lead: pl.BlockSpec((lead, block, columns), lambda i: (0, i, 0))
    exps, logits, means, inverses = call(
        functools.partial(pair_kernel, heads),
        [
            shape((heads + 1, rows, columns), BF16),
            shape((heads, rows, columns), F32),
            shape((rows, columns), F32),
            shape((rows, columns), F32),
        ],
        "pair",
        operands=(pair_features, moments, squares, centers, token_row),
        scratch=[pltpu.VMEM((block * heads, columns), F32), pltpu.VMEM((block, columns), F32)],
        grid=(steps,),
        in_specs=[by_row(columns, pair_width)] + [whole] * 4,
        out_specs=[by_middle(heads + 1), by_middle(heads), by_row(columns), by_row(columns)],
    )
    exps = [exps] + [along_res(exps, k) for k in range(1, R)]
    far = [other_core(e[heads]) for e in exps]

    partial, mixed_grad, probs, scales = call(
        functools.partial(rows_kernel, dims, heads),
        [
            shape((Z * R, columns, width), BF16),
            shape((heads, rows, quads * step), BF16),
            shape((heads, rows, R * columns), BF16),
            shape((R, rows, columns), F32),
        ],
        "rows",
        scalars=1,
        operands=(place, *own, *other, *exps, *far, spread_value, spread_gate, spread_output),
        scratch=[
            pltpu.VMEM((Z, 2 * rows, width), BF16),
            pltpu.VMEM((quads, R * columns, heads * step), BF16),
        ],
    )
    collected = lax.all_to_all(partial, ("seq", "res"), 0, 0, tiled=True)

    values, own_scores, *score_messages = call(
        functools.partial(scores_kernel, dims, heads),
        [shape((heads, R * columns, quads * step), BF16), shape((heads, rows, columns), F32)]
        + [shape((heads + 1, rows, columns), BF16)] * (R - 1),
        "scores",
        scalars=1,
        operands=(place, everywhere, spread_value, mixed_grad, scales, *exps),
        scratch=[pltpu.VMEM((rows, R * columns), F32)],
    )
    scores = [along_res(m, R - r) for r, m in enumerate(score_messages, 1)]
    own_total = score_messages[0][heads:]
    totals = [own_total, other_core(own_total)] + [other_core(m[heads:]) for m in scores]

    keep, send = call(
        functools.partial(mixed_kernel, dims, heads),
        [shape((ways, 2 * rows, width), F32), shape((ways, 2 * rows, width), BF16)],
        "mixed",
        scalars=1,
        operands=(place, *own, *other, values, probs, spread_gate, spread_output),
        scratch=[
            pltpu.VMEM((Z, 2 * rows, width), BF16),
            pltpu.VMEM((quads, rows, heads * step), F32),
            pltpu.VMEM((Z, 2 * rows, width), F32),
        ],
    )
    replies = call(
        functools.partial(reply_kernel, dims),
        [message] * ways,
        "reply",
        scalars=1,
        operands=(place, keep, other_core(send)),
    )
    replies = [
        lax.ppermute(m, everyone, [(b, a) for a, b in owner_moves(k)]) for k, m in enumerate(replies)
    ]

    (pair_gradient,) = call(
        functools.partial(pair_back_kernel, R, heads),
        [shape(pair_features.shape, BF16)],
        "pair_back",
        operands=(
            pair_features, logits, means, inverses, exps[0], scales, own_scores, back, *scores, *totals,
        ),
        scratch=[pltpu.VMEM((block * SLOTS, columns), F32)],
        grid=(steps,),
        in_specs=[
            by_row(columns, pair_width), by_middle(heads), by_row(columns), by_row(columns),
            by_middle(heads + 1), by_middle(1), by_middle(heads), whole,
        ]
        + [by_middle(heads + 1)] * (R - 1)
        + [by_middle(1)] * (R + 1),
        out_specs=[by_row(columns, pair_width)],
    )
    alignment_update, alignment_gradient = call(
        functools.partial(last_kernel, dims),
        [shape(alignment_input.shape, BF16)] * 2,
        "last",
        scalars=2,
        operands=(place, sequence_mask, alignment_input, gain2, token_row, collected, *replies),
        scratch=[pltpu.VMEM((columns, R * width), F32), pltpu.VMEM((columns, R * width), F32)],
    )
    return alignment_update, alignment_gradient, pair_gradient


def solution(mesh):
    split = P(("groups", "seq"), ("res", "sub"), None)
    sizes = (mesh.shape["seq"], mesh.shape["res"], mesh.shape["sub"])
    return jax.shard_map(
        functools.partial(shards, *sizes),
        mesh=mesh,
        in_specs=(split, split, split, P(), P(), P(), P(), P(), P())
        + (P(("groups", "seq")), P(("groups", "res", "sub"))),
        out_specs=(split, split, split),
        check_vma=False,
    )
```

```python
import functools

import jax
import jax.numpy as jnp
from jax import lax
from jax.experimental import pallas as pl
from jax.experimental.pallas import tpu as pltpu
from jax.sharding import PartitionSpec as P

F32 = jnp.float32
BF16 = jnp.bfloat16
EPS = 1e-05
QUAD = 4
GROUP = 4
SLOTS = 32
COST = dict(
    first=1.5, pack=0.4, weights=1.3, pair=6.5, pick=0.4, probs=0.8, work=4.0, scores=1.5, finish=0.6,
    pair_back=8.0, fold=0.6, last=2.7,
)
VMEM = 20 * 1024 * 1024


def dot(a, b):
    return jnp.dot(a, b, preferred_element_type=F32)


def dot_nt(a, b):
    return lax.dot_general(a, b, (((1,), (1,)), ((), ())), preferred_element_type=F32)


def dot_tn(a, b):
    return lax.dot_general(a, b, (((0,), (0,)), ((), ())), preferred_element_type=F32)


def iota(shape, dim):
    return lax.broadcasted_iota(jnp.int32, shape, dim)


def split3(value):
    high = value.astype(BF16).astype(F32)
    rest = value - high
    middle = rest.astype(BF16).astype(F32)
    return high, middle, rest - middle


def split2(value):
    high = value.astype(BF16)
    return high, (value - high.astype(F32)).astype(BF16)


def call(kernel, out_shape, name, scratch=(), flops=None, scalars=0, operands=(), grid=None, in_specs=None, out_specs=None):
    whole = pl.BlockSpec(memory_space=pltpu.VMEM)
    if in_specs is None:
        in_specs = [pl.BlockSpec(memory_space=pltpu.SMEM)] * scalars + [whole] * (len(operands) - scalars)
        out_specs = [whole] * len(out_shape)
    extra = {} if grid is None else {"grid": grid}
    moved = sum(o.size * o.dtype.itemsize for o in operands) + sum(
        o.size * o.dtype.itemsize for o in out_shape
    )
    return pl.pallas_call(
        kernel,
        out_shape=out_shape,
        in_specs=in_specs,
        out_specs=out_specs,
        scratch_shapes=list(scratch),
        compiler_params=pltpu.CompilerParams(vmem_limit_bytes=VMEM),
        cost_estimate=pl.CostEstimate(flops=int(COST[name] * 3e9), bytes_accessed=0, transcendentals=0),
        name=name,
        **extra,
    )(*operands)


def shape(dims, dtype):
    return jax.ShapeDtypeStruct(tuple(dims), dtype)


def spread(matrix, channels, depth):
    hidden = matrix.shape[1]
    wide = hidden * QUAD
    row, col = iota((hidden, wide), 0), iota((hidden, wide), 1)
    pick = (row // depth == col // (depth * QUAD)) & (row % depth == col % depth)
    placed = dot(matrix, pick.astype(F32).astype(BF16))
    tall = jnp.concatenate([placed] * QUAD, axis=0)
    row, col = iota(tall.shape, 0), iota(tall.shape, 1)
    return jnp.where(row // channels == (col // depth) % QUAD, tall, 0.0).astype(BF16)


def weights_kernel(
    depth, value_ref, gate_ref, output_ref, bias_ref, gain_ref,
    spread_value, spread_gate, spread_output, moments, squares, centers, back,
):
    channels = value_ref.shape[0]
    spread_value[...] = spread(value_ref[...], channels, depth)
    spread_gate[...] = spread(gate_ref[...], channels, depth)
    spread_output[...] = spread(output_ref[...], channels, depth)
    scaled = bias_ref[...].astype(F32) * gain_ref[...].astype(F32)
    heads, width = scaled.shape
    total = jnp.sum(scaled, axis=1, keepdims=True)
    centers[...] = jnp.broadcast_to(total, (heads, width))
    high, middle, low = split3(scaled)
    tail = (SLOTS - 3 * heads, width)
    row = iota(tail, 0)
    slots = jnp.concatenate([high, middle, low, jnp.where(row < 4, 1.0, 0.0)], axis=0)
    square_slots = jnp.concatenate(
        [jnp.zeros((3 * heads, width), F32), jnp.where(row >= 4, 1.0, 0.0)], axis=0
    )

    def diagonal(tile):
        tall = jnp.concatenate([tile] * GROUP, axis=0)
        full = jnp.concatenate([tall] * GROUP, axis=1)
        row, col = iota(full.shape, 0), iota(full.shape, 1)
        return jnp.where(row // SLOTS == col // tile.shape[1], full, 0.0).astype(BF16)

    moments[...] = diagonal(slots)
    squares[...] = diagonal(square_slots)
    high, middle, _ = split3(scaled - total * (1.0 / width))
    left = jnp.concatenate([high, middle, high, jnp.where(row < 3, 1.0, 0.0)], axis=0)
    right = jnp.concatenate(
        [jnp.zeros((3 * heads, width), F32), jnp.where((row >= 3) & (row < 6), 1.0, 0.0)], axis=0
    )
    back[...] = diagonal(jnp.concatenate([left, right], axis=1))


def side_by_side(ref, pair, channels):
    both = jnp.concatenate([ref[2 * pair], ref[2 * pair + 1]], axis=0)
    return jnp.transpose(both.astype(F32))


def averaging(channels):
    row, col = iota((2 * channels, 2 * channels), 0), iota((2 * channels, 2 * channels), 1)
    return jnp.where(row // channels == col // channels, 1.0 / channels, 0.0).astype(BF16)


def average(value, mean_matrix):
    high, low = split2(value)
    return dot(high, mean_matrix) + dot(low, mean_matrix)


def normalized(value, mean_matrix):
    center = value - dot(value.astype(BF16), mean_matrix)
    inverse = lax.rsqrt(average(center * center, mean_matrix) + EPS)
    return center * inverse, inverse


def column(row_value, lanes):
    return jnp.transpose(jnp.broadcast_to(row_value, (lanes, row_value.shape[1])))


def place_of(dims):
    return lax.axis_index("seq"), lax.axis_index("res"), lax.axis_index("sub")


def rows_place(dims):
    Z, R, C, rows, parts, width = dims
    z, x, c = place_of(dims)
    block = z // parts
    return c == lax.rem(block, C), x ^ (block // C), lax.rem(z, parts)


def first_kernel(dims, seq_mask_ref, x_ref, u_ref, gain_ref, token_ref, *shares):
    Z, R, C, rows, parts, width = dims
    channels, columns = x_ref.shape[1:]
    mean_matrix = averaging(channels)
    live = column(token_ref[...].astype(F32), 2 * channels)
    gain = jnp.concatenate([gain_ref[...].astype(F32)] * 2, axis=1)
    second_half = iota(live.shape, 1) >= channels
    normed, masked = [], []
    for pair in range(x_ref.shape[0] // 2):
        scaled, _ = normalized(side_by_side(x_ref, pair, channels), mean_matrix)
        normed.append((scaled * gain).astype(BF16))
        keep = jnp.where(second_half, seq_mask_ref[2 * pair + 1], seq_mask_ref[2 * pair]).astype(F32)
        masked.append((side_by_side(u_ref, pair, channels) * keep * live).astype(BF16))
    both = jnp.concatenate(
        [jnp.concatenate(normed, axis=1), jnp.concatenate(masked, axis=1)], axis=0
    )
    x = place_of(dims)[1]
    for b, share in enumerate(shares):
        for group in range(R):

            @pl.when(x ^ b == group)
            def _():
                share[...] = both[:, group * width : (group + 1) * width]


def pack_kernel(dims, slim, *refs):
    Z, R, C, rows, parts, width = dims
    held, messages = refs[:R], refs[R:]
    columns = held[0].shape[0] // 2
    for message in messages:
        for b in range(R):
            message[b * columns : (b + 1) * columns] = held[b][0:columns]
    if slim:
        near = rows_place(dims)[1]
        for far, message in enumerate(messages):
            for b in range(R):

                @pl.when(near ^ far == b)
                def _():
                    message[R * columns :] = held[b][columns:]
    else:
        for b in range(R):
            messages[0][(R + b) * columns : (R + b + 1) * columns] = held[b][columns:]


def pick_kernel(dims, slim, *refs):
    Z, R, C, rows, parts, width = dims
    messages, picked = refs[:-1], refs[-1]
    columns = messages[0].shape[0] // (R + 1 if slim else 2 * R)
    _, block, part = rows_place(dims)
    at = pl.multiple_of(block * columns + part * rows, rows)
    for n, message in enumerate(messages):
        picked[n, 0:rows] = message[pl.ds(at, rows)]
        picked[n, rows : 2 * rows] = message[R * columns :] if slim else message[pl.ds(R * columns + at, rows)]


def pair_kernel(heads, x_ref, moments, squares, centers, token_ref, e_ref, stat_ref, logit_ref, mean_ref, inverse_ref, scratch):
    count, columns, width = x_ref.shape
    groups = count // GROUP
    x = x_ref[...].reshape(groups, GROUP, columns, width)
    parts, highs, lows = [], [], []
    for g in range(GROUP):
        part = x[:, g].reshape(groups * columns, width)
        value = part.astype(F32)
        high, low = split2(value * value)
        parts.append(part)
        highs.append(high)
        lows.append(low)
    both = squares[...]
    product = (
        dot_nt(jnp.concatenate(parts, axis=1), moments[...])
        + dot_nt(jnp.concatenate(highs, axis=1), both)
        + dot_nt(jnp.concatenate(lows, axis=1), both)
    )
    padding = 1000000000.0 * (token_ref[...].astype(F32) - 1.0)
    center = centers[...]
    for group in range(groups):
        turned = jnp.transpose(product[group * columns : (group + 1) * columns])
        for g in range(GROUP):
            i = group * GROUP + g
            base = g * SLOTS
            raw = (
                turned[base : base + heads]
                + turned[base + heads : base + 2 * heads]
                + turned[base + 2 * heads : base + 3 * heads]
            )
            total = turned[base + 3 * heads : base + 3 * heads + 1]
            square = turned[base + 3 * heads + 4 : base + 3 * heads + 5]
            mean = total * (1.0 / width)
            upper = total.astype(BF16).astype(F32)
            lower = total - upper
            spread_sum = (square - upper * upper * (1.0 / width)) - (
                2.0 * upper * lower + lower * lower
            ) * (1.0 / width)
            inverse = lax.rsqrt(jnp.maximum(spread_sum, 0.0) * (1.0 / width) + EPS)
            scratch[i * heads : (i + 1) * heads] = inverse * (raw - mean * center)
            mean_ref[i : i + 1] = mean
            inverse_ref[i : i + 1] = inverse
    lane = iota((count, columns), 1)
    stats = jnp.zeros((count, columns), F32)
    for h in range(heads):
        logit = scratch[pl.ds(h, count, stride=heads), :]
        logit_ref[h] = logit
        logit = logit + padding
        peak = jnp.max(logit, axis=1, keepdims=True)
        e = jnp.exp(logit - peak).astype(BF16)
        e_ref[h] = e
        total = jnp.sum(e.astype(F32), axis=1, keepdims=True)
        for t, part in enumerate(split3(peak)):
            stats = jnp.where(lane == t * heads + h, part, stats)
        for t, part in enumerate(split3(total)):
            stats = jnp.where(lane == (t + 3) * heads + h, part, stats)
    stats = stats.astype(BF16)
    e_ref[heads] = stats
    stat_ref[...] = stats


def joined_thirds(stats, heads):
    lanes = stats.shape[1]
    return (
        stats
        + pltpu.roll(stats, lanes - heads, 1)
        + pltpu.roll(stats, lanes - 2 * heads, 1)
    )


def probs_kernel(R, heads, *refs):
    exps, far, (probs, scales) = refs[:R], refs[R : 2 * R], refs[2 * R :]
    columns = exps[0].shape[2]
    near = [joined_thirds(e[heads].astype(F32), heads) for e in exps]
    everything = near + [joined_thirds(s[...].astype(F32), heads) for s in far]
    peak = functools.reduce(jnp.maximum, everything)
    total = 0.0
    for s in everything:
        total = total + jnp.exp(s - peak) * pltpu.roll(s, s.shape[1] - 3 * heads, 1)
    for b in range(R):
        scale = jnp.exp(near[b] - peak) / total
        scales[b] = scale
        for h in range(heads):
            weight = exps[b][h].astype(F32) * scale[:, h : h + 1]
            probs[h, :, b * columns : (b + 1) * columns] = weight.astype(BF16)


def quad(refs, q, rows, lanes):
    per = max(lanes // refs[0].shape[-1], 1)
    return jnp.concatenate([refs[q * per + g][rows] for g in range(per)], axis=1)


def work_kernel(dims, heads, mine, other, *refs):
    Z, R, C, rows, parts, width = dims
    n = mine.shape[0]
    messages, refs = refs[:n], refs[n:]
    probs, value_ref, gate_ref, output_ref, *refs = refs
    values, mixed_grad, keep, send, partial, gathered, gates, grads, turned = refs
    columns = probs.shape[2] // R
    lanes, step = value_ref.shape[0], value_ref.shape[1] // heads
    quads = n * width // lanes
    per = n // quads
    here, _, _ = rows_place(dims)

    @pl.when(here)
    def _():
        gathered[...] = mine[...]

    @pl.when(jnp.logical_not(here))
    def _():
        gathered[...] = other[...]

    planes = [gathered.at[a] for a in range(n)]
    for q in range(quads):
        at = slice(q * step, (q + 1) * step)
        gate = jax.nn.sigmoid(dot(quad(planes, q, slice(0, rows), lanes), gate_ref[...]))
        grad = dot(quad(planes, q, slice(rows, 2 * rows), lanes), output_ref[...])
        product = (gate * grad).astype(BF16)
        gates[q] = gate
        grads[q] = grad
        tokens = dot(quad(messages, q, slice(0, R * columns), lanes), value_ref[...]).astype(BF16)
        for h in range(heads):
            mixed_grad[h, :, at] = product[:, h * step : (h + 1) * step]
            values[h, :, at] = tokens[:, h * step : (h + 1) * step]
    for h in range(heads):
        sums = dot_tn(probs[h], mixed_grad[h]).astype(BF16)
        for q in range(quads):
            turned[q, :, h * step : (h + 1) * step] = sums[:, q * step : (q + 1) * step]
    for q in range(quads):
        sums = dot_nt(turned[q], value_ref[...])
        for g in range(per):
            partial[q * per + g] = sums[:, g * width : (g + 1) * width]
    for q in range(quads):
        at = slice(q * step, (q + 1) * step)
        gate, grad = gates[q], grads[q]
        mixed = jnp.concatenate([dot(probs[h], values[h, :, at]) for h in range(heads)], axis=1)
        gated = mixed * gate
        gate_grad = (grad * gated * (1.0 - gate)).astype(BF16)
        update = dot_nt(gated.astype(BF16), output_ref[...])
        through = dot_nt(gate_grad, gate_ref[...])
        for g in range(per):
            for low, value in ((0, update), (rows, through)):
                value = value[:, g * width : (g + 1) * width]
                keep[q * per + g, low : low + rows] = value
                send[q * per + g, low : low + rows] = value.astype(BF16)


def finish_kernel(dims, keep, received, partial, *messages):
    Z, R, C, rows, parts, width = dims
    n, tall, _ = partial.shape
    here, block, part = rows_place(dims)
    at = pl.multiple_of(block * (tall // R) + part * rows, rows)
    for a, message in enumerate(messages):
        message[0:tall] = partial[a].astype(BF16)

        @pl.when(here)
        def _():
            both = keep[a] + received[a].astype(F32)
            message[tall:] = both[0:rows].astype(BF16)
            message[pl.ds(at, rows)] = (partial[a, pl.ds(at, rows)] + both[rows:]).astype(BF16)


def scores_kernel(R, heads, count, *refs):
    mixed_grads, refs = refs[:count], refs[count:]
    values, refs = refs[:count], refs[count:]
    scales, *refs = refs
    exps, refs = refs[:R], refs[R:]
    own_scores, total_ref, *messages = refs
    rows, columns = exps[0].shape[1:]
    lane = iota((rows, columns), 1)
    sums = jnp.zeros((rows, columns), F32)
    for h in range(heads):
        scores = sum(dot_nt(g[h], v[h]) for g, v in zip(mixed_grads, values))
        total = 0.0
        for b in range(R):
            part = scores[:, b * columns : (b + 1) * columns]
            if b == 0:
                own_scores[h] = part
            else:
                part = part.astype(BF16)
                messages[b - 1][h] = part
                part = part.astype(F32)
            weight = exps[b][h].astype(F32) * scales[b][:, h : h + 1]
            total = total + jnp.sum(weight * part, axis=1, keepdims=True)
        for t, part in enumerate(split3(total)):
            sums = jnp.where(lane == t * heads + h, part, sums)
    sums = sums.astype(BF16)
    total_ref[...] = sums
    for message in messages:
        message[heads] = sums


def pair_back_kernel(R, heads, x_ref, logit_ref, mean_ref, inverse_ref, e_ref, scale_ref, own_ref, back_ref, *refs):
    received, refs = refs[: R - 1], refs[R - 1 :]
    totals, refs = refs[: R + 1], refs[R + 1 :]
    out_ref, scratch = refs
    count, columns, width = x_ref.shape
    total = sum(t[...].astype(F32) for t in totals) + sum(m[heads].astype(F32) for m in received)
    total = joined_thirds(total, heads)
    scale = scale_ref[0]
    inverse = inverse_ref[...]
    cross = 0.0
    for h in range(heads):
        scores = own_ref[h]
        for m in received:
            scores = scores + m[h].astype(F32)
        prob = e_ref[h].astype(F32) * scale[:, h : h + 1]
        grad = prob * (scores - total[:, h : h + 1])
        cross = cross + grad * logit_ref[h]
        scaled = grad * inverse
        high = scaled.astype(BF16).astype(F32)
        scratch[pl.ds(h, count, stride=SLOTS), :] = high
        scratch[pl.ds(heads + h, count, stride=SLOTS), :] = high
        scratch[pl.ds(2 * heads + h, count, stride=SLOTS), :] = scaled - high
    factor = inverse * inverse * cross * (1.0 / width)
    rest = list(split3(factor * mean_ref[...])) + list(split3(factor))
    rest += [jnp.zeros_like(factor)] * (SLOTS - 3 * heads - len(rest))
    for t, part in enumerate(rest):
        scratch[pl.ds(3 * heads + t, count, stride=SLOTS), :] = part
    back = back_ref[...]
    for group in range(count // GROUP):
        tile = scratch[group * GROUP * SLOTS : (group + 1) * GROUP * SLOTS]
        product = dot(jnp.transpose(tile).astype(BF16), back)
        for g in range(GROUP):
            i = group * GROUP + g
            plain = product[:, 2 * g * width : (2 * g + 1) * width]
            slope = product[:, (2 * g + 1) * width : (2 * g + 2) * width]
            out_ref[i] = (plain - slope * x_ref[i].astype(F32)).astype(BF16)


def fold_kernel(dims, *refs):
    Z, R, C, rows, parts, width = dims
    messages, shares = refs[:Z], refs[Z:]
    columns = shares[0].shape[0] // 2
    z, x, c = place_of(dims)
    for b, share in enumerate(shares):
        at = slice(b * columns, (b + 1) * columns)
        share[0:columns] = sum(m[at].astype(F32) for m in messages).astype(BF16)
        for part in range(parts):
            plane = ((x ^ b) * C + c) * parts + part
            for a, message in enumerate(messages):

                @pl.when(plane ^ z == a)
                def _():
                    share[columns + part * rows : columns + (part + 1) * rows] = message[R * columns :]


def last_kernel(dims, seq_mask_ref, x_ref, gain_ref, token_ref, *refs):
    Z, R, C, rows, parts, width = dims
    shares, refs = refs[:R], refs[R:]
    update_ref, grad_ref, updates, through = refs
    channels, columns = x_ref.shape[1:]
    x = place_of(dims)[1]
    for b, share in enumerate(shares):
        at = pl.multiple_of((x ^ b) * width, width)
        through[:, pl.ds(at, width)] = share[0:columns].astype(F32)
        updates[:, pl.ds(at, width)] = share[columns:].astype(F32)

    mean_matrix = averaging(channels)
    live = column(token_ref[...].astype(F32), 2 * channels)
    gain = jnp.concatenate([gain_ref[...].astype(F32)] * 2, axis=1)
    second_half = iota(live.shape, 1) >= channels
    for pair in range(x_ref.shape[0] // 2):
        at = slice(pair * 2 * channels, (pair + 1) * 2 * channels)
        grad = through[:, at] * gain
        scaled, inverse = normalized(side_by_side(x_ref, pair, channels), mean_matrix)
        grad = inverse * (
            grad - average(grad, mean_matrix) - scaled * average(grad * scaled, mean_matrix)
        )
        grad = jnp.transpose(grad).astype(BF16)
        keep = jnp.where(second_half, seq_mask_ref[2 * pair + 1], seq_mask_ref[2 * pair]).astype(F32)
        update = jnp.transpose(updates[:, at] * keep * live).astype(BF16)
        for s in range(2):
            at = slice(s * channels, (s + 1) * channels)
            grad_ref[2 * pair + s] = grad[at]
            update_ref[2 * pair + s] = update[at]


def shards(
    Z, R, C,
    alignment_input, pair_features, update_cotangent, alignment_norm_gain, pair_norm_gain,
    value_matrix, gate_matrix, output_matrix, head_bias_matrix, sequence_mask, token_padding_mask,
):
    sequences, columns, channels = alignment_input.shape
    rows, _, pair_width = pair_features.shape
    heads = head_bias_matrix.shape[1]
    hidden = value_matrix.shape[1]
    depth = hidden // heads
    parts = columns // rows
    width = sequences // R * channels
    lanes = QUAD * channels
    step = QUAD * depth
    dims = (Z, R, C, rows, parts, width)
    slim = (Z, R, C, parts) == (4, 2, 2, 1)
    everyone = ("seq", "res", "sub")

    def exchange(value, dz=0, dx=0, dc=0):
        at = lambda z, x, c: (z * R + x) * C + c
        places = [(z, x, c) for z in range(Z) for x in range(R) for c in range(C)]
        return lax.ppermute(value, everyone, [(at(z, x, c), at(z ^ dz, x ^ dx, c ^ dc)) for z, x, c in places])

    in_hbm = lambda value: pltpu.with_memory_space_constraint(value, pltpu.HBM)

    gain = in_hbm(alignment_norm_gain.reshape(1, channels))
    by_channel = lambda value: jnp.swapaxes(value, 1, 2)
    alignment_turned = in_hbm(by_channel(alignment_input))
    token_row = in_hbm(token_padding_mask.reshape(1, columns))
    seq_mask = sequence_mask
    pair_input = in_hbm(pair_features)
    share = shape((2 * columns, width), BF16)

    held = call(
        functools.partial(first_kernel, dims),
        [share] * R,
        "first",
        scalars=1,
        operands=(seq_mask, alignment_turned, in_hbm(by_channel(update_cotangent)), gain, token_row),
    )
    held = [held[0]] + [exchange(m, dx=b) for b, m in enumerate(held) if b]
    tall = R * columns + (rows if slim else R * columns)
    packed = call(
        functools.partial(pack_kernel, dims, slim),
        [shape((tall, width), BF16)] * (2 if slim else 1),
        "pack",
        operands=held,
    )
    if slim:
        near, far = packed
        arrived = {0: near, 2: exchange(far, dz=2), 1: exchange(near, dz=1)}
        arrived[3] = exchange(arrived[2], dz=1)
    else:
        arrived, stride = {0: packed[0]}, Z // 2
        while stride:
            arrived |= {a ^ stride: exchange(m, dz=stride) for a, m in arrived.items()}
            stride //= 2

    spread_value, spread_gate, spread_output, moments, squares, centers, back = call(
        functools.partial(weights_kernel, depth),
        [shape((lanes, hidden * QUAD), BF16)] * 3
        + [shape((GROUP * SLOTS, GROUP * pair_width), BF16)] * 2
        + [shape((heads, pair_width), F32), shape((GROUP * SLOTS, 2 * GROUP * pair_width), BF16)],
        "weights",
        operands=(
            in_hbm(value_matrix), in_hbm(gate_matrix), in_hbm(output_matrix.T), in_hbm(head_bias_matrix.T),
            in_hbm(pair_norm_gain.reshape(1, pair_width)),
        ),
    )

    block = min(32, rows)
    steps = rows // block
    whole = pl.BlockSpec(memory_space=pltpu.VMEM)
    by_row = lambda *tail: pl.BlockSpec((block, *tail), lambda i: (i,) + (0,) * len(tail))
    by_middle = lambda lead: pl.BlockSpec((lead, block, columns), lambda i: (0, i, 0))
    exps, stats, logits, means, inverses = call(
        functools.partial(pair_kernel, heads),
        [
            shape((heads + 1, rows, columns), BF16),
            shape((rows, columns), BF16),
            shape((heads, rows, columns), F32),
            shape((rows, columns), F32),
            shape((rows, columns), F32),
        ],
        "pair",
        operands=(pair_input, moments, squares, centers, token_row),
        scratch=[pltpu.VMEM((block * heads, columns), F32)],
        grid=(steps,),
        in_specs=[by_row(columns, pair_width)] + [whole] * 3 + [pl.BlockSpec((1, columns), lambda i: (0, 0))],
        out_specs=[by_middle(heads + 1), by_row(columns), by_middle(heads), by_row(columns), by_row(columns)],
    )
    exps = [exps] + [exchange(exps, dx=b) for b in range(1, R)]
    far = [exchange(stats, dx=b, dc=1) for b in range(R)]
    probs, scales = call(
        functools.partial(probs_kernel, R, heads),
        [shape((heads, rows, R * columns), BF16), shape((R, rows, columns), F32)],
        "probs",
        operands=(*exps, *far),
    )

    values, mixed_grads, outgoing = [], [], {}
    for phase in [(0, 1, 2), (3,)] if slim else [tuple(range(Z))]:
        n = len(phase)
        quads = n * width // lanes
        messages = [arrived[a] for a in phase]
        (picked,) = call(
            functools.partial(pick_kernel, dims, slim),
            [shape((n, 2 * rows, width), BF16)],
            "pick",
            operands=messages,
        )
        value, mixed_grad, keep, send, partial = call(
            functools.partial(work_kernel, dims, heads),
            [
                shape((heads, R * columns, quads * step), BF16),
                shape((heads, rows, quads * step), BF16),
                shape((n, 2 * rows, width), F32),
                shape((n, 2 * rows, width), BF16),
                shape((n, R * columns, width), F32),
            ],
            "work",
            operands=(
                picked, exchange(picked, dc=1), *messages, probs, spread_value, spread_gate, spread_output,
            ),
            scratch=[
                pltpu.VMEM((n, 2 * rows, width), BF16),
                pltpu.VMEM((quads, rows, heads * step), F32),
                pltpu.VMEM((quads, rows, heads * step), F32),
                pltpu.VMEM((quads, R * columns, heads * step), BF16),
            ],
        )
        values.append(value)
        mixed_grads.append(mixed_grad)
        finished = call(
            functools.partial(finish_kernel, dims),
            [shape((R * columns + rows, width), BF16)] * n,
            "finish",
            operands=(keep, exchange(send, dc=1), partial),
        )
        outgoing |= dict(zip(phase, finished))
    collected = [exchange(outgoing[a], dz=a) if a else outgoing[a] for a in range(Z)]

    own_scores, own_total, *scores = call(
        functools.partial(scores_kernel, R, heads, len(values)),
        [shape((heads, rows, columns), F32), shape((rows, columns), BF16)]
        + [shape((heads + 1, rows, columns), BF16)] * (R - 1),
        "scores",
        operands=(*mixed_grads, *values, scales, *exps),
    )
    scores = [exchange(m, dx=b) for b, m in enumerate(scores, 1)]
    totals = [own_total] + [exchange(own_total, dx=b, dc=1) for b in range(R)]

    (pair_gradient,) = call(
        functools.partial(pair_back_kernel, R, heads),
        [shape(pair_features.shape, BF16)],
        "pair_back",
        operands=(
            pair_input, logits, means, inverses, exps[0], scales, own_scores, back, *scores, *totals,
        ),
        scratch=[pltpu.VMEM((block * SLOTS, columns), F32)],
        grid=(steps,),
        in_specs=[
            by_row(columns, pair_width), by_middle(heads), by_row(columns), by_row(columns),
            by_middle(heads + 1), by_middle(1), by_middle(heads), whole,
        ]
        + [by_middle(heads + 1)] * (R - 1)
        + [by_row(columns)] * (R + 1),
        out_specs=[by_row(columns, pair_width)],
    )
    shares = call(
        functools.partial(fold_kernel, dims), [share] * R, "fold", operands=collected
    )
    shares = [shares[0]] + [exchange(m, dx=b) for b, m in enumerate(shares) if b]
    alignment_update, alignment_gradient = call(
        functools.partial(last_kernel, dims),
        [shape(alignment_turned.shape, BF16)] * 2,
        "last",
        scalars=1,
        operands=(seq_mask, alignment_turned, gain, token_row, *shares),
        scratch=[pltpu.VMEM((columns, R * width), F32)] * 2,
    )
    return by_channel(alignment_update), by_channel(alignment_gradient), pair_gradient


def solution(mesh):
    split = P(("groups", "seq"), ("res", "sub"), None)
    sizes = (mesh.shape["seq"], mesh.shape["res"], mesh.shape["sub"])
    return jax.shard_map(
        functools.partial(shards, *sizes),
        mesh=mesh,
        in_specs=(split, split, split, P(), P(), P(), P(), P(), P())
        + (P(("groups", "seq")), P(("groups", "res", "sub"))),
        out_specs=(split, split, split),
        check_vma=False,
    )
```

```python
import functools

import jax
import jax.numpy as jnp
from jax import lax
from jax.experimental import pallas as pl
from jax.experimental.pallas import tpu as pltpu
from jax.sharding import PartitionSpec as P

F32 = jnp.float32
BF16 = jnp.bfloat16
EPS = 1e-05
QUAD = 4
GROUP = 4
SLOTS = 32
COST = dict(first=1.5, pack=0.1, weights=1.3, pair=5, attach=0, pick=1, probs=0, work=0.0, scores=0.0, finish=0, pair_back=0, gather=5, fold=0, last=0)
VMEM = 20 * 1024 * 1024


def dot(a, b):
    return jnp.dot(a, b, preferred_element_type=F32)


def dot_nt(a, b):
    return lax.dot_general(a, b, (((1,), (1,)), ((), ())), preferred_element_type=F32)


def dot_tn(a, b):
    return lax.dot_general(a, b, (((0,), (0,)), ((), ())), preferred_element_type=F32)


def iota(shape, dim):
    return lax.broadcasted_iota(jnp.int32, shape, dim)


def split3(value):
    high = value.astype(BF16).astype(F32)
    rest = value - high
    middle = rest.astype(BF16).astype(F32)
    return high, middle, rest - middle


def split2(value):
    high = value.astype(BF16)
    return high, (value - high.astype(F32)).astype(BF16)


def call(kernel, out_shape, name, operands, scratch=(), after=(), grid=None, out_specs=None, into=None):
    whole = pl.BlockSpec(memory_space=pltpu.VMEM)
    count = len(operands)
    body = lambda *refs: kernel(*refs[:count], *refs[count + len(after) :])
    extra = {} if grid is None else {"grid": grid}
    if into is not None:
        extra["input_output_aliases"] = {count + len(after): 0}
        after = [*after, into]
    return pl.pallas_call(
        body,
        out_shape=out_shape,
        in_specs=[whole] * count + [pl.BlockSpec(memory_space=pl.ANY)] * len(after),
        out_specs=out_specs or [whole] * len(out_shape),
        scratch_shapes=list(scratch),
        compiler_params=pltpu.CompilerParams(vmem_limit_bytes=VMEM),
        cost_estimate=pl.CostEstimate(flops=int(COST[name] * 3e9), bytes_accessed=0, transcendentals=0),
        name=name,
        **extra,
    )(*operands, *after)


def shape(dims, dtype):
    return jax.ShapeDtypeStruct(tuple(dims), dtype)


def spread(matrix, channels, depth):
    hidden = matrix.shape[1]
    wide = hidden * QUAD
    row, col = iota((hidden, wide), 0), iota((hidden, wide), 1)
    pick = (row // depth == col // (depth * QUAD)) & (row % depth == col % depth)
    placed = dot(matrix, pick.astype(F32).astype(BF16))
    tall = jnp.concatenate([placed] * QUAD, axis=0)
    row, col = iota(tall.shape, 0), iota(tall.shape, 1)
    return jnp.where(row // channels == (col // depth) % QUAD, tall, 0.0).astype(BF16)


def weights_kernel(
    depth, value_ref, gate_ref, output_ref, bias_ref, gain_ref,
    spread_value, spread_gate, spread_output, moments, squares, centers, back,
):
    channels = value_ref.shape[0]
    spread_value[...] = spread(value_ref[...], channels, depth)
    spread_gate[...] = spread(gate_ref[...], channels, depth)
    spread_output[...] = spread(output_ref[...], channels, depth)
    scaled = bias_ref[...].astype(F32) * gain_ref[...].astype(F32)
    heads, width = scaled.shape
    total = jnp.sum(scaled, axis=1, keepdims=True)
    centers[...] = jnp.broadcast_to(total, (heads, width))
    high, middle, low = split3(scaled)
    tail = (SLOTS - 3 * heads, width)
    row = iota(tail, 0)
    slots = jnp.concatenate([high, middle, low, jnp.where(row < 4, 1.0, 0.0)], axis=0)
    square_slots = jnp.concatenate(
        [jnp.zeros((3 * heads, width), F32), jnp.where(row >= 4, 1.0, 0.0)], axis=0
    )

    def diagonal(tile):
        tall = jnp.concatenate([tile] * GROUP, axis=0)
        full = jnp.concatenate([tall] * GROUP, axis=1)
        row, col = iota(full.shape, 0), iota(full.shape, 1)
        return jnp.where(row // SLOTS == col // tile.shape[1], full, 0.0).astype(BF16)

    moments[...] = diagonal(slots)
    squares[...] = diagonal(square_slots)
    high, middle, _ = split3(scaled - total * (1.0 / width))
    back[...] = diagonal(jnp.concatenate([high, middle, high, jnp.where(row < 3, 1.0, 0.0)], axis=0))


def side_by_side(ref, pair, channels):
    both = jnp.concatenate([ref[2 * pair], ref[2 * pair + 1]], axis=0)
    return jnp.transpose(both.astype(F32))


def averaging(channels):
    row, col = iota((2 * channels, 2 * channels), 0), iota((2 * channels, 2 * channels), 1)
    return jnp.where(row // channels == col // channels, 1.0 / channels, 0.0).astype(BF16)


def average(value, mean_matrix):
    high, low = split2(value)
    return dot(high, mean_matrix) + dot(low, mean_matrix)


def normalized(value, mean_matrix):
    center = value - dot(value.astype(BF16), mean_matrix)
    inverse = lax.rsqrt(average(center * center, mean_matrix) + EPS)
    return center * inverse, inverse


def column(row_value, lanes):
    return jnp.transpose(jnp.broadcast_to(row_value, (lanes, row_value.shape[1])))


def place_of(dims):
    return lax.axis_index("seq"), lax.axis_index("res"), lax.axis_index("sub")


def rows_place(dims):
    Z, R, C, rows, parts, width = dims
    z, x, c = place_of(dims)
    block = z // parts
    return c == lax.rem(block, C), x ^ (block // C), lax.rem(z, parts)


def first_kernel(dims, seq_mask_ref, x_ref, u_ref, gain_ref, token_ref, scaled_out, inverse_out, alive_out, gain_out, *shares):
    Z, R, C, rows, parts, width = dims
    channels, columns = x_ref.shape[1:]
    mean_matrix = averaging(channels)
    live = column(token_ref[...].astype(F32), 2 * channels)
    seq_mask = seq_mask_ref[...].astype(F32)
    gain = jnp.concatenate([gain_ref[...].astype(F32)] * 2, axis=1)
    second_half = iota((1, 2 * channels), 1) >= channels
    normed, masked = [], []
    for pair in range(x_ref.shape[0] // 2):
        at = slice(pair * 2 * channels, (pair + 1) * 2 * channels)
        scaled, inverse = normalized(side_by_side(x_ref, pair, channels), mean_matrix)
        scaled_out[:, at] = scaled
        inverse_out[:, at] = inverse
        normed.append((scaled * gain).astype(BF16))
        keep = jnp.where(
            second_half, seq_mask[:, 2 * pair + 1 : 2 * pair + 2], seq_mask[:, 2 * pair : 2 * pair + 1]
        )
        alive = keep * live
        alive_out[:, at] = alive
        masked.append((side_by_side(u_ref, pair, channels) * alive).astype(BF16))
    gain_out[...] = jnp.broadcast_to(gain, gain_out.shape)
    both = jnp.concatenate(
        [jnp.concatenate(normed, axis=1), jnp.concatenate(masked, axis=1)], axis=0
    )
    x = place_of(dims)[1]
    for b, share in enumerate(shares):
        for group in range(R):

            @pl.when(x ^ b == group)
            def _():
                share[...] = both[:, group * width : (group + 1) * width]


def pack_kernel(dims, slim, *refs):
    Z, R, C, rows, parts, width = dims
    held, messages = refs[:R], refs[R:]
    columns = held[0].shape[0] // 2
    for message in messages:
        for b in range(R):
            message[b * columns : (b + 1) * columns] = held[b][0:columns]
    if slim:
        near = rows_place(dims)[1]
        for far, message in enumerate(messages):
            for b in range(R):

                @pl.when(near ^ far == b)
                def _():
                    message[R * columns :] = held[b][columns:]
    else:
        for b in range(R):
            messages[0][(R + b) * columns : (R + b + 1) * columns] = held[b][columns:]


def pick_kernel(dims, slim, count, *refs):
    Z, R, C, rows, parts, width = dims
    messages, picked, relayed = refs[:count], refs[count], refs[count + 1 :]
    for source, target in zip(messages, relayed):
        target[...] = source[...]
    columns = messages[0].shape[0] // (R + 1 if slim else 2 * R)
    _, block, part = rows_place(dims)
    at = pl.multiple_of(block * columns + part * rows, rows)
    for n, message in enumerate(messages):
        picked[n, 0:rows] = message[pl.ds(at, rows)]
        picked[n, rows : 2 * rows] = message[R * columns :] if slim else message[pl.ds(R * columns + at, rows)]


def pair_kernel(heads, block, x_ref, moments, squares, centers, token_ref, *refs):
    e_upper, e_lower, stat_ref, logit_ref, mean_ref, inverse_ref, scratch = refs
    rows, columns, width = x_ref.shape
    cut = e_upper.shape[1]
    groups = block // GROUP
    padding = 1000000000.0 * (token_ref[...].astype(F32) - 1.0)
    lane = iota((rows, columns), 1)

    def step(index, carry):
        low = pl.multiple_of(index * block, block)
        x = x_ref[pl.ds(low, block)].reshape(groups, GROUP, columns, width)
        parts, highs, lows = [], [], []
        for g in range(GROUP):
            part = x[:, g].reshape(groups * columns, width)
            value = part.astype(F32)
            high, rest = split2(value * value)
            parts.append(part)
            highs.append(high)
            lows.append(rest)
        product = dot_nt(
            jnp.concatenate(parts + highs + lows, axis=1),
            jnp.concatenate([moments[...], squares[...], squares[...]], axis=1),
        )
        center = centers[...]
        for group in range(groups):
            turned = jnp.transpose(product[group * columns : (group + 1) * columns])
            for g in range(GROUP):
                i = group * GROUP + g
                base = g * SLOTS
                raw = (
                    turned[base : base + heads]
                    + turned[base + heads : base + 2 * heads]
                    + turned[base + 2 * heads : base + 3 * heads]
                )
                total = turned[base + 3 * heads : base + 3 * heads + 1]
                square = turned[base + 3 * heads + 4 : base + 3 * heads + 5]
                mean = total * (1.0 / width)
                upper = total.astype(BF16).astype(F32)
                lower = total - upper
                spread_sum = (square - upper * upper * (1.0 / width)) - (
                    2.0 * upper * lower + lower * lower
                ) * (1.0 / width)
                inverse = lax.rsqrt(jnp.maximum(spread_sum, 0.0) * (1.0 / width) + EPS)
                scratch[pl.ds(pl.multiple_of((low + i) * heads, heads), heads)] = inverse * (raw - mean * center)
                mean_ref[pl.ds(low + i, 1)] = mean
                inverse_ref[pl.ds(low + i, 1)] = inverse
        return carry

    lax.fori_loop(0, rows // block, step, 0, unroll=True)
    stats = jnp.zeros((rows, columns), F32)
    ones = jnp.ones((columns, columns), BF16)
    for h in range(heads):
        logit = scratch[pl.ds(h, rows, stride=heads), :]
        logit_ref[h] = logit
        logit = logit + padding
        peak = jnp.max(logit, axis=1, keepdims=True)
        e = jnp.exp(logit - peak).astype(BF16)
        e_upper[h] = e[:cut]
        e_lower[h] = e[cut:]
        stats = jnp.where(lane == h, peak, stats)
        stats = jnp.where(lane == 3 * heads + h, dot(e, ones), stats)
    high, middle, rest = split3(stats)
    stats = high + pltpu.roll(middle, heads, 1) + pltpu.roll(rest, 2 * heads, 1)
    stat_ref[...] = stats.astype(BF16)


def thirds(value, heads):
    lane = iota(value.shape, 1)
    high, middle, low = split3(jnp.where(lane < heads, value, 0.0))
    return high + pltpu.roll(middle, heads, 1) + pltpu.roll(low, 2 * heads, 1)


def joined_thirds(stats, heads):
    lanes = stats.shape[1]
    return (
        stats
        + pltpu.roll(stats, lanes - heads, 1)
        + pltpu.roll(stats, lanes - 2 * heads, 1)
    )


def attach_kernel(heads, e_ref, own_ref, other_ref, message):
    size = e_ref.shape[1]
    message[0:heads] = e_ref[...]
    at = heads
    for ref in (own_ref, other_ref):
        for low in range(0, ref.shape[0], size):
            message[at] = ref[low : low + size]
            at += 1


def attached(message, heads, rows):
    count = rows // message.shape[1]
    return [
        jnp.concatenate([message[at + n] for n in range(count)], axis=0).astype(F32)
        for at in (heads, heads + count)
    ]


def probs_kernel(R, heads, *refs):
    exps, (probs, scales) = refs[: 2 * R], refs[2 * R :]
    rows, columns = scales.shape[1:]
    exps = [exps[2 * b : 2 * b + 2] for b in range(R)]
    stats = [[joined_thirds(s, heads) for s in attached(lower, heads, rows)] for _, lower in exps]
    near = [pair[0] for pair in stats]
    everything = near + [pair[1] for pair in stats]
    peak = functools.reduce(jnp.maximum, everything)
    total = 0.0
    for s in everything:
        total = total + jnp.exp(s - peak) * pltpu.roll(s, s.shape[1] - 3 * heads, 1)
    for b in range(R):
        scale = jnp.exp(near[b] - peak) / total
        scales[b] = scale
        for h in range(heads):
            low = 0
            for e in exps[b]:
                at = slice(low, low + e.shape[1])
                low += e.shape[1]
                weight = e[h].astype(F32) * scale[at, h : h + 1]
                probs[h, at, b * columns : (b + 1) * columns] = weight.astype(BF16)


def quad(refs, q, rows, lanes):
    per = max(lanes // refs[0].shape[-1], 1)
    return jnp.concatenate([refs[q * per + g][rows] for g in range(per)], axis=1)


def work_kernel(dims, heads, mine, other, *refs):
    Z, R, C, rows, parts, width = dims
    n = mine.shape[0]
    messages, refs = refs[:n], refs[n:]
    probs, value_ref, gate_ref, output_ref, *refs = refs
    values, mixed_grad, keep, send, partial, gathered, gates, grads, turned = refs
    columns = probs.shape[2] // R
    lanes, step = value_ref.shape[0], value_ref.shape[1] // heads
    quads = n * width // lanes
    per = n // quads
    here, _, _ = rows_place(dims)

    @pl.when(here)
    def _():
        gathered[...] = mine[...]

    @pl.when(jnp.logical_not(here))
    def _():
        gathered[...] = other[...]

    planes = [gathered.at[a] for a in range(n)]
    for q in range(quads):
        at = slice(q * step, (q + 1) * step)
        gate = jax.nn.sigmoid(dot(quad(planes, q, slice(0, rows), lanes), gate_ref[...]))
        grad = dot(quad(planes, q, slice(rows, 2 * rows), lanes), output_ref[...])
        product = (gate * grad).astype(BF16)
        gates[q] = gate
        grads[q] = grad
        tokens = dot(quad(messages, q, slice(0, R * columns), lanes), value_ref[...]).astype(BF16)
        for h in range(heads):
            mixed_grad[h, :, at] = product[:, h * step : (h + 1) * step]
            values[h, :, at] = tokens[:, h * step : (h + 1) * step]
    for h in range(heads):
        sums = dot_tn(probs[h], mixed_grad[h]).astype(BF16)
        for q in range(quads):
            turned[q, :, h * step : (h + 1) * step] = sums[:, q * step : (q + 1) * step]
    for q in range(quads):
        sums = dot_nt(turned[q], value_ref[...])
        for g in range(per):
            partial[q * per + g] = sums[:, g * width : (g + 1) * width]
    for q in range(quads):
        at = slice(q * step, (q + 1) * step)
        gate, grad = gates[q], grads[q]
        mixed = jnp.concatenate([dot(probs[h], values[h, :, at]) for h in range(heads)], axis=1)
        gated = mixed * gate
        gate_grad = (grad * gated * (1.0 - gate)).astype(BF16)
        update = dot_nt(gated.astype(BF16), output_ref[...])
        through = dot_nt(gate_grad, gate_ref[...])
        for g in range(per):
            for low, value in ((0, update), (rows, through)):
                value = value[:, g * width : (g + 1) * width]
                keep[q * per + g, low : low + rows] = value
                send[q * per + g, low : low + rows] = value.astype(BF16)


def finish_kernel(dims, keep, received, partial, *messages):
    Z, R, C, rows, parts, width = dims
    n, tall, _ = partial.shape
    here, block, part = rows_place(dims)
    at = pl.multiple_of(block * (tall // R) + part * rows, rows)
    for a, message in enumerate(messages):
        message[0:tall] = partial[a].astype(BF16)

        @pl.when(here)
        def _():
            both = keep[a] + received[a].astype(F32)
            message[tall:] = both[0:rows].astype(BF16)
            message[pl.ds(at, rows)] = (partial[a, pl.ds(at, rows)] + both[rows:]).astype(BF16)


def scores_kernel(R, heads, count, *refs):
    mixed_grads, refs = refs[:count], refs[count:]
    values, refs = refs[:count], refs[count:]
    scales, *refs = refs
    exps, refs = refs[: 2 * R], refs[2 * R :]
    own_scores, total_ref, *messages = refs
    half = heads // 2
    rows, columns = total_ref.shape
    lane = iota((rows, columns), 1)
    sums = jnp.zeros((rows, columns), F32)
    for h in range(heads):
        scores = sum(dot_nt(g[h], v[h]) for g, v in zip(mixed_grads, values))
        total = 0.0
        for b in range(R):
            part = scores[:, b * columns : (b + 1) * columns]
            if b == 0:
                own_scores[h] = part
            else:
                part = part.astype(BF16)
                messages[2 * b - 2 + h // half][h % half] = part
                part = part.astype(F32)
            weight = jnp.concatenate([e[h] for e in exps[2 * b : 2 * b + 2]], axis=0)
            weight = weight.astype(F32) * scales[b][:, h : h + 1]
            total = total + jnp.sum(weight * part, axis=1, keepdims=True)
        for t, part in enumerate(split3(total)):
            sums = jnp.where(lane == t * heads + h, part, sums)
    total_ref[...] = sums.astype(BF16)


def attach_total_kernel(heads, scores_ref, own_ref, other_ref, message):
    count = scores_ref.shape[0]
    message[0:count] = scores_ref[...]
    total = sum(joined_thirds(ref[...].astype(F32), heads) for ref in (own_ref, other_ref))
    message[count] = thirds(total, heads).astype(BF16)


def pair_back_kernel(R, heads, first, x_ref, e_ref, logit_ref, mean_ref, inverse_ref, scale_ref, own_ref, back_ref, *refs):
    own_total, received, refs = refs[0], refs[1 : 2 * R - 1], refs[2 * R - 1 :]
    firsts, seconds, half = received[::2], received[1::2], heads // 2
    out_ref, done_ref, scratch, turned, rounded = refs
    count, columns, width = out_ref.shape
    here = pl.ds(pl.multiple_of(pl.program_id(0) * count, count), count)
    low = pl.multiple_of(first + pl.program_id(0) * count, count)
    at = pl.ds(low, count)
    done_ref[...] = jnp.zeros_like(done_ref)
    total = sum(m[half, at].astype(F32) for m in (own_total, *seconds))
    total = joined_thirds(total, heads)
    scale = scale_ref[0, at]
    inverse = inverse_ref[at]
    cross = 0.0
    for h in range(heads):
        scores = own_ref[h, at]
        for m in (firsts, seconds)[h // half]:
            scores = scores + m[h % half, at].astype(F32)
        prob = e_ref[h, here].astype(F32) * scale[:, h : h + 1]
        grad = prob * (scores - total[:, h : h + 1])
        cross = cross + grad * logit_ref[h, at]
        scaled = grad * inverse
        high = scaled.astype(BF16).astype(F32)
        scratch[pl.ds(h, count, stride=SLOTS), :] = high
        scratch[pl.ds(heads + h, count, stride=SLOTS), :] = high
        scratch[pl.ds(2 * heads + h, count, stride=SLOTS), :] = scaled - high
    factor = inverse * inverse * cross * (1.0 / width)
    rest = [*split3(factor * mean_ref[at]), factor]
    rest += [jnp.zeros_like(factor)] * (SLOTS - 3 * heads - len(rest))
    for t, part in enumerate(rest):
        scratch[pl.ds(3 * heads + t, count, stride=SLOTS), :] = part
    groups = count // GROUP
    for group in range(groups):
        rows = slice(group * columns, (group + 1) * columns)
        tile = jnp.transpose(scratch[group * GROUP * SLOTS : (group + 1) * GROUP * SLOTS])
        turned[rows] = tile
        rounded[rows] = tile.astype(BF16)
    for g in range(0, GROUP, 2):
        product = dot(rounded[...], back_ref[:, g * width : (g + 2) * width])
        for group in range(groups):
            rows = slice(group * columns, (group + 1) * columns)
            for s in range(2):
                i = group * GROUP + g + s
                lane = (g + s) * SLOTS + 3 * heads + 3
                slope = turned[rows, lane : lane + 1] * x_ref[low + i].astype(F32)
                out_ref[i] = (product[rows, s * width : (s + 1) * width] - slope).astype(BF16)


def gather_kernel(one, other, total):
    at = slice(0, total.shape[0])
    total[...] = one[at].astype(F32) + other[at].astype(F32)


def fold_kernel(dims, sums, *refs):
    Z, R, C, rows, parts, width = dims
    messages, refs = refs[:Z], refs[Z:]
    early, shares = refs[:-R], refs[-R:]
    columns = shares[0].shape[0] // 2
    z, x, c = place_of(dims)
    for b, share in enumerate(shares):
        at = slice(b * columns, (b + 1) * columns)
        total = sum(m[at].astype(F32) for a, m in enumerate(messages) if a not in sums)
        share[0:columns] = sum((m[at] for m in early), total).astype(BF16)
        for part in range(parts):
            plane = ((x ^ b) * C + c) * parts + part
            for a, message in enumerate(messages):

                @pl.when(plane ^ z == a)
                def _():
                    share[columns + part * rows : columns + (part + 1) * rows] = message[R * columns :]


def last_kernel(dims, scaled_ref, inverse_ref, alive_ref, gain_ref, *refs):
    Z, R, C, rows, parts, width = dims
    shares, refs = refs[:R], refs[R:]
    update_ref, grad_ref, updates, through = refs
    channels, columns = grad_ref.shape[1:]
    x = place_of(dims)[1]
    for b, share in enumerate(shares):
        at = pl.multiple_of((x ^ b) * width, width)
        through[:, pl.ds(at, width)] = share[0:columns].astype(F32)
        updates[:, pl.ds(at, width)] = share[columns:].astype(F32)
    mean_matrix = averaging(channels)
    gain = gain_ref[0:1]
    for pair in range(grad_ref.shape[0] // 2):
        at = slice(pair * 2 * channels, (pair + 1) * 2 * channels)
        scaled = scaled_ref[:, at]
        grad = through[:, at] * gain
        grad = inverse_ref[:, at] * (
            grad - average(grad, mean_matrix) - scaled * average(grad * scaled, mean_matrix)
        )
        grad = jnp.transpose(grad).astype(BF16)
        update = jnp.transpose(updates[:, at] * alive_ref[:, at]).astype(BF16)
        for s in range(2):
            at = slice(s * channels, (s + 1) * channels)
            grad_ref[2 * pair + s] = grad[at]
            update_ref[2 * pair + s] = update[at]


def shards(
    Z, R, C,
    alignment_input, pair_features, update_cotangent, alignment_norm_gain, pair_norm_gain,
    value_matrix, gate_matrix, output_matrix, head_bias_matrix, sequence_mask, token_padding_mask,
):
    sequences, columns, channels = alignment_input.shape
    rows, _, pair_width = pair_features.shape
    heads = head_bias_matrix.shape[1]
    hidden = value_matrix.shape[1]
    depth = hidden // heads
    parts = columns // rows
    width = sequences // R * channels
    lanes = QUAD * channels
    step = QUAD * depth
    dims = (Z, R, C, rows, parts, width)
    slim = (Z, R, C, parts) == (4, 2, 2, 1)
    everyone = ("seq", "res", "sub")

    def exchange(value, dz=0, dx=0, dc=0):
        at = lambda z, x, c: (z * R + x) * C + c
        places = [(z, x, c) for z in range(Z) for x in range(R) for c in range(C)]
        return lax.ppermute(value, everyone, [(at(z, x, c), at(z ^ dz, x ^ dx, c ^ dc)) for z, x, c in places])

    in_hbm = lambda value: pltpu.with_memory_space_constraint(value, pltpu.HBM)

    gain = in_hbm(alignment_norm_gain.reshape(1, channels))
    by_channel = lambda value: jnp.swapaxes(value, 1, 2)
    alignment_turned = in_hbm(by_channel(alignment_input))
    token_row = in_hbm(token_padding_mask.reshape(1, columns))
    seq_mask = in_hbm(sequence_mask.reshape(1, sequences))
    share = shape((2 * columns, width), BF16)

    kept = shape((columns, sequences * channels), F32)
    scaled, inverse, alive, wide_gain, *held = call(
        functools.partial(first_kernel, dims),
        [kept] * 3 + [shape((8, 2 * channels), F32)] + [share] * R,
        "first",
        operands=(seq_mask, alignment_turned, in_hbm(by_channel(update_cotangent)), gain, token_row),
    )
    held = [held[0]] + [exchange(m, dx=b) for b, m in enumerate(held) if b]
    tall = R * columns + (rows if slim else R * columns)
    packed = call(
        functools.partial(pack_kernel, dims, slim),
        [shape((tall, width), BF16)] * (2 if slim else 1),
        "pack",
        operands=held,
    )
    if slim:
        near, away = packed
        arrived = {0: near, 2: exchange(away, dz=2), 1: exchange(near, dz=1)}
    else:
        arrived, stride = {0: packed[0]}, Z // 2
        while stride:
            arrived |= {a ^ stride: exchange(m, dz=stride) for a, m in arrived.items()}
            stride //= 2

    spread_value, spread_gate, spread_output, moments, squares, centers, back = call(
        functools.partial(weights_kernel, depth),
        [shape((lanes, hidden * QUAD), BF16)] * 3
        + [shape((GROUP * SLOTS, GROUP * pair_width), BF16)] * 2
        + [shape((heads, pair_width), F32), shape((GROUP * SLOTS, GROUP * pair_width), BF16)],
        "weights",
        operands=(
            in_hbm(value_matrix), in_hbm(gate_matrix), in_hbm(output_matrix.T), in_hbm(head_bias_matrix.T),
            in_hbm(pair_norm_gain.reshape(1, pair_width)),
        ),
    )

    block = rows // 4
    cuts = ((0, 3 * block), (3 * block, block))
    upper, lower, stats, logits, means, inverses = call(
        functools.partial(pair_kernel, heads, block),
        [shape((heads, size, columns), BF16) for _, size in cuts]
        + [
            shape((rows, columns), BF16),
            shape((heads, rows, columns), F32),
            shape((rows, columns), F32),
            shape((rows, columns), F32),
        ],
        "pair",
        operands=(pair_features, moments, squares, centers, token_row),
        scratch=[pltpu.VMEM((rows * heads, columns), F32)],
    )
    (lower,) = call(
        functools.partial(attach_kernel, heads),
        [shape((heads + 2 * rows // lower.shape[1], *lower.shape[1:]), BF16)],
        "attach",
        operands=(lower, stats, exchange(stats, dc=1)),
    )
    exps = [upper, lower]
    exps = exps + [exchange(e, dx=b) for b in range(1, R) for e in exps]
    phases = [(2,), (3,), (1, 0)] if slim else [tuple(range(Z))]

    def pick(phase, relays=0, after=()):
        return call(
            functools.partial(pick_kernel, dims, slim, len(phase)),
            [shape((len(phase), 2 * rows, width), BF16)] + [shape((tall, width), BF16)] * relays,
            "pick",
            after=after,
            operands=[arrived[a] for a in phase],
        )

    first_picked, *relayed = pick(phases[0], relays=int(slim), after=[lower])
    if slim:
        arrived[3] = exchange(relayed[0], dz=1)
    probs, scales = call(
        functools.partial(probs_kernel, R, heads),
        [shape((heads, rows, R * columns), BF16), shape((R, rows, columns), F32)],
        "probs",
        operands=exps,
        after=[first_picked],
    )

    values, mixed_grads, outgoing = [], [], {}
    for phase in phases:
        n = len(phase)
        quads = n * width // lanes
        messages = [arrived[a] for a in phase]
        picked = first_picked if phase == phases[0] else pick(phase, after=[probs])[0]
        value, mixed_grad, keep, send, partial = call(
            functools.partial(work_kernel, dims, heads),
            [
                shape((heads, R * columns, quads * step), BF16),
                shape((heads, rows, quads * step), BF16),
                shape((n, 2 * rows, width), F32),
                shape((n, 2 * rows, width), BF16),
                shape((n, R * columns, width), F32),
            ],
            "work",
            after=[outgoing[2]] if slim and 3 in phase else [],
            operands=(
                picked, exchange(picked, dc=1), *messages, probs, spread_value, spread_gate, spread_output,
            ),
            scratch=[
                pltpu.VMEM((n, 2 * rows, width), BF16),
                pltpu.VMEM((quads, rows, heads * step), F32),
                pltpu.VMEM((quads, rows, heads * step), F32),
                pltpu.VMEM((quads, R * columns, heads * step), BF16),
            ],
        )
        values.append(value)
        mixed_grads.append(mixed_grad)
        finished = call(
            functools.partial(finish_kernel, dims),
            [shape((R * columns + rows, width), BF16)] * n,
            "finish",
            operands=(keep, exchange(send, dc=1), partial),
        )
        outgoing |= dict(zip(phase, finished))
    collected = [exchange(outgoing[a], dz=a) if a else outgoing[a] for a in range(Z)]

    own_scores, own_total, *scores = call(
        functools.partial(scores_kernel, R, heads, len(values)),
        [shape((heads, rows, columns), F32), shape((rows, columns), BF16)]
        + [shape((heads // 2, rows, columns), BF16)] * (2 * R - 2),
        "scores",
        operands=(*mixed_grads, *values, scales, *exps),
    )
    other_total = exchange(own_total, dc=1)
    received = []
    for b in range(1, R):
        upper, lower = scores[2 * b - 2 : 2 * b]
        (lower,) = call(
            functools.partial(attach_total_kernel, heads),
            [shape((heads // 2 + 1, rows, columns), BF16)],
            "attach",
            operands=(lower, own_total, other_total),
        )
        received += [exchange(upper, dx=b), exchange(lower, dx=b)]
    received = [lower, *received]

    def pair_back(index, into=None, after=()):
        first, part_rows = cuts[index]
        return call(
            functools.partial(pair_back_kernel, R, heads, first),
            [shape(pair_features.shape, BF16), shape((8, 128), F32)],
            "pair_back",
            operands=(pair_features, exps[index], logits, means, inverses, scales, own_scores, back, *received),
            scratch=[
                pltpu.VMEM((block * SLOTS, columns), F32),
                pltpu.VMEM((block // GROUP * columns, GROUP * SLOTS), F32),
                pltpu.VMEM((block // GROUP * columns, GROUP * SLOTS), BF16),
            ],
            grid=(part_rows // block,),
            out_specs=[
                pl.BlockSpec((block, columns, pair_width), lambda i: (first // block + i, 0, 0)),
                pl.BlockSpec((8, 128), lambda i: (0, 0)),
            ],
            into=into,
            after=after,
        )

    sums, early = (), []
    if slim:
        sums = (0, 2)
        early = call(
            gather_kernel,
            [shape((R * columns, width), F32)],
            "gather",
            operands=[collected[a] for a in sums],
        )
    pair_gradient, done = pair_back(0, after=early)
    shares = call(
        functools.partial(fold_kernel, dims, sums),
        [share] * R,
        "fold",
        operands=(*collected, *early),
        after=[done],
    )
    pair_gradient, _ = pair_back(1, into=pair_gradient, after=[shares[0]])
    shares = [shares[0]] + [exchange(m, dx=b) for b, m in enumerate(shares) if b]
    alignment_update, alignment_gradient = call(
        functools.partial(last_kernel, dims),
        [shape(alignment_turned.shape, BF16)] * 2,
        "last",
        operands=(scaled, inverse, alive, wide_gain, *shares),
        scratch=[pltpu.VMEM((columns, R * width), F32)] * 2,
    )
    return by_channel(alignment_update), by_channel(alignment_gradient), pair_gradient


def solution(mesh):
    split = P(("groups", "seq"), ("res", "sub"), None)
    sizes = (mesh.shape["seq"], mesh.shape["res"], mesh.shape["sub"])
    return jax.shard_map(
        functools.partial(shards, *sizes),
        mesh=mesh,
        in_specs=(split, split, split, P(), P(), P(), P(), P(), P())
        + (P(("groups", "seq")), P(("groups", "res", "sub"))),
        out_specs=(split, split, split),
        check_vma=False,
    )
```

```python
import functools

import jax
import jax.numpy as jnp
from jax import lax
from jax.experimental import pallas as pl
from jax.experimental.pallas import tpu as pltpu
from jax.sharding import PartitionSpec as P

F32 = jnp.float32
BF16 = jnp.bfloat16
EPS = 1e-05
QUAD = 4
GROUP = 4
SLOTS = 32
COST = dict(first=1.5, pack=0.1, weights=1.3, pair=2.5, attach=0, pick=0, probs=0, prepare=0, work=0.0, scores=0.0, finish=0, pair_back=0, gather=5, settle=5, fold=0, last=0)
VMEM = 20 * 1024 * 1024


def dot(a, b):
    return jnp.dot(a, b, preferred_element_type=F32)


def dot_nt(a, b):
    return lax.dot_general(a, b, (((1,), (1,)), ((), ())), preferred_element_type=F32)


def dot_tn(a, b):
    return lax.dot_general(a, b, (((0,), (0,)), ((), ())), preferred_element_type=F32)


def iota(shape, dim):
    return lax.broadcasted_iota(jnp.int32, shape, dim)


def split3(value):
    high = value.astype(BF16).astype(F32)
    rest = value - high
    middle = rest.astype(BF16).astype(F32)
    return high, middle, rest - middle


def split2(value):
    high = value.astype(BF16)
    return high, (value - high.astype(F32)).astype(BF16)


def call(kernel, out_shape, name, operands, scratch=(), after=(), grid=None, out_specs=None, into=None):
    whole = pl.BlockSpec(memory_space=pltpu.VMEM)
    count = len(operands)
    body = lambda *refs: kernel(*refs[:count], *refs[count + len(after) :])
    extra = {} if grid is None else {"grid": grid}
    if into is not None:
        extra["input_output_aliases"] = {count + len(after): 0}
        after = [*after, into]
    return pl.pallas_call(
        body,
        out_shape=out_shape,
        in_specs=[whole] * count + [pl.BlockSpec(memory_space=pl.ANY)] * len(after),
        out_specs=out_specs or [whole] * len(out_shape),
        scratch_shapes=list(scratch),
        compiler_params=pltpu.CompilerParams(vmem_limit_bytes=VMEM),
        cost_estimate=pl.CostEstimate(flops=int(COST[name] * 3e9), bytes_accessed=0, transcendentals=0),
        name=name,
        **extra,
    )(*operands, *after)


def shape(dims, dtype):
    return jax.ShapeDtypeStruct(tuple(dims), dtype)


def spread(matrix, channels, depth):
    hidden = matrix.shape[1]
    wide = hidden * QUAD
    row, col = iota((hidden, wide), 0), iota((hidden, wide), 1)
    pick = (row // depth == col // (depth * QUAD)) & (row % depth == col % depth)
    placed = dot(matrix, pick.astype(F32).astype(BF16))
    tall = jnp.concatenate([placed] * QUAD, axis=0)
    row, col = iota(tall.shape, 0), iota(tall.shape, 1)
    return jnp.where(row // channels == (col // depth) % QUAD, tall, 0.0).astype(BF16)


def weights_kernel(
    depth, value_ref, gate_ref, output_ref, bias_ref, gain_ref,
    spread_value, spread_gate, spread_output, moments, squares, centers, back,
):
    channels = value_ref.shape[0]
    spread_value[...] = spread(value_ref[...], channels, depth)
    spread_gate[...] = spread(gate_ref[...], channels, depth)
    spread_output[...] = spread(output_ref[...], channels, depth)
    scaled = bias_ref[...].astype(F32) * gain_ref[...].astype(F32)
    heads, width = scaled.shape
    total = jnp.sum(scaled, axis=1, keepdims=True)
    centers[...] = jnp.broadcast_to(total, (heads, width))
    high, middle, low = split3(scaled)
    tail = (SLOTS - 3 * heads, width)
    row = iota(tail, 0)
    slots = jnp.concatenate([high, middle, low, jnp.where(row < 4, 1.0, 0.0)], axis=0)
    square_slots = jnp.concatenate(
        [jnp.zeros((3 * heads, width), F32), jnp.where(row >= 4, 1.0, 0.0)], axis=0
    )

    def diagonal(tile):
        tall = jnp.concatenate([tile] * GROUP, axis=0)
        full = jnp.concatenate([tall] * GROUP, axis=1)
        row, col = iota(full.shape, 0), iota(full.shape, 1)
        return jnp.where(row // SLOTS == col // tile.shape[1], full, 0.0).astype(BF16)

    moments[...] = diagonal(slots)
    squares[...] = diagonal(square_slots)
    high, middle, _ = split3(scaled - total * (1.0 / width))
    back[...] = diagonal(jnp.concatenate([high, middle, high, jnp.where(row < 3, 1.0, 0.0)], axis=0))


def side_by_side(ref, pair, channels):
    both = jnp.concatenate([ref[2 * pair], ref[2 * pair + 1]], axis=0)
    return jnp.transpose(both.astype(F32))


def averaging(channels):
    row, col = iota((2 * channels, 2 * channels), 0), iota((2 * channels, 2 * channels), 1)
    return jnp.where(row // channels == col // channels, 1.0 / channels, 0.0).astype(BF16)


def average(value, mean_matrix):
    high, low = split2(value)
    return dot(high, mean_matrix) + dot(low, mean_matrix)


def normalized(value, mean_matrix):
    center = value - dot(value.astype(BF16), mean_matrix)
    inverse = lax.rsqrt(average(center * center, mean_matrix) + EPS)
    return center * inverse, inverse


def column(row_value, lanes):
    return jnp.transpose(jnp.broadcast_to(row_value, (lanes, row_value.shape[1])))


def place_of(dims):
    return lax.axis_index("seq"), lax.axis_index("res"), lax.axis_index("sub")


def rows_place(dims):
    Z, R, C, rows, parts, width = dims
    z, x, c = place_of(dims)
    block = z // parts
    return c == lax.rem(block, C), x ^ (block // C), lax.rem(z, parts)


def first_kernel(dims, seq_mask_ref, x_ref, u_ref, gain_ref, token_ref, scaled_out, inverse_out, alive_out, gain_out, *shares):
    Z, R, C, rows, parts, width = dims
    channels, columns = x_ref.shape[1:]
    mean_matrix = averaging(channels)
    live = column(token_ref[...].astype(F32), 2 * channels)
    seq_mask = seq_mask_ref[...].astype(F32)
    gain = jnp.concatenate([gain_ref[...].astype(F32)] * 2, axis=1)
    second_half = iota((1, 2 * channels), 1) >= channels
    normed, masked = [], []
    for pair in range(x_ref.shape[0] // 2):
        at = slice(pair * 2 * channels, (pair + 1) * 2 * channels)
        scaled, inverse = normalized(side_by_side(x_ref, pair, channels), mean_matrix)
        scaled_out[:, at] = scaled
        inverse_out[:, at] = inverse
        normed.append((scaled * gain).astype(BF16))
        keep = jnp.where(
            second_half, seq_mask[:, 2 * pair + 1 : 2 * pair + 2], seq_mask[:, 2 * pair : 2 * pair + 1]
        )
        alive = keep * live
        alive_out[:, at] = alive
        masked.append((side_by_side(u_ref, pair, channels) * alive).astype(BF16))
    gain_out[...] = jnp.broadcast_to(gain, gain_out.shape)
    both = jnp.concatenate(
        [jnp.concatenate(normed, axis=1), jnp.concatenate(masked, axis=1)], axis=0
    )
    x = place_of(dims)[1]
    for b, share in enumerate(shares):
        for group in range(R):

            @pl.when(x ^ b == group)
            def _():
                share[...] = both[:, group * width : (group + 1) * width]


def pack_kernel(dims, slim, *refs):
    Z, R, C, rows, parts, width = dims
    held, messages = refs[:R], refs[R:]
    columns = held[0].shape[0] // 2
    for message in messages:
        for b in range(R):
            message[b * columns : (b + 1) * columns] = held[b][0:columns]
    if slim:
        near = rows_place(dims)[1]
        for far, message in enumerate(messages):
            for b in range(R):

                @pl.when(near ^ far == b)
                def _():
                    message[R * columns :] = held[b][columns:]
    else:
        for b in range(R):
            messages[0][(R + b) * columns : (R + b + 1) * columns] = held[b][columns:]


def pick_kernel(dims, slim, count, *refs):
    Z, R, C, rows, parts, width = dims
    messages, picked, relayed = refs[:count], refs[count], refs[count + 1 :]
    for source, target in zip(messages, relayed):
        target[...] = source[...]
    columns = messages[0].shape[0] // (R + 1 if slim else 2 * R)
    _, block, part = rows_place(dims)
    at = pl.multiple_of(block * columns + part * rows, rows)
    for n, message in enumerate(messages):
        picked[n, 0:rows] = message[pl.ds(at, rows)]
        picked[n, rows : 2 * rows] = message[R * columns :] if slim else message[pl.ds(R * columns + at, rows)]


def pair_kernel(heads, block, first, x_ref, moments, squares, centers, token_ref, *refs):
    before, refs = refs[:-6], refs[-6:]
    e_ref, stat_ref, logit_ref, mean_ref, inverse_ref, scratch = refs
    rows, columns, width = e_ref.shape[1], *x_ref.shape[1:]
    groups = block // GROUP
    padding = 1000000000.0 * (token_ref[...].astype(F32) - 1.0)
    lane = iota((rows, columns), 1)

    def step(index, carry):
        low = pl.multiple_of(index * block, block)
        x = x_ref[pl.ds(first + low, block)].reshape(groups, GROUP, columns, width)
        parts, highs, lows = [], [], []
        for g in range(GROUP):
            part = x[:, g].reshape(groups * columns, width)
            value = part.astype(F32)
            high, rest = split2(value * value)
            parts.append(part)
            highs.append(high)
            lows.append(rest)
        product = dot_nt(
            jnp.concatenate(parts + highs + lows, axis=1),
            jnp.concatenate([moments[...], squares[...], squares[...]], axis=1),
        )
        center = centers[...]
        for group in range(groups):
            turned = jnp.transpose(product[group * columns : (group + 1) * columns])
            for g in range(GROUP):
                i = group * GROUP + g
                base = g * SLOTS
                raw = (
                    turned[base : base + heads]
                    + turned[base + heads : base + 2 * heads]
                    + turned[base + 2 * heads : base + 3 * heads]
                )
                total = turned[base + 3 * heads : base + 3 * heads + 1]
                square = turned[base + 3 * heads + 4 : base + 3 * heads + 5]
                mean = total * (1.0 / width)
                upper = total.astype(BF16).astype(F32)
                lower = total - upper
                spread_sum = (square - upper * upper * (1.0 / width)) - (
                    2.0 * upper * lower + lower * lower
                ) * (1.0 / width)
                inverse = lax.rsqrt(jnp.maximum(spread_sum, 0.0) * (1.0 / width) + EPS)
                scratch[pl.ds(pl.multiple_of((low + i) * heads, heads), heads)] = inverse * (raw - mean * center)
                mean_ref[pl.ds(low + i, 1)] = mean
                inverse_ref[pl.ds(low + i, 1)] = inverse
        return carry

    lax.fori_loop(0, rows // block, step, 0, unroll=True)
    stats = jnp.zeros((rows, columns), F32)
    ones = jnp.ones((columns, columns), BF16)
    for h in range(heads):
        logit = scratch[pl.ds(h, rows, stride=heads), :]
        logit_ref[h] = logit
        logit = logit + padding
        peak = jnp.max(logit, axis=1, keepdims=True)
        e = jnp.exp(logit - peak).astype(BF16)
        e_ref[h] = e
        stats = jnp.where(lane == h, peak, stats)
        stats = jnp.where(lane == 3 * heads + h, dot(e, ones), stats)
    high, middle, rest = split3(stats)
    stats = high + pltpu.roll(middle, heads, 1) + pltpu.roll(rest, 2 * heads, 1)
    stat_ref[first:] = stats.astype(BF16)
    for ref in before:
        stat_ref[0:first] = ref[...]


def thirds(value, heads):
    lane = iota(value.shape, 1)
    high, middle, low = split3(jnp.where(lane < heads, value, 0.0))
    return high + pltpu.roll(middle, heads, 1) + pltpu.roll(low, 2 * heads, 1)


def joined_thirds(stats, heads):
    lanes = stats.shape[1]
    return (
        stats
        + pltpu.roll(stats, lanes - heads, 1)
        + pltpu.roll(stats, lanes - 2 * heads, 1)
    )


def attach_kernel(heads, e_ref, own_ref, other_ref, message):
    size = e_ref.shape[1]
    message[0:heads] = e_ref[...]
    both = own_ref[...].astype(F32) + pltpu.roll(other_ref[...].astype(F32), own_ref.shape[1] // 2, 1)
    for n in range(own_ref.shape[0] // size):
        message[heads + n] = both[n * size : (n + 1) * size].astype(BF16)


def attached(message, heads, rows):
    parts = [message[heads + n] for n in range(rows // message.shape[1])]
    both = jnp.concatenate(parts, axis=0).astype(F32)
    return [both, pltpu.roll(both, both.shape[1] // 2, 1)]


def probs_kernel(R, heads, *refs):
    exps, (probs, scales) = refs[: 2 * R], refs[2 * R :]
    rows, columns = scales.shape[1:]
    exps = [exps[2 * b : 2 * b + 2] for b in range(R)]
    stats = [[joined_thirds(s, heads) for s in attached(lower, heads, rows)] for _, lower in exps]
    near = [pair[0] for pair in stats]
    everything = near + [pair[1] for pair in stats]
    peak = functools.reduce(jnp.maximum, everything)
    total = 0.0
    for s in everything:
        total = total + jnp.exp(s - peak) * pltpu.roll(s, s.shape[1] - 3 * heads, 1)
    for b in range(R):
        scale = jnp.exp(near[b] - peak) / total
        scales[b] = scale
        for h in range(heads):
            low = 0
            for e in exps[b]:
                at = slice(low, low + e.shape[1])
                low += e.shape[1]
                weight = e[h].astype(F32) * scale[at, h : h + 1]
                probs[h, at, b * columns : (b + 1) * columns] = weight.astype(BF16)


def quad(refs, q, rows, lanes):
    per = max(lanes // refs[0].shape[-1], 1)
    return jnp.concatenate([refs[q * per + g][rows] for g in range(per)], axis=1)


def prepare_kernel(dims, heads, mine, other, *refs):
    Z, R, C, rows, parts, width = dims
    n = mine.shape[0]
    messages, refs = refs[:n], refs[n:]
    value_ref, gate_ref, output_ref, values, mixed_grad, gates, grads, gathered = refs
    columns = values.shape[1] // R
    lanes, step = value_ref.shape[0], value_ref.shape[1] // heads
    here, _, _ = rows_place(dims)

    @pl.when(here)
    def _():
        gathered[...] = mine[...]

    @pl.when(jnp.logical_not(here))
    def _():
        gathered[...] = other[...]

    planes = [gathered.at[a] for a in range(n)]
    for q in range(n * width // lanes):
        at = slice(q * step, (q + 1) * step)
        gate = jax.nn.sigmoid(dot(quad(planes, q, slice(0, rows), lanes), gate_ref[...]))
        grad = dot(quad(planes, q, slice(rows, 2 * rows), lanes), output_ref[...])
        product = (gate * grad).astype(BF16)
        gates[q] = gate
        grads[q] = grad
        tokens = dot(quad(messages, q, slice(0, R * columns), lanes), value_ref[...]).astype(BF16)
        for h in range(heads):
            mixed_grad[h, :, at] = product[:, h * step : (h + 1) * step]
            values[h, :, at] = tokens[:, h * step : (h + 1) * step]


def work_kernel(dims, heads, values, mixed_grad, gates, grads, probs, value_ref, gate_ref, output_ref, *refs):
    Z, R, C, rows, parts, width = dims
    keep, send, partial, turned = refs
    n = partial.shape[0]
    step = value_ref.shape[1] // heads
    quads = gates.shape[0]
    per = n // quads
    for h in range(heads):
        sums = dot_tn(probs[h], mixed_grad[h]).astype(BF16)
        for q in range(quads):
            turned[q, :, h * step : (h + 1) * step] = sums[:, q * step : (q + 1) * step]
    for q in range(quads):
        sums = dot_nt(turned[q], value_ref[...])
        for g in range(per):
            partial[q * per + g] = sums[:, g * width : (g + 1) * width]
    for q in range(quads):
        at = slice(q * step, (q + 1) * step)
        gate, grad = gates[q], grads[q]
        mixed = jnp.concatenate([dot(probs[h], values[h, :, at]) for h in range(heads)], axis=1)
        gated = mixed * gate
        gate_grad = (grad * gated * (1.0 - gate)).astype(BF16)
        update = dot_nt(gated.astype(BF16), output_ref[...])
        through = dot_nt(gate_grad, gate_ref[...])
        for g in range(per):
            for low, value in ((0, update), (rows, through)):
                value = value[:, g * width : (g + 1) * width]
                keep[q * per + g, low : low + rows] = value
                send[q * per + g, low : low + rows] = value.astype(BF16)


def finish_kernel(dims, keep, received, partial, *messages):
    Z, R, C, rows, parts, width = dims
    n, tall, _ = partial.shape
    here, block, part = rows_place(dims)
    at = pl.multiple_of(block * (tall // R) + part * rows, rows)
    for a, message in enumerate(messages):
        message[0:tall] = partial[a].astype(BF16)

        @pl.when(here)
        def _():
            both = keep[a] + received[a].astype(F32)
            message[tall:] = both[0:rows].astype(BF16)
            message[pl.ds(at, rows)] = (partial[a, pl.ds(at, rows)] + both[rows:]).astype(BF16)


def scores_kernel(R, heads, count, *refs):
    mixed_grads, refs = refs[:count], refs[count:]
    values, refs = refs[:count], refs[count:]
    scales, *refs = refs
    exps, refs = refs[: 2 * R], refs[2 * R :]
    own_scores, total_ref, *messages = refs
    half = heads // 2
    rows, columns = total_ref.shape
    lane = iota((rows, columns), 1)
    sums = jnp.zeros((rows, columns), F32)
    for h in range(heads):
        scores = dot_nt(
            jnp.concatenate([g[h] for g in mixed_grads], axis=1),
            jnp.concatenate([v[h] for v in values], axis=1),
        )
        total = 0.0
        for b in range(R):
            part = scores[:, b * columns : (b + 1) * columns]
            if b == 0:
                own_scores[h] = part
            else:
                part = part.astype(BF16)
                messages[2 * b - 2 + h // half][h % half] = part
                part = part.astype(F32)
            weight = jnp.concatenate([e[h] for e in exps[2 * b : 2 * b + 2]], axis=0)
            weight = weight.astype(F32) * scales[b][:, h : h + 1]
            total = total + jnp.sum(weight * part, axis=1, keepdims=True)
        for t, part in enumerate(split3(total)):
            sums = jnp.where(lane == t * heads + h, part, sums)
    total_ref[...] = sums.astype(BF16)


def attach_total_kernel(heads, scores_ref, own_ref, other_ref, message):
    count = scores_ref.shape[0]
    message[0:count] = scores_ref[...]
    total = sum(joined_thirds(ref[...].astype(F32), heads) for ref in (own_ref, other_ref))
    message[count] = thirds(total, heads).astype(BF16)


def pair_back_kernel(R, heads, first, x_ref, e_ref, logit_ref, mean_ref, inverse_ref, scale_ref, own_ref, back_ref, *refs):
    own_total, received, refs = refs[0], refs[1 : 2 * R - 1], refs[2 * R - 1 :]
    firsts, seconds, half = received[::2], received[1::2], heads // 2
    out_ref, done_ref, scratch, turned, rounded = refs
    count, columns, width = out_ref.shape
    here = pl.ds(pl.multiple_of(pl.program_id(0) * count, count), count)
    low = pl.multiple_of(first + pl.program_id(0) * count, count)
    at = pl.ds(low, count)
    done_ref[...] = jnp.zeros_like(done_ref)
    total = sum(m[half, at].astype(F32) for m in (own_total, *seconds))
    total = joined_thirds(total, heads)
    scale = scale_ref[0, at]
    inverse = inverse_ref[here]
    cross = 0.0
    for h in range(heads):
        scores = own_ref[h, at]
        for m in (firsts, seconds)[h // half]:
            scores = scores + m[h % half, at].astype(F32)
        prob = e_ref[h, here].astype(F32) * scale[:, h : h + 1]
        grad = prob * (scores - total[:, h : h + 1])
        cross = cross + grad * logit_ref[h, here]
        scaled = grad * inverse
        high = scaled.astype(BF16).astype(F32)
        scratch[pl.ds(h, count, stride=SLOTS), :] = high
        scratch[pl.ds(heads + h, count, stride=SLOTS), :] = high
        scratch[pl.ds(2 * heads + h, count, stride=SLOTS), :] = scaled - high
    factor = inverse * inverse * cross * (1.0 / width)
    rest = [*split3(factor * mean_ref[here]), factor]
    rest += [jnp.zeros_like(factor)] * (SLOTS - 3 * heads - len(rest))
    for t, part in enumerate(rest):
        scratch[pl.ds(3 * heads + t, count, stride=SLOTS), :] = part
    groups = count // GROUP
    for group in range(groups):
        rows = slice(group * columns, (group + 1) * columns)
        tile = jnp.transpose(scratch[group * GROUP * SLOTS : (group + 1) * GROUP * SLOTS])
        turned[rows] = tile
        rounded[rows] = tile.astype(BF16)
    for g in range(0, GROUP, 2):
        product = dot(rounded[...], back_ref[:, g * width : (g + 2) * width])
        for group in range(groups):
            rows = slice(group * columns, (group + 1) * columns)
            for s in range(2):
                i = group * GROUP + g + s
                lane = (g + s) * SLOTS + 3 * heads + 3
                slope = turned[rows, lane : lane + 1] * x_ref[low + i].astype(F32)
                out_ref[i] = (product[rows, s * width : (s + 1) * width] - slope).astype(BF16)


def settle_kernel(out):
    out[...] = jnp.zeros_like(out)


def gather_kernel(one, other, total):
    at = slice(0, total.shape[0])
    total[...] = one[at].astype(F32) + other[at].astype(F32)


def fold_kernel(dims, sums, *refs):
    Z, R, C, rows, parts, width = dims
    messages, refs = refs[:Z], refs[Z:]
    early, shares = refs[:-R], refs[-R:]
    columns = shares[0].shape[0] // 2
    z, x, c = place_of(dims)
    for b, share in enumerate(shares):
        at = slice(b * columns, (b + 1) * columns)
        total = sum(m[at].astype(F32) for a, m in enumerate(messages) if a not in sums)
        share[0:columns] = sum((m[at] for m in early), total).astype(BF16)
        for part in range(parts):
            plane = ((x ^ b) * C + c) * parts + part
            for a, message in enumerate(messages):

                @pl.when(plane ^ z == a)
                def _():
                    share[columns + part * rows : columns + (part + 1) * rows] = message[R * columns :]


def last_kernel(dims, scaled_ref, inverse_ref, alive_ref, gain_ref, *refs):
    Z, R, C, rows, parts, width = dims
    shares, refs = refs[:R], refs[R:]
    update_ref, grad_ref, updates, through = refs
    channels, columns = grad_ref.shape[1:]
    x = place_of(dims)[1]
    for b, share in enumerate(shares):
        at = pl.multiple_of((x ^ b) * width, width)
        through[:, pl.ds(at, width)] = share[0:columns].astype(F32)
        updates[:, pl.ds(at, width)] = share[columns:].astype(F32)
    mean_matrix = averaging(channels)
    gain = gain_ref[0:1]
    for pair in range(grad_ref.shape[0] // 2):
        at = slice(pair * 2 * channels, (pair + 1) * 2 * channels)
        scaled = scaled_ref[:, at]
        grad = through[:, at] * gain
        grad = inverse_ref[:, at] * (
            grad - average(grad, mean_matrix) - scaled * average(grad * scaled, mean_matrix)
        )
        grad = jnp.transpose(grad).astype(BF16)
        update = jnp.transpose(updates[:, at] * alive_ref[:, at]).astype(BF16)
        for s in range(2):
            at = slice(s * channels, (s + 1) * channels)
            grad_ref[2 * pair + s] = grad[at]
            update_ref[2 * pair + s] = update[at]


def shards(
    Z, R, C,
    alignment_input, pair_features, update_cotangent, alignment_norm_gain, pair_norm_gain,
    value_matrix, gate_matrix, output_matrix, head_bias_matrix, sequence_mask, token_padding_mask,
):
    sequences, columns, channels = alignment_input.shape
    rows, _, pair_width = pair_features.shape
    heads = head_bias_matrix.shape[1]
    hidden = value_matrix.shape[1]
    depth = hidden // heads
    parts = columns // rows
    width = sequences // R * channels
    lanes = QUAD * channels
    step = QUAD * depth
    dims = (Z, R, C, rows, parts, width)
    slim = (Z, R, C, parts) == (4, 2, 2, 1)
    everyone = ("seq", "res", "sub")

    def exchange(value, dz=0, dx=0, dc=0):
        at = lambda z, x, c: (z * R + x) * C + c
        places = [(z, x, c) for z in range(Z) for x in range(R) for c in range(C)]
        return lax.ppermute(value, everyone, [(at(z, x, c), at(z ^ dz, x ^ dx, c ^ dc)) for z, x, c in places])

    in_hbm = lambda value: pltpu.with_memory_space_constraint(value, pltpu.HBM)

    gain = in_hbm(alignment_norm_gain.reshape(1, channels))
    by_channel = lambda value: jnp.swapaxes(value, 1, 2)
    alignment_turned = in_hbm(by_channel(alignment_input))
    token_row = in_hbm(token_padding_mask.reshape(1, columns))
    seq_mask = in_hbm(sequence_mask.reshape(1, sequences))
    share = shape((2 * columns, width), BF16)

    kept = shape((columns, sequences * channels), F32)
    scaled, inverse, alive, wide_gain, *held = call(
        functools.partial(first_kernel, dims),
        [kept] * 3 + [shape((8, 2 * channels), F32)] + [share] * R,
        "first",
        operands=(seq_mask, alignment_turned, in_hbm(by_channel(update_cotangent)), gain, token_row),
    )
    first_kept = held[0]
    held = [held[0]] + [exchange(m, dx=b) for b, m in enumerate(held) if b]
    tall = R * columns + (rows if slim else R * columns)

    def pack(after):
        return call(
            functools.partial(pack_kernel, dims, slim),
            [shape((tall, width), BF16)] * (2 if slim else 1),
            "pack",
            operands=held,
            after=after,
        )

    spread_value, spread_gate, spread_output, moments, squares, centers, back = call(
        functools.partial(weights_kernel, depth),
        [shape((lanes, hidden * QUAD), BF16)] * 3
        + [shape((GROUP * SLOTS, GROUP * pair_width), BF16)] * 2
        + [shape((heads, pair_width), F32), shape((GROUP * SLOTS, GROUP * pair_width), BF16)],
        "weights",
        operands=(
            in_hbm(value_matrix), in_hbm(gate_matrix), in_hbm(output_matrix.T), in_hbm(head_bias_matrix.T),
            in_hbm(pair_norm_gain.reshape(1, pair_width)),
        ),
    )

    block = rows // 4
    cuts = ((0, 2 * block), (2 * block, 2 * block))
    def pair(index, before=(), after=()):
        first, size = cuts[index]
        return call(
            functools.partial(pair_kernel, heads, block, first),
            [
                shape((heads, size, columns), BF16),
                shape((first + size, columns), BF16),
                shape((heads, size, columns), F32),
                shape((size, columns), F32),
                shape((size, columns), F32),
            ],
            "pair",
            operands=(pair_features, moments, squares, centers, token_row, *before),
            scratch=[pltpu.VMEM((size * heads, columns), F32)],
            after=after,
        )

    upper, stats, *upper_kept = pair(0, after=[first_kept])
    packed = pack(after=[stats])
    if slim:
        near, away = packed
        arrived = {0: near, 2: exchange(away, dz=2), 1: exchange(near, dz=1)}
    else:
        arrived, stride = {0: packed[0]}, Z // 2
        while stride:
            arrived |= {a ^ stride: exchange(m, dz=stride) for a, m in arrived.items()}
            stride //= 2
    lower, stats, *lower_kept = pair(1, before=[stats], after=packed[:1])
    forward = [(upper, *upper_kept), (lower, *lower_kept)]
    uppers = [upper] + [exchange(upper, dx=b) for b in range(1, R)]
    (lower,) = call(
        functools.partial(attach_kernel, heads),
        [shape((heads + rows // lower.shape[1], *lower.shape[1:]), BF16)],
        "attach",
        operands=(lower, stats, exchange(stats, dc=1)),
        after=uppers[1:],
    )
    lowers = [lower] + [exchange(lower, dx=b) for b in range(1, R)]
    exps = [e for pair_of in zip(uppers, lowers) for e in pair_of]
    phases = [(2,), (0,), (1,), (3,)] if slim else [tuple(range(Z))]
    prepared, unfinished, outgoing = {}, {}, {}

    def pick(phase, relays=0, after=()):
        return call(
            functools.partial(pick_kernel, dims, slim, len(phase)),
            [shape((len(phase), 2 * rows, width), BF16)] + [shape((tall, width), BF16)] * relays,
            "pick",
            after=after,
            operands=[arrived[a] for a in phase],
        )

    def prepare(phase, picked, after=()):
        n = len(phase)
        quads = n * width // lanes
        prepared[phase] = call(
            functools.partial(prepare_kernel, dims, heads),
            [
                shape((heads, R * columns, quads * step), BF16),
                shape((heads, rows, quads * step), BF16),
                shape((quads, rows, heads * step), F32),
                shape((quads, rows, heads * step), F32),
            ],
            "prepare",
            operands=(
                picked, exchange(picked, dc=1), *[arrived[a] for a in phase],
                spread_value, spread_gate, spread_output,
            ),
            scratch=[pltpu.VMEM((n, 2 * rows, width), BF16)],
            after=after,
        )

    def work(phase, after=()):
        n = len(phase)
        keep, send, partial = call(
            functools.partial(work_kernel, dims, heads),
            [
                shape((n, 2 * rows, width), F32),
                shape((n, 2 * rows, width), BF16),
                shape((n, R * columns, width), F32),
            ],
            "work",
            operands=(*prepared[phase], probs, spread_value, spread_gate, spread_output),
            scratch=[pltpu.VMEM((n * width // lanes, R * columns, heads * step), BF16)],
            after=after,
        )
        unfinished[phase] = keep, exchange(send, dc=1), partial

    def finish(phase, after=()):
        finished = call(
            functools.partial(finish_kernel, dims),
            [shape((R * columns + rows, width), BF16)] * len(phase),
            "finish",
            operands=unfinished[phase],
            after=after,
        )
        outgoing.update(zip(phase, finished))

    early_phases = phases[:3]
    first_picked, *relayed = pick(phases[0], relays=int(slim), after=[lower, *arrived.values()][:3 if slim else 1])
    prepare(phases[0], first_picked)
    if slim:
        arrived[3] = exchange(relayed[0], dz=1)
    for phase in early_phases[1:]:
        prepare(phase, *pick(phase, after=[first_picked]))
    probs, scales = call(
        functools.partial(probs_kernel, R, heads),
        [shape((heads, rows, R * columns), BF16), shape((R, rows, columns), F32)],
        "probs",
        operands=exps,
        after=[prepared[phase][1] for phase in early_phases],
    )

    work(phases[0])
    if slim:
        work((1,))
        finish((2,), after=[unfinished[(1,)][2]])
        (picked,) = pick((3,), after=[outgoing[2]])
        work((0,), after=[picked])
        prepare((3,), picked, after=[unfinished[(0,)][2]])
    else:
        finish(phases[0])

    own_scores, own_total, *scores = call(
        functools.partial(scores_kernel, R, heads, len(prepared)),
        [shape((heads, rows, columns), F32), shape((rows, columns), BF16)]
        + [shape((heads // 2, rows, columns), BF16)] * (2 * R - 2),
        "scores",
        after=[],
        operands=(
            *[p[1] for p in prepared.values()], *[p[0] for p in prepared.values()], scales, *exps,
        ),
    )
    other_total = exchange(own_total, dc=1)
    received = []
    for b in range(1, R):
        upper, lower = scores[2 * b - 2 : 2 * b]
        (lower,) = call(
            functools.partial(attach_total_kernel, heads),
            [shape((heads // 2 + 1, rows, columns), BF16)],
            "attach",
            operands=(lower, own_total, other_total),
        )
        received += [exchange(upper, dx=b), exchange(lower, dx=b)]
    if slim:
        work((3,), after=[])
        finish((3,))
        finish((1,), after=[unfinished[(3,)][2]])
        finish((0,))
    received = [lower, *received]
    collected = [exchange(outgoing[a], dz=a) if a else outgoing[a] for a in range(Z)]

    def pair_back(index, into=None, after=()):
        first, part_rows = cuts[index]
        return call(
            functools.partial(pair_back_kernel, R, heads, first),
            [shape(pair_features.shape, BF16), shape((8, 128), F32)],
            "pair_back",
            operands=(pair_features, *forward[index], scales, own_scores, back, *received),
            scratch=[
                pltpu.VMEM((block * SLOTS, columns), F32),
                pltpu.VMEM((block // GROUP * columns, GROUP * SLOTS), F32),
                pltpu.VMEM((block // GROUP * columns, GROUP * SLOTS), BF16),
            ],
            grid=(part_rows // block,),
            out_specs=[
                pl.BlockSpec((block, columns, pair_width), lambda i: (first // block + i, 0, 0)),
                pl.BlockSpec((8, 128), lambda i: (0, 0)),
            ],
            into=into,
            after=after,
        )

    sums, early = (), []
    if slim:
        sums = (0, 2)
        early = call(
            gather_kernel,
            [shape((R * columns, width), F32)],
            "gather",
            operands=[collected[a] for a in sums],
        )
    settled = call(settle_kernel, [shape((8, 128), F32)], "settle", operands=[], after=received[1:])
    pair_gradient, done = pair_back(0, after=[*settled, *early])
    shares = call(
        functools.partial(fold_kernel, dims, sums),
        [share] * R,
        "fold",
        operands=(*collected, *early),
        after=[done],
    )
    pair_gradient, _ = pair_back(1, into=pair_gradient, after=[shares[0]])
    shares = [shares[0]] + [exchange(m, dx=b) for b, m in enumerate(shares) if b]
    alignment_update, alignment_gradient = call(
        functools.partial(last_kernel, dims),
        [shape(alignment_turned.shape, BF16)] * 2,
        "last",
        operands=(scaled, inverse, alive, wide_gain, *shares),
        scratch=[pltpu.VMEM((columns, R * width), F32)] * 2,
    )
    return by_channel(alignment_update), by_channel(alignment_gradient), pair_gradient


def solution(mesh):
    split = P(("groups", "seq"), ("res", "sub"), None)
    sizes = (mesh.shape["seq"], mesh.shape["res"], mesh.shape["sub"])
    return jax.shard_map(
        functools.partial(shards, *sizes),
        mesh=mesh,
        in_specs=(split, split, split, P(), P(), P(), P(), P(), P())
        + (P(("groups", "seq")), P(("groups", "res", "sub"))),
        out_specs=(split, split, split),
        check_vma=False,
    )
```

```python
import functools

import jax
import jax.numpy as jnp
from jax import lax
from jax.experimental import pallas as pl
from jax.experimental.pallas import tpu as pltpu
from jax.sharding import PartitionSpec as P

F32 = jnp.float32
BF16 = jnp.bfloat16
EPS = 1e-05
QUAD = 4
GROUP = 4
SLOTS = 32
BACK_SLOTS = 16
BACK_GROUP = 8
COST = dict(first=1.5, pack=0.1, weights=1.3, pair=2.5, attach=0, pick=0, probs=0, prepare=0, work=0.0, scores=0.0, finish=0, pair_back=0, gather=5, settle=5, fold=0, last=0)
VMEM = 20 * 1024 * 1024


def dot(a, b):
    return jnp.dot(a, b, preferred_element_type=F32)


def dot_nt(a, b):
    return lax.dot_general(a, b, (((1,), (1,)), ((), ())), preferred_element_type=F32)


def dot_tn(a, b):
    return lax.dot_general(a, b, (((0,), (0,)), ((), ())), preferred_element_type=F32)


def iota(shape, dim):
    return lax.broadcasted_iota(jnp.int32, shape, dim)


def split3(value):
    high = value.astype(BF16).astype(F32)
    rest = value - high
    middle = rest.astype(BF16).astype(F32)
    return high, middle, rest - middle


def split2(value):
    high = value.astype(BF16)
    return high, (value - high.astype(F32)).astype(BF16)


def call(kernel, out_shape, name, operands, scratch=(), after=(), grid=None, out_specs=None, into=None):
    whole = pl.BlockSpec(memory_space=pltpu.VMEM)
    count = len(operands)
    body = lambda *refs: kernel(*refs[:count], *refs[count + len(after) :])
    extra = {} if grid is None else {"grid": grid}
    if into is not None:
        extra["input_output_aliases"] = {count + len(after): 0}
        after = [*after, into]
    return pl.pallas_call(
        body,
        out_shape=out_shape,
        in_specs=[whole] * count + [pl.BlockSpec(memory_space=pl.ANY)] * len(after),
        out_specs=out_specs or [whole] * len(out_shape),
        scratch_shapes=list(scratch),
        compiler_params=pltpu.CompilerParams(vmem_limit_bytes=VMEM),
        cost_estimate=pl.CostEstimate(flops=int(COST[name] * 3e9), bytes_accessed=0, transcendentals=0),
        name=name,
        **extra,
    )(*operands, *after)


def shape(dims, dtype):
    return jax.ShapeDtypeStruct(tuple(dims), dtype)


def spread(matrix, channels, depth):
    hidden = matrix.shape[1]
    wide = hidden * QUAD
    row, col = iota((hidden, wide), 0), iota((hidden, wide), 1)
    pick = (row // depth == col // (depth * QUAD)) & (row % depth == col % depth)
    placed = dot(matrix, pick.astype(F32).astype(BF16))
    tall = jnp.concatenate([placed] * QUAD, axis=0)
    row, col = iota(tall.shape, 0), iota(tall.shape, 1)
    return jnp.where(row // channels == (col // depth) % QUAD, tall, 0.0).astype(BF16)


def weights_kernel(
    depth, value_ref, gate_ref, output_ref, bias_ref, gain_ref,
    spread_value, spread_gate, spread_output, moments, squares, centers, back,
):
    channels = value_ref.shape[0]
    spread_value[...] = spread(value_ref[...], channels, depth)
    spread_gate[...] = spread(gate_ref[...], channels, depth)
    spread_output[...] = spread(output_ref[...], channels, depth)
    scaled = bias_ref[...].astype(F32) * gain_ref[...].astype(F32)
    heads, width = scaled.shape
    total = jnp.sum(scaled, axis=1, keepdims=True)
    centers[...] = jnp.broadcast_to(total, (heads, width))
    high, middle, low = split3(scaled)
    tail = (SLOTS - 3 * heads, width)
    row = iota(tail, 0)
    slots = jnp.concatenate([high, middle, low, jnp.where(row < 4, 1.0, 0.0)], axis=0)
    square_slots = jnp.concatenate(
        [jnp.zeros((3 * heads, width), F32), jnp.where(row >= 4, 1.0, 0.0)], axis=0
    )

    def diagonal(tile):
        copies = GROUP * SLOTS // tile.shape[0]
        tall = jnp.concatenate([tile] * copies, axis=0)
        full = jnp.concatenate([tall] * copies, axis=1)
        row, col = iota(full.shape, 0), iota(full.shape, 1)
        return jnp.where(row // tile.shape[0] == col // tile.shape[1], full, 0.0).astype(BF16)

    moments[...] = diagonal(slots)
    squares[...] = diagonal(square_slots)
    row = iota((BACK_SLOTS - heads, width), 0)
    back[...] = diagonal(
        jnp.concatenate([scaled - total * (1.0 / width), jnp.where(row < 3, 1.0, 0.0)], axis=0)
    )


def side_by_side(ref, pair, channels):
    both = jnp.concatenate([ref[2 * pair], ref[2 * pair + 1]], axis=0)
    return jnp.transpose(both.astype(F32))


def averaging(channels):
    row, col = iota((2 * channels, 2 * channels), 0), iota((2 * channels, 2 * channels), 1)
    return jnp.where(row // channels == col // channels, 1.0 / channels, 0.0).astype(BF16)


def average(value, mean_matrix):
    high, low = split2(value)
    return dot(high, mean_matrix) + dot(low, mean_matrix)


def normalized(value, mean_matrix):
    center = value - dot(value.astype(BF16), mean_matrix)
    inverse = lax.rsqrt(average(center * center, mean_matrix) + EPS)
    return center * inverse, inverse


def column(row_value, lanes):
    return jnp.transpose(jnp.broadcast_to(row_value, (lanes, row_value.shape[1])))


def place_of(dims):
    return lax.axis_index("seq"), lax.axis_index("res"), lax.axis_index("sub")


def rows_place(dims):
    Z, R, C, rows, parts, width = dims
    z, x, c = place_of(dims)
    block = z // parts
    return c == lax.rem(block, C), x ^ (block // C), lax.rem(z, parts)


def first_kernel(dims, seq_mask_ref, x_ref, u_ref, gain_ref, token_ref, scaled_out, inverse_out, alive_out, gain_out, *shares):
    Z, R, C, rows, parts, width = dims
    channels, columns = x_ref.shape[1:]
    mean_matrix = averaging(channels)
    live = column(token_ref[...].astype(F32), 2 * channels)
    seq_mask = seq_mask_ref[...].astype(F32)
    gain = jnp.concatenate([gain_ref[...].astype(F32)] * 2, axis=1)
    second_half = iota((1, 2 * channels), 1) >= channels
    normed, masked = [], []
    for pair in range(x_ref.shape[0] // 2):
        at = slice(pair * 2 * channels, (pair + 1) * 2 * channels)
        scaled, inverse = normalized(side_by_side(x_ref, pair, channels), mean_matrix)
        scaled_out[:, at] = scaled
        inverse_out[:, at] = inverse
        normed.append((scaled * gain).astype(BF16))
        keep = jnp.where(
            second_half, seq_mask[:, 2 * pair + 1 : 2 * pair + 2], seq_mask[:, 2 * pair : 2 * pair + 1]
        )
        alive = keep * live
        alive_out[:, at] = alive
        masked.append((side_by_side(u_ref, pair, channels) * alive).astype(BF16))
    gain_out[...] = jnp.broadcast_to(gain, gain_out.shape)
    both = jnp.concatenate(
        [jnp.concatenate(normed, axis=1), jnp.concatenate(masked, axis=1)], axis=0
    )
    x = place_of(dims)[1]
    for b, share in enumerate(shares):
        for group in range(R):

            @pl.when(x ^ b == group)
            def _():
                share[...] = both[:, group * width : (group + 1) * width]


def pack_kernel(dims, slim, *refs):
    Z, R, C, rows, parts, width = dims
    held, messages = refs[:R], refs[R:]
    columns = held[0].shape[0] // 2
    for message in messages:
        for b in range(R):
            message[b * columns : (b + 1) * columns] = held[b][0:columns]
    if slim:
        near = rows_place(dims)[1]
        for far, message in enumerate(messages):
            for b in range(R):

                @pl.when(near ^ far == b)
                def _():
                    message[R * columns :] = held[b][columns:]
    else:
        for b in range(R):
            messages[0][(R + b) * columns : (R + b + 1) * columns] = held[b][columns:]


def pick_kernel(dims, slim, count, *refs):
    Z, R, C, rows, parts, width = dims
    messages, picked, relayed = refs[:count], refs[count], refs[count + 1 :]
    for source, target in zip(messages, relayed):
        target[...] = source[...]
    columns = messages[0].shape[0] // (R + 1 if slim else 2 * R)
    _, block, part = rows_place(dims)
    at = pl.multiple_of(block * columns + part * rows, rows)
    for n, message in enumerate(messages):
        picked[n, 0:rows] = message[pl.ds(at, rows)]
        picked[n, rows : 2 * rows] = message[R * columns :] if slim else message[pl.ds(R * columns + at, rows)]


def pair_kernel(heads, block, first, x_ref, moments, squares, centers, token_ref, *refs):
    before, refs = refs[:-6], refs[-6:]
    e_ref, stat_ref, logit_ref, mean_ref, inverse_ref, scratch = refs
    rows, columns, width = e_ref.shape[1], *x_ref.shape[1:]
    groups = block // GROUP
    padding = 1000000000.0 * (token_ref[...].astype(F32) - 1.0)
    lane = iota((rows, columns), 1)

    def step(index, carry):
        low = pl.multiple_of(index * block, block)
        x = x_ref[pl.ds(first + low, block)].reshape(groups, GROUP, columns, width)
        parts, highs, lows = [], [], []
        for g in range(GROUP):
            part = x[:, g].reshape(groups * columns, width)
            value = part.astype(F32)
            high, rest = split2(value * value)
            parts.append(part)
            highs.append(high)
            lows.append(rest)
        product = dot_nt(
            jnp.concatenate(parts + highs + lows, axis=1),
            jnp.concatenate([moments[...], squares[...], squares[...]], axis=1),
        )
        center = centers[...]
        for group in range(groups):
            turned = jnp.transpose(product[group * columns : (group + 1) * columns])
            for g in range(GROUP):
                i = group * GROUP + g
                base = g * SLOTS
                raw = (
                    turned[base : base + heads]
                    + turned[base + heads : base + 2 * heads]
                    + turned[base + 2 * heads : base + 3 * heads]
                )
                total = turned[base + 3 * heads : base + 3 * heads + 1]
                square = turned[base + 3 * heads + 4 : base + 3 * heads + 5]
                mean = total * (1.0 / width)
                upper = total.astype(BF16).astype(F32)
                lower = total - upper
                spread_sum = (square - upper * upper * (1.0 / width)) - (
                    2.0 * upper * lower + lower * lower
                ) * (1.0 / width)
                inverse = lax.rsqrt(jnp.maximum(spread_sum, 0.0) * (1.0 / width) + EPS)
                scratch[pl.ds(pl.multiple_of((low + i) * heads, heads), heads)] = inverse * (raw - mean * center)
                mean_ref[pl.ds(low + i, 1)] = mean
                inverse_ref[pl.ds(low + i, 1)] = inverse
        return carry

    lax.fori_loop(0, rows // block, step, 0, unroll=True)
    stats = jnp.zeros((rows, columns), F32)
    ones = jnp.ones((columns, columns), BF16)
    for h in range(heads):
        logit = scratch[pl.ds(h, rows, stride=heads), :]
        logit_ref[h] = logit
        logit = logit + padding
        peak = jnp.max(logit, axis=1, keepdims=True)
        e = jnp.exp(logit - peak).astype(BF16)
        e_ref[h] = e
        stats = jnp.where(lane == h, peak, stats)
        stats = jnp.where(lane == 3 * heads + h, dot(e, ones), stats)
    high, middle, rest = split3(stats)
    stats = high + pltpu.roll(middle, heads, 1) + pltpu.roll(rest, 2 * heads, 1)
    stat_ref[first:] = stats.astype(BF16)
    for ref in before:
        stat_ref[0:first] = ref[...]


def thirds(value, heads):
    lane = iota(value.shape, 1)
    high, middle, low = split3(jnp.where(lane < heads, value, 0.0))
    return high + pltpu.roll(middle, heads, 1) + pltpu.roll(low, 2 * heads, 1)


def joined_thirds(stats, heads):
    lanes = stats.shape[1]
    return (
        stats
        + pltpu.roll(stats, lanes - heads, 1)
        + pltpu.roll(stats, lanes - 2 * heads, 1)
    )


def attach_kernel(heads, e_ref, own_ref, other_ref, message):
    size = e_ref.shape[1]
    message[0:heads] = e_ref[...]
    both = own_ref[...].astype(F32) + pltpu.roll(other_ref[...].astype(F32), own_ref.shape[1] // 2, 1)
    for n in range(own_ref.shape[0] // size):
        message[heads + n] = both[n * size : (n + 1) * size].astype(BF16)


def attached(message, heads, rows):
    parts = [message[heads + n] for n in range(rows // message.shape[1])]
    both = jnp.concatenate(parts, axis=0).astype(F32)
    return [both, pltpu.roll(both, both.shape[1] // 2, 1)]


def probs_kernel(R, heads, *refs):
    exps, (probs, scales) = refs[: 2 * R], refs[2 * R :]
    rows, columns = scales.shape[1:]
    exps = [exps[2 * b : 2 * b + 2] for b in range(R)]
    stats = [[joined_thirds(s, heads) for s in attached(lower, heads, rows)] for _, lower in exps]
    near = [pair[0] for pair in stats]
    everything = near + [pair[1] for pair in stats]
    peak = functools.reduce(jnp.maximum, everything)
    total = 0.0
    for s in everything:
        total = total + jnp.exp(s - peak) * pltpu.roll(s, s.shape[1] - 3 * heads, 1)
    for b in range(R):
        scale = jnp.exp(near[b] - peak) / total
        scales[b] = scale
        for h in range(heads):
            low = 0
            for e in exps[b]:
                at = slice(low, low + e.shape[1])
                low += e.shape[1]
                weight = e[h].astype(F32) * scale[at, h : h + 1]
                probs[h, at, b * columns : (b + 1) * columns] = weight.astype(BF16)


def quad(refs, q, rows, lanes):
    per = max(lanes // refs[0].shape[-1], 1)
    return jnp.concatenate([refs[q * per + g][rows] for g in range(per)], axis=1)


def prepare_kernel(dims, heads, mine, other, *refs):
    Z, R, C, rows, parts, width = dims
    n = mine.shape[0]
    messages, refs = refs[:n], refs[n:]
    value_ref, gate_ref, output_ref, values, mixed_grad, gates, grads, gathered = refs
    columns = values.shape[1] // R
    lanes, step = value_ref.shape[0], value_ref.shape[1] // heads
    here, _, _ = rows_place(dims)

    @pl.when(here)
    def _():
        gathered[...] = mine[...]

    @pl.when(jnp.logical_not(here))
    def _():
        gathered[...] = other[...]

    planes = [gathered.at[a] for a in range(n)]
    for q in range(n * width // lanes):
        at = slice(q * step, (q + 1) * step)
        gate = jax.nn.sigmoid(dot(quad(planes, q, slice(0, rows), lanes), gate_ref[...]))
        grad = dot(quad(planes, q, slice(rows, 2 * rows), lanes), output_ref[...])
        product = (gate * grad).astype(BF16)
        gates[q] = gate
        grads[q] = grad
        tokens = dot(quad(messages, q, slice(0, R * columns), lanes), value_ref[...]).astype(BF16)
        for h in range(heads):
            mixed_grad[h, :, at] = product[:, h * step : (h + 1) * step]
            values[h, :, at] = tokens[:, h * step : (h + 1) * step]


def work_kernel(dims, heads, values, mixed_grad, gates, grads, probs, value_ref, gate_ref, output_ref, *refs):
    Z, R, C, rows, parts, width = dims
    keep, send, partial, turned = refs
    n = partial.shape[0]
    step = value_ref.shape[1] // heads
    quads = gates.shape[0]
    per = n // quads
    for h in range(heads):
        sums = dot_tn(probs[h], mixed_grad[h]).astype(BF16)
        for q in range(quads):
            turned[q, :, h * step : (h + 1) * step] = sums[:, q * step : (q + 1) * step]
    for q in range(quads):
        sums = dot_nt(turned[q], value_ref[...])
        for g in range(per):
            partial[q * per + g] = sums[:, g * width : (g + 1) * width]
    for q in range(quads):
        at = slice(q * step, (q + 1) * step)
        gate, grad = gates[q], grads[q]
        mixed = jnp.concatenate([dot(probs[h], values[h, :, at]) for h in range(heads)], axis=1)
        gated = mixed * gate
        gate_grad = (grad * gated * (1.0 - gate)).astype(BF16)
        update = dot_nt(gated.astype(BF16), output_ref[...])
        through = dot_nt(gate_grad, gate_ref[...])
        for g in range(per):
            for low, value in ((0, update), (rows, through)):
                value = value[:, g * width : (g + 1) * width]
                keep[q * per + g, low : low + rows] = value
                send[q * per + g, low : low + rows] = value.astype(BF16)


def finish_kernel(dims, keep, received, partial, *messages):
    Z, R, C, rows, parts, width = dims
    n, tall, _ = partial.shape
    here, block, part = rows_place(dims)
    at = pl.multiple_of(block * (tall // R) + part * rows, rows)
    for a, message in enumerate(messages):
        message[0:tall] = partial[a].astype(BF16)

        @pl.when(here)
        def _():
            both = keep[a] + received[a].astype(F32)
            message[tall:] = both[0:rows].astype(BF16)
            message[pl.ds(at, rows)] = (partial[a, pl.ds(at, rows)] + both[rows:]).astype(BF16)


def scores_kernel(R, heads, count, *refs):
    mixed_grads, refs = refs[:count], refs[count:]
    values, refs = refs[:count], refs[count:]
    scales, *refs = refs
    exps, refs = refs[: 2 * R], refs[2 * R :]
    own_scores, total_ref, *messages = refs
    half = heads // 2
    rows, columns = total_ref.shape
    lane = iota((rows, columns), 1)
    sums = jnp.zeros((rows, columns), F32)
    for h in range(heads):
        scores = dot_nt(
            jnp.concatenate([g[h] for g in mixed_grads], axis=1),
            jnp.concatenate([v[h] for v in values], axis=1),
        )
        total = 0.0
        for b in range(R):
            part = scores[:, b * columns : (b + 1) * columns]
            if b == 0:
                own_scores[h] = part
            else:
                part = part.astype(BF16)
                messages[2 * b - 2 + h // half][h % half] = part
                part = part.astype(F32)
            weight = jnp.concatenate([e[h] for e in exps[2 * b : 2 * b + 2]], axis=0)
            weight = weight.astype(F32) * scales[b][:, h : h + 1]
            total = total + jnp.sum(weight * part, axis=1, keepdims=True)
        for t, part in enumerate(split3(total)):
            sums = jnp.where(lane == t * heads + h, part, sums)
    total_ref[...] = sums.astype(BF16)


def attach_total_kernel(heads, scores_ref, own_ref, other_ref, message):
    count = scores_ref.shape[0]
    message[0:count] = scores_ref[...]
    total = sum(joined_thirds(ref[...].astype(F32), heads) for ref in (own_ref, other_ref))
    message[count] = thirds(total, heads).astype(BF16)


def pair_back_kernel(R, heads, first, x_ref, e_ref, logit_ref, mean_ref, inverse_ref, scale_ref, own_ref, back_ref, *refs):
    own_total, received, refs = refs[0], refs[1 : 2 * R - 1], refs[2 * R - 1 :]
    firsts, seconds, half = received[::2], received[1::2], heads // 2
    out_ref, done_ref, scratch, turned, rounded = refs
    count, columns, width = out_ref.shape
    here = pl.ds(pl.multiple_of(pl.program_id(0) * count, count), count)
    low = pl.multiple_of(first + pl.program_id(0) * count, count)
    at = pl.ds(low, count)
    done_ref[...] = jnp.zeros_like(done_ref)
    total = sum(m[half, at].astype(F32) for m in (own_total, *seconds))
    total = joined_thirds(total, heads)
    scale = scale_ref[0, at]
    inverse = inverse_ref[here]
    cross = 0.0
    for h in range(heads):
        scores = own_ref[h, at]
        for m in (firsts, seconds)[h // half]:
            scores = scores + m[h % half, at].astype(F32)
        prob = e_ref[h, here].astype(F32) * scale[:, h : h + 1]
        grad = prob * (scores - total[:, h : h + 1])
        cross = cross + grad * logit_ref[h, here]
        scratch[pl.ds(h, count, stride=BACK_SLOTS), :] = grad * inverse
    factor = inverse * inverse * cross * (1.0 / width)
    rest = [*split3(factor * mean_ref[here]), factor]
    rest += [jnp.zeros_like(factor)] * (BACK_SLOTS - heads - len(rest))
    for t, part in enumerate(rest):
        scratch[pl.ds(heads + t, count, stride=BACK_SLOTS), :] = part
    groups = count // BACK_GROUP
    size = BACK_GROUP * BACK_SLOTS
    for group in range(groups):
        rows = slice(group * columns, (group + 1) * columns)
        tile = jnp.transpose(scratch[group * size : (group + 1) * size])
        turned[rows] = tile
        rounded[rows] = tile.astype(BF16)
    for g in range(0, BACK_GROUP, 2):
        product = dot(rounded[...], back_ref[:, g * width : (g + 2) * width])
        for group in range(groups):
            rows = slice(group * columns, (group + 1) * columns)
            for s in range(2):
                i = group * BACK_GROUP + g + s
                lane = (g + s) * BACK_SLOTS + heads + 3
                slope = turned[rows, lane : lane + 1] * x_ref[low + i].astype(F32)
                out_ref[i] = (product[rows, s * width : (s + 1) * width] - slope).astype(BF16)


def settle_kernel(out):
    out[...] = jnp.zeros_like(out)


def gather_kernel(one, other, total):
    at = slice(0, total.shape[0])
    total[...] = one[at].astype(F32) + other[at].astype(F32)


def fold_kernel(dims, sums, *refs):
    Z, R, C, rows, parts, width = dims
    messages, refs = refs[:Z], refs[Z:]
    early, shares = refs[:-R], refs[-R:]
    columns = shares[0].shape[0] // 2
    z, x, c = place_of(dims)
    for b, share in enumerate(shares):
        at = slice(b * columns, (b + 1) * columns)
        total = sum(m[at].astype(F32) for a, m in enumerate(messages) if a not in sums)
        share[0:columns] = sum((m[at] for m in early), total).astype(BF16)
        for part in range(parts):
            plane = ((x ^ b) * C + c) * parts + part
            for a, message in enumerate(messages):

                @pl.when(plane ^ z == a)
                def _():
                    share[columns + part * rows : columns + (part + 1) * rows] = message[R * columns :]


def last_kernel(dims, scaled_ref, inverse_ref, alive_ref, gain_ref, *refs):
    Z, R, C, rows, parts, width = dims
    shares, refs = refs[:R], refs[R:]
    update_ref, grad_ref, updates, through = refs
    channels, columns = grad_ref.shape[1:]
    x = place_of(dims)[1]
    for b, share in enumerate(shares):
        at = pl.multiple_of((x ^ b) * width, width)
        through[:, pl.ds(at, width)] = share[0:columns].astype(F32)
        updates[:, pl.ds(at, width)] = share[columns:].astype(F32)
    mean_matrix = averaging(channels)
    gain = gain_ref[0:1]
    for pair in range(grad_ref.shape[0] // 2):
        at = slice(pair * 2 * channels, (pair + 1) * 2 * channels)
        scaled = scaled_ref[:, at]
        grad = through[:, at] * gain
        grad = inverse_ref[:, at] * (
            grad - average(grad, mean_matrix) - scaled * average(grad * scaled, mean_matrix)
        )
        grad = jnp.transpose(grad).astype(BF16)
        update = jnp.transpose(updates[:, at] * alive_ref[:, at]).astype(BF16)
        for s in range(2):
            at = slice(s * channels, (s + 1) * channels)
            grad_ref[2 * pair + s] = grad[at]
            update_ref[2 * pair + s] = update[at]


def shards(
    Z, R, C,
    alignment_input, pair_features, update_cotangent, alignment_norm_gain, pair_norm_gain,
    value_matrix, gate_matrix, output_matrix, head_bias_matrix, sequence_mask, token_padding_mask,
):
    sequences, columns, channels = alignment_input.shape
    rows, _, pair_width = pair_features.shape
    heads = head_bias_matrix.shape[1]
    hidden = value_matrix.shape[1]
    depth = hidden // heads
    parts = columns // rows
    width = sequences // R * channels
    lanes = QUAD * channels
    step = QUAD * depth
    dims = (Z, R, C, rows, parts, width)
    slim = (Z, R, C, parts) == (4, 2, 2, 1)
    everyone = ("seq", "res", "sub")

    def exchange(value, dz=0, dx=0, dc=0):
        at = lambda z, x, c: (z * R + x) * C + c
        places = [(z, x, c) for z in range(Z) for x in range(R) for c in range(C)]
        return lax.ppermute(value, everyone, [(at(z, x, c), at(z ^ dz, x ^ dx, c ^ dc)) for z, x, c in places])

    in_hbm = lambda value: pltpu.with_memory_space_constraint(value, pltpu.HBM)

    gain = in_hbm(alignment_norm_gain.reshape(1, channels))
    by_channel = lambda value: jnp.swapaxes(value, 1, 2)
    alignment_turned = in_hbm(by_channel(alignment_input))
    token_row = in_hbm(token_padding_mask.reshape(1, columns))
    seq_mask = in_hbm(sequence_mask.reshape(1, sequences))
    share = shape((2 * columns, width), BF16)

    kept = shape((columns, sequences * channels), F32)
    scaled, inverse, alive, wide_gain, *held = call(
        functools.partial(first_kernel, dims),
        [kept] * 3 + [shape((8, 2 * channels), F32)] + [share] * R,
        "first",
        operands=(seq_mask, alignment_turned, in_hbm(by_channel(update_cotangent)), gain, token_row),
    )
    first_kept = held[0]
    held = [held[0]] + [exchange(m, dx=b) for b, m in enumerate(held) if b]
    tall = R * columns + (rows if slim else R * columns)

    def pack(after):
        return call(
            functools.partial(pack_kernel, dims, slim),
            [shape((tall, width), BF16)] * (2 if slim else 1),
            "pack",
            operands=held,
            after=after,
        )

    spread_value, spread_gate, spread_output, moments, squares, centers, back = call(
        functools.partial(weights_kernel, depth),
        [shape((lanes, hidden * QUAD), BF16)] * 3
        + [shape((GROUP * SLOTS, GROUP * pair_width), BF16)] * 2
        + [shape((heads, pair_width), F32), shape((BACK_GROUP * BACK_SLOTS, BACK_GROUP * pair_width), BF16)],
        "weights",
        operands=(
            in_hbm(value_matrix), in_hbm(gate_matrix), in_hbm(output_matrix.T), in_hbm(head_bias_matrix.T),
            in_hbm(pair_norm_gain.reshape(1, pair_width)),
        ),
    )

    block = rows // 4
    cuts = ((0, 2 * block), (2 * block, 2 * block))
    def pair(index, before=(), after=()):
        first, size = cuts[index]
        return call(
            functools.partial(pair_kernel, heads, block, first),
            [
                shape((heads, size, columns), BF16),
                shape((first + size, columns), BF16),
                shape((heads, size, columns), F32),
                shape((size, columns), F32),
                shape((size, columns), F32),
            ],
            "pair",
            operands=(pair_features, moments, squares, centers, token_row, *before),
            scratch=[pltpu.VMEM((size * heads, columns), F32)],
            after=after,
        )

    upper, stats, *upper_kept = pair(0, after=[first_kept])
    packed = pack(after=[stats])
    if slim:
        near, away = packed
        arrived = {0: near, 2: exchange(away, dz=2), 1: exchange(near, dz=1)}
    else:
        arrived, stride = {0: packed[0]}, Z // 2
        while stride:
            arrived |= {a ^ stride: exchange(m, dz=stride) for a, m in arrived.items()}
            stride //= 2
    lower, stats, *lower_kept = pair(1, before=[stats], after=packed[:1])
    forward = [(upper, *upper_kept), (lower, *lower_kept)]
    uppers = [upper] + [exchange(upper, dx=b) for b in range(1, R)]
    (lower,) = call(
        functools.partial(attach_kernel, heads),
        [shape((heads + rows // lower.shape[1], *lower.shape[1:]), BF16)],
        "attach",
        operands=(lower, stats, exchange(stats, dc=1)),
        after=uppers[1:],
    )
    lowers = [lower] + [exchange(lower, dx=b) for b in range(1, R)]
    exps = [e for pair_of in zip(uppers, lowers) for e in pair_of]
    phases = [(2,), (0,), (1,), (3,)] if slim else [tuple(range(Z))]
    prepared, unfinished, outgoing = {}, {}, {}

    def pick(phase, relays=0, after=()):
        return call(
            functools.partial(pick_kernel, dims, slim, len(phase)),
            [shape((len(phase), 2 * rows, width), BF16)] + [shape((tall, width), BF16)] * relays,
            "pick",
            after=after,
            operands=[arrived[a] for a in phase],
        )

    def prepare(phase, picked, after=()):
        n = len(phase)
        quads = n * width // lanes
        prepared[phase] = call(
            functools.partial(prepare_kernel, dims, heads),
            [
                shape((heads, R * columns, quads * step), BF16),
                shape((heads, rows, quads * step), BF16),
                shape((quads, rows, heads * step), F32),
                shape((quads, rows, heads * step), F32),
            ],
            "prepare",
            operands=(
                picked, exchange(picked, dc=1), *[arrived[a] for a in phase],
                spread_value, spread_gate, spread_output,
            ),
            scratch=[pltpu.VMEM((n, 2 * rows, width), BF16)],
            after=after,
        )

    def work(phase, after=()):
        n = len(phase)
        keep, send, partial = call(
            functools.partial(work_kernel, dims, heads),
            [
                shape((n, 2 * rows, width), F32),
                shape((n, 2 * rows, width), BF16),
                shape((n, R * columns, width), F32),
            ],
            "work",
            operands=(*prepared[phase], probs, spread_value, spread_gate, spread_output),
            scratch=[pltpu.VMEM((n * width // lanes, R * columns, heads * step), BF16)],
            after=after,
        )
        unfinished[phase] = keep, exchange(send, dc=1), partial

    def finish(phase, after=()):
        finished = call(
            functools.partial(finish_kernel, dims),
            [shape((R * columns + rows, width), BF16)] * len(phase),
            "finish",
            operands=unfinished[phase],
            after=after,
        )
        outgoing.update(zip(phase, finished))

    early_phases = phases[:3]
    first_picked, *relayed = pick(phases[0], relays=int(slim), after=[lower, *arrived.values()][:3 if slim else 1])
    prepare(phases[0], first_picked)
    if slim:
        arrived[3] = exchange(relayed[0], dz=1)
    for phase in early_phases[1:]:
        prepare(phase, *pick(phase, after=[first_picked]))
    probs, scales = call(
        functools.partial(probs_kernel, R, heads),
        [shape((heads, rows, R * columns), BF16), shape((R, rows, columns), F32)],
        "probs",
        operands=exps,
        after=[prepared[phase][1] for phase in early_phases[:2]],
    )

    work(phases[0])
    if slim:
        work((1,))
        finish((2,), after=[unfinished[(1,)][2]])
        (picked,) = pick((3,), after=[outgoing[2]])
        work((0,), after=[picked])
        prepare((3,), picked, after=[unfinished[(0,)][2]])
    else:
        finish(phases[0])

    own_scores, own_total, *scores = call(
        functools.partial(scores_kernel, R, heads, len(prepared)),
        [shape((heads, rows, columns), F32), shape((rows, columns), BF16)]
        + [shape((heads // 2, rows, columns), BF16)] * (2 * R - 2),
        "scores",
        after=[],
        operands=(
            *[p[1] for p in prepared.values()], *[p[0] for p in prepared.values()], scales, *exps,
        ),
    )
    other_total = exchange(own_total, dc=1)
    received = []
    for b in range(1, R):
        upper, lower = scores[2 * b - 2 : 2 * b]
        (lower,) = call(
            functools.partial(attach_total_kernel, heads),
            [shape((heads // 2 + 1, rows, columns), BF16)],
            "attach",
            operands=(lower, own_total, other_total),
        )
        received += [exchange(upper, dx=b), exchange(lower, dx=b)]
    if slim:
        work((3,), after=[])
        finish((3,))
        finish((1,), after=[unfinished[(3,)][2]])
        finish((0,))
    received = [lower, *received]
    collected = [exchange(outgoing[a], dz=a) if a else outgoing[a] for a in range(Z)]

    def pair_back(index, into=None, after=()):
        first, part_rows = cuts[index]
        return call(
            functools.partial(pair_back_kernel, R, heads, first),
            [shape(pair_features.shape, BF16), shape((8, 128), F32)],
            "pair_back",
            operands=(pair_features, *forward[index], scales, own_scores, back, *received),
            scratch=[
                pltpu.VMEM((block * BACK_SLOTS, columns), F32),
                pltpu.VMEM((block // BACK_GROUP * columns, BACK_GROUP * BACK_SLOTS), F32),
                pltpu.VMEM((block // BACK_GROUP * columns, BACK_GROUP * BACK_SLOTS), BF16),
            ],
            grid=(part_rows // block,),
            out_specs=[
                pl.BlockSpec((block, columns, pair_width), lambda i: (first // block + i, 0, 0)),
                pl.BlockSpec((8, 128), lambda i: (0, 0)),
            ],
            into=into,
            after=after,
        )

    sums, early = (), []
    if slim:
        sums = (0, 2)
        early = call(
            gather_kernel,
            [shape((R * columns, width), F32)],
            "gather",
            operands=[collected[a] for a in sums],
        )
    settled = call(settle_kernel, [shape((8, 128), F32)], "settle", operands=[], after=received[1:])
    pair_gradient, done = pair_back(0, after=[*settled, *early])
    shares = call(
        functools.partial(fold_kernel, dims, sums),
        [share] * R,
        "fold",
        operands=(*collected, *early),
        after=[done],
    )
    pair_gradient, _ = pair_back(1, into=pair_gradient, after=[shares[0]])
    shares = [shares[0]] + [exchange(m, dx=b) for b, m in enumerate(shares) if b]
    alignment_update, alignment_gradient = call(
        functools.partial(last_kernel, dims),
        [shape(alignment_turned.shape, BF16)] * 2,
        "last",
        operands=(scaled, inverse, alive, wide_gain, *shares),
        scratch=[pltpu.VMEM((columns, R * width), F32)] * 2,
    )
    return by_channel(alignment_update), by_channel(alignment_gradient), pair_gradient


def solution(mesh):
    split = P(("groups", "seq"), ("res", "sub"), None)
    sizes = (mesh.shape["seq"], mesh.shape["res"], mesh.shape["sub"])
    return jax.shard_map(
        functools.partial(shards, *sizes),
        mesh=mesh,
        in_specs=(split, split, split, P(), P(), P(), P(), P(), P())
        + (P(("groups", "seq")), P(("groups", "res", "sub"))),
        out_specs=(split, split, split),
        check_vma=False,
    )
```

```python
import functools

import jax
import jax.numpy as jnp
from jax import lax
from jax.experimental import pallas as pl
from jax.experimental.pallas import tpu as pltpu
from jax.sharding import PartitionSpec as P

F32 = jnp.float32
BF16 = jnp.bfloat16
EPS = 1e-05
QUAD = 4
GROUP = 4
SLOTS = 32
BACK_SLOTS = 16
BACK_GROUP = 8
TOTAL_LANES = 32
COST = dict(first=1.5, pack=0.1, weights=1.3, pair=2.5, attach=0, pick=0, probs=0, prepare=0, work=0.0, scores=0.0, finish=0, pair_back=0, gather=5, settle=5, fold=0, last=0)
VMEM = 20 * 1024 * 1024


def dot(a, b):
    return jnp.dot(a, b, preferred_element_type=F32)


def dot_nt(a, b):
    return lax.dot_general(a, b, (((1,), (1,)), ((), ())), preferred_element_type=F32)


def dot_tn(a, b):
    return lax.dot_general(a, b, (((0,), (0,)), ((), ())), preferred_element_type=F32)


def iota(shape, dim):
    return lax.broadcasted_iota(jnp.int32, shape, dim)


def split3(value):
    high = value.astype(BF16).astype(F32)
    rest = value - high
    middle = rest.astype(BF16).astype(F32)
    return high, middle, rest - middle


def split2(value):
    high = value.astype(BF16)
    return high, (value - high.astype(F32)).astype(BF16)


def call(kernel, out_shape, name, operands, scratch=(), after=(), grid=None, out_specs=None, into=None):
    whole = pl.BlockSpec(memory_space=pltpu.VMEM)
    count = len(operands)
    body = lambda *refs: kernel(*refs[:count], *refs[count + len(after) :])
    extra = {} if grid is None else {"grid": grid}
    if into is not None:
        extra["input_output_aliases"] = {count + len(after): 0}
        after = [*after, into]
    return pl.pallas_call(
        body,
        out_shape=out_shape,
        in_specs=[whole] * count + [pl.BlockSpec(memory_space=pl.ANY)] * len(after),
        out_specs=out_specs or [whole] * len(out_shape),
        scratch_shapes=list(scratch),
        compiler_params=pltpu.CompilerParams(vmem_limit_bytes=VMEM),
        cost_estimate=pl.CostEstimate(flops=int(COST[name] * 3e9), bytes_accessed=0, transcendentals=0),
        name=name,
        **extra,
    )(*operands, *after)


def shape(dims, dtype):
    return jax.ShapeDtypeStruct(tuple(dims), dtype)


def spread(matrix, channels, depth):
    hidden = matrix.shape[1]
    wide = hidden * QUAD
    row, col = iota((hidden, wide), 0), iota((hidden, wide), 1)
    pick = (row // depth == col // (depth * QUAD)) & (row % depth == col % depth)
    placed = dot(matrix, pick.astype(F32).astype(BF16))
    tall = jnp.concatenate([placed] * QUAD, axis=0)
    row, col = iota(tall.shape, 0), iota(tall.shape, 1)
    return jnp.where(row // channels == (col // depth) % QUAD, tall, 0.0).astype(BF16)


def weights_kernel(
    depth, value_ref, gate_ref, output_ref, bias_ref, gain_ref,
    spread_value, spread_gate, spread_output, moments, squares, centers, back,
):
    channels = value_ref.shape[0]
    spread_value[...] = spread(value_ref[...], channels, depth)
    spread_gate[...] = spread(gate_ref[...], channels, depth)
    spread_output[...] = spread(output_ref[...], channels, depth)
    scaled = bias_ref[...].astype(F32) * gain_ref[...].astype(F32)
    heads, width = scaled.shape
    total = jnp.sum(scaled, axis=1, keepdims=True)
    centers[...] = jnp.broadcast_to(total, (heads, width))
    high, middle, low = split3(scaled)
    tail = (SLOTS - 3 * heads, width)
    row = iota(tail, 0)
    slots = jnp.concatenate([high, middle, low, jnp.where(row < 4, 1.0, 0.0)], axis=0)
    square_slots = jnp.concatenate(
        [jnp.zeros((3 * heads, width), F32), jnp.where(row >= 4, 1.0, 0.0)], axis=0
    )

    def diagonal(tile):
        copies = GROUP * SLOTS // tile.shape[0]
        tall = jnp.concatenate([tile] * copies, axis=0)
        full = jnp.concatenate([tall] * copies, axis=1)
        row, col = iota(full.shape, 0), iota(full.shape, 1)
        return jnp.where(row // tile.shape[0] == col // tile.shape[1], full, 0.0).astype(BF16)

    moments[...] = diagonal(slots)
    squares[...] = diagonal(square_slots)
    row = iota((BACK_SLOTS - heads, width), 0)
    back[...] = diagonal(
        jnp.concatenate([scaled - total * (1.0 / width), jnp.where(row < 3, 1.0, 0.0)], axis=0)
    )


def side_by_side(ref, pair, channels):
    both = jnp.concatenate([ref[2 * pair], ref[2 * pair + 1]], axis=0)
    return jnp.transpose(both.astype(F32))


def averaging(channels):
    row, col = iota((2 * channels, 2 * channels), 0), iota((2 * channels, 2 * channels), 1)
    return jnp.where(row // channels == col // channels, 1.0 / channels, 0.0).astype(BF16)


def average(value, mean_matrix):
    high, low = split2(value)
    return dot(high, mean_matrix) + dot(low, mean_matrix)


def normalized(value, mean_matrix):
    center = value - dot(value.astype(BF16), mean_matrix)
    inverse = lax.rsqrt(average(center * center, mean_matrix) + EPS)
    return center * inverse, inverse


def column(row_value, lanes):
    return jnp.transpose(jnp.broadcast_to(row_value, (lanes, row_value.shape[1])))


def place_of(dims):
    return lax.axis_index("seq"), lax.axis_index("res"), lax.axis_index("sub")


def rows_place(dims):
    Z, R, C, rows, parts, width = dims
    z, x, c = place_of(dims)
    block = z // parts
    return c == lax.rem(block, C), x ^ (block // C), lax.rem(z, parts)


def first_kernel(dims, seq_mask_ref, x_ref, u_ref, gain_ref, token_ref, scaled_out, inverse_out, alive_out, gain_out, *shares):
    Z, R, C, rows, parts, width = dims
    channels, columns = x_ref.shape[1:]
    mean_matrix = averaging(channels)
    live = column(token_ref[...].astype(F32), 2 * channels)
    seq_mask = seq_mask_ref[...].astype(F32)
    gain = jnp.concatenate([gain_ref[...].astype(F32)] * 2, axis=1)
    second_half = iota((1, 2 * channels), 1) >= channels
    normed, masked = [], []
    for pair in range(x_ref.shape[0] // 2):
        at = slice(pair * 2 * channels, (pair + 1) * 2 * channels)
        scaled, inverse = normalized(side_by_side(x_ref, pair, channels), mean_matrix)
        scaled_out[:, at] = scaled
        inverse_out[:, at] = inverse
        normed.append((scaled * gain).astype(BF16))
        keep = jnp.where(
            second_half, seq_mask[:, 2 * pair + 1 : 2 * pair + 2], seq_mask[:, 2 * pair : 2 * pair + 1]
        )
        alive = keep * live
        alive_out[:, at] = alive
        masked.append((side_by_side(u_ref, pair, channels) * alive).astype(BF16))
    gain_out[...] = jnp.broadcast_to(gain, gain_out.shape)
    both = jnp.concatenate(
        [jnp.concatenate(normed, axis=1), jnp.concatenate(masked, axis=1)], axis=0
    )
    x = place_of(dims)[1]
    for b, share in enumerate(shares):
        for group in range(R):

            @pl.when(x ^ b == group)
            def _():
                share[...] = both[:, group * width : (group + 1) * width]


def pack_kernel(dims, slim, *refs):
    Z, R, C, rows, parts, width = dims
    held, messages = refs[:R], refs[R:]
    columns = held[0].shape[0] // 2
    for message in messages:
        for b in range(R):
            message[b * columns : (b + 1) * columns] = held[b][0:columns]
    if slim:
        near = rows_place(dims)[1]
        for far, message in enumerate(messages):
            for b in range(R):

                @pl.when(near ^ far == b)
                def _():
                    message[R * columns :] = held[b][columns:]
    else:
        for b in range(R):
            messages[0][(R + b) * columns : (R + b + 1) * columns] = held[b][columns:]


def pick_kernel(dims, slim, count, *refs):
    Z, R, C, rows, parts, width = dims
    messages, picked, relayed = refs[:count], refs[count], refs[count + 1 :]
    for source, target in zip(messages, relayed):
        target[...] = source[...]
    columns = messages[0].shape[0] // (R + 1 if slim else 2 * R)
    _, block, part = rows_place(dims)
    at = pl.multiple_of(block * columns + part * rows, rows)
    for n, message in enumerate(messages):
        picked[n, 0:rows] = message[pl.ds(at, rows)]
        picked[n, rows : 2 * rows] = message[R * columns :] if slim else message[pl.ds(R * columns + at, rows)]


def pair_kernel(heads, block, first, x_ref, moments, squares, centers, token_ref, *refs):
    before, refs = refs[:-6], refs[-6:]
    e_ref, stat_ref, logit_ref, mean_ref, inverse_ref, scratch = refs
    rows, columns, width = e_ref.shape[1], *x_ref.shape[1:]
    groups = block // GROUP
    padding = 1000000000.0 * (token_ref[...].astype(F32) - 1.0)
    lane = iota((rows, columns), 1)

    def step(index, carry):
        low = pl.multiple_of(index * block, block)
        x = x_ref[pl.ds(first + low, block)].reshape(groups, GROUP, columns, width)
        parts, highs, lows = [], [], []
        for g in range(GROUP):
            part = x[:, g].reshape(groups * columns, width)
            value = part.astype(F32)
            high, rest = split2(value * value)
            parts.append(part)
            highs.append(high)
            lows.append(rest)
        product = dot_nt(
            jnp.concatenate(parts + highs + lows, axis=1),
            jnp.concatenate([moments[...], squares[...], squares[...]], axis=1),
        )
        center = centers[...]
        for group in range(groups):
            turned = jnp.transpose(product[group * columns : (group + 1) * columns])
            for g in range(GROUP):
                i = group * GROUP + g
                base = g * SLOTS
                raw = (
                    turned[base : base + heads]
                    + turned[base + heads : base + 2 * heads]
                    + turned[base + 2 * heads : base + 3 * heads]
                )
                total = turned[base + 3 * heads : base + 3 * heads + 1]
                square = turned[base + 3 * heads + 4 : base + 3 * heads + 5]
                mean = total * (1.0 / width)
                upper = total.astype(BF16).astype(F32)
                lower = total - upper
                spread_sum = (square - upper * upper * (1.0 / width)) - (
                    2.0 * upper * lower + lower * lower
                ) * (1.0 / width)
                inverse = lax.rsqrt(jnp.maximum(spread_sum, 0.0) * (1.0 / width) + EPS)
                scratch[pl.ds(pl.multiple_of((low + i) * heads, heads), heads)] = inverse * (raw - mean * center)
                mean_ref[pl.ds(low + i, 1)] = mean
                inverse_ref[pl.ds(low + i, 1)] = inverse
        return carry

    lax.fori_loop(0, rows // block, step, 0, unroll=True)
    stats = jnp.zeros((rows, columns), F32)
    ones = jnp.ones((columns, columns), BF16)
    for h in range(heads):
        logit = scratch[pl.ds(h, rows, stride=heads), :]
        logit_ref[h] = logit
        logit = logit + padding
        peak = jnp.max(logit, axis=1, keepdims=True)
        e = jnp.exp(logit - peak).astype(BF16)
        e_ref[h] = e
        stats = jnp.where(lane == h, peak, stats)
        stats = jnp.where(lane == 3 * heads + h, dot(e, ones), stats)
    high, middle, rest = split3(stats)
    stats = high + pltpu.roll(middle, heads, 1) + pltpu.roll(rest, 2 * heads, 1)
    stat_ref[first:] = stats.astype(BF16)
    for ref in before:
        stat_ref[0:first] = ref[...]


def thirds(value, heads):
    lane = iota(value.shape, 1)
    high, middle, low = split3(jnp.where(lane < heads, value, 0.0))
    return high + pltpu.roll(middle, heads, 1) + pltpu.roll(low, 2 * heads, 1)


def joined_thirds(stats, heads):
    lanes = stats.shape[1]
    return (
        stats
        + pltpu.roll(stats, lanes - heads, 1)
        + pltpu.roll(stats, lanes - 2 * heads, 1)
    )


def attach_kernel(heads, e_ref, own_ref, other_ref, message):
    size = e_ref.shape[1]
    message[0:heads] = e_ref[...]
    both = own_ref[...].astype(F32) + pltpu.roll(other_ref[...].astype(F32), own_ref.shape[1] // 2, 1)
    for n in range(own_ref.shape[0] // size):
        message[heads + n] = both[n * size : (n + 1) * size].astype(BF16)


def attached(message, heads, rows):
    parts = [message[heads + n] for n in range(rows // message.shape[1])]
    both = jnp.concatenate(parts, axis=0).astype(F32)
    return [both, pltpu.roll(both, both.shape[1] // 2, 1)]


def probs_kernel(R, heads, *refs):
    exps, (probs, scales) = refs[: 2 * R], refs[2 * R :]
    rows, columns = scales.shape[1:]
    exps = [exps[2 * b : 2 * b + 2] for b in range(R)]
    stats = [[joined_thirds(s, heads) for s in attached(lower, heads, rows)] for _, lower in exps]
    near = [pair[0] for pair in stats]
    everything = near + [pair[1] for pair in stats]
    peak = functools.reduce(jnp.maximum, everything)
    total = 0.0
    for s in everything:
        total = total + jnp.exp(s - peak) * pltpu.roll(s, s.shape[1] - 3 * heads, 1)
    for b in range(R):
        scale = jnp.exp(near[b] - peak) / total
        scales[b] = scale
        for h in range(heads):
            low = 0
            for e in exps[b]:
                at = slice(low, low + e.shape[1])
                low += e.shape[1]
                weight = e[h].astype(F32) * scale[at, h : h + 1]
                probs[h, at, b * columns : (b + 1) * columns] = weight.astype(BF16)


def quad(refs, q, rows, lanes):
    per = max(lanes // refs[0].shape[-1], 1)
    return jnp.concatenate([refs[q * per + g][rows] for g in range(per)], axis=1)


def prepare_kernel(dims, heads, mine, other, *refs):
    Z, R, C, rows, parts, width = dims
    n = mine.shape[0]
    messages, refs = refs[:n], refs[n:]
    value_ref, gate_ref, output_ref, values, mixed_grad, gates, grads, gathered = refs
    columns = values.shape[1] // R
    lanes, step = value_ref.shape[0], value_ref.shape[1] // heads
    here, _, _ = rows_place(dims)

    @pl.when(here)
    def _():
        gathered[...] = mine[...]

    @pl.when(jnp.logical_not(here))
    def _():
        gathered[...] = other[...]

    planes = [gathered.at[a] for a in range(n)]
    for q in range(n * width // lanes):
        at = slice(q * step, (q + 1) * step)
        gate = jax.nn.sigmoid(dot(quad(planes, q, slice(0, rows), lanes), gate_ref[...]))
        grad = dot(quad(planes, q, slice(rows, 2 * rows), lanes), output_ref[...])
        product = (gate * grad).astype(BF16)
        gates[q] = gate
        grads[q] = grad
        tokens = dot(quad(messages, q, slice(0, R * columns), lanes), value_ref[...]).astype(BF16)
        for h in range(heads):
            mixed_grad[h, :, at] = product[:, h * step : (h + 1) * step]
            values[h, :, at] = tokens[:, h * step : (h + 1) * step]


def work_kernel(dims, heads, values, mixed_grad, gates, grads, probs, value_ref, gate_ref, output_ref, *refs):
    Z, R, C, rows, parts, width = dims
    keep, send, partial, turned = refs
    n = partial.shape[0]
    step = value_ref.shape[1] // heads
    quads = gates.shape[0]
    per = n // quads
    for h in range(heads):
        sums = dot_tn(probs[h], mixed_grad[h]).astype(BF16)
        for q in range(quads):
            turned[q, :, h * step : (h + 1) * step] = sums[:, q * step : (q + 1) * step]
    for q in range(quads):
        sums = dot_nt(turned[q], value_ref[...])
        for g in range(per):
            partial[q * per + g] = sums[:, g * width : (g + 1) * width]
    for q in range(quads):
        at = slice(q * step, (q + 1) * step)
        gate, grad = gates[q], grads[q]
        mixed = jnp.concatenate([dot(probs[h], values[h, :, at]) for h in range(heads)], axis=1)
        gated = mixed * gate
        gate_grad = (grad * gated * (1.0 - gate)).astype(BF16)
        update = dot_nt(gated.astype(BF16), output_ref[...])
        through = dot_nt(gate_grad, gate_ref[...])
        for g in range(per):
            for low, value in ((0, update), (rows, through)):
                value = value[:, g * width : (g + 1) * width]
                keep[q * per + g, low : low + rows] = value
                send[q * per + g, low : low + rows] = value.astype(BF16)


def finish_kernel(dims, keep, received, partial, *messages):
    Z, R, C, rows, parts, width = dims
    n, tall, _ = partial.shape
    here, block, part = rows_place(dims)
    at = pl.multiple_of(block * (tall // R) + part * rows, rows)
    for a, message in enumerate(messages):
        message[0:tall] = partial[a].astype(BF16)

        @pl.when(here)
        def _():
            both = keep[a] + received[a].astype(F32)
            message[tall:] = both[0:rows].astype(BF16)
            message[pl.ds(at, rows)] = (partial[a, pl.ds(at, rows)] + both[rows:]).astype(BF16)


def first_heads(heads):
    return heads * 5 // 8


def scores_kernel(R, heads, count, *refs):
    mixed_grads, refs = refs[:count], refs[count:]
    values, refs = refs[:count], refs[count:]
    scales, *refs = refs
    exps, refs = refs[: 2 * R], refs[2 * R :]
    own_scores, total_ref, *messages = refs
    half = first_heads(heads)
    rows, columns = total_ref.shape
    lane = iota((rows, columns), 1)
    sums = jnp.zeros((rows, columns), F32)
    for h in range(heads):
        scores = dot_nt(
            jnp.concatenate([g[h] for g in mixed_grads], axis=1),
            jnp.concatenate([v[h] for v in values], axis=1),
        )
        total = 0.0
        for b in range(R):
            part = scores[:, b * columns : (b + 1) * columns]
            if b == 0:
                own_scores[h] = part
            else:
                part = part.astype(BF16)
                messages[2 * b - 2 + h // half][h % half] = part
                part = part.astype(F32)
            weight = jnp.concatenate([e[h] for e in exps[2 * b : 2 * b + 2]], axis=0)
            weight = weight.astype(F32) * scales[b][:, h : h + 1]
            total = total + jnp.sum(weight * part, axis=1, keepdims=True)
        for t, part in enumerate(split3(total)):
            sums = jnp.where(lane == t * heads + h, part, sums)
    total_ref[...] = sums.astype(BF16)


def attach_total_kernel(heads, scores_ref, own_ref, other_ref, message):
    count, rows, columns = scores_ref.shape
    for h in range(count):
        message[h * rows : (h + 1) * rows] = scores_ref[h]
    total = sum(joined_thirds(ref[...].astype(F32), heads) for ref in (own_ref, other_ref))
    total = thirds(total, heads)
    packed, size = 0.0, message.shape[0] - count * rows
    for n in range(rows // size):
        part = total[n * size : (n + 1) * size]
        packed = packed + (pltpu.roll(part, n * TOTAL_LANES, 1) if n else part)
    message[count * rows :] = packed.astype(BF16)


def pair_back_kernel(R, heads, first, x_ref, e_ref, logit_ref, mean_ref, inverse_ref, scale_ref, own_ref, back_ref, *refs):
    own_total, received, refs = refs[0], refs[1 : 2 * R - 1], refs[2 * R - 1 :]
    firsts, seconds, half = received[::2], received[1::2], first_heads(heads)
    out_ref, done_ref, scratch, turned, rounded = refs
    count, columns, width = out_ref.shape
    here = pl.ds(pl.multiple_of(pl.program_id(0) * count, count), count)
    low = pl.multiple_of(first + pl.program_id(0) * count, count)
    at = pl.ds(low, count)
    done_ref[...] = jnp.zeros_like(done_ref)
    rows = own_ref.shape[1]
    total = sum(m[(heads - half) * rows :].astype(F32) for m in (own_total, *seconds))
    lanes = total.shape[1]
    total = pltpu.roll(total, lax.rem(lanes - low // count * TOTAL_LANES, lanes), 1)
    total = joined_thirds(total, heads)
    scale = scale_ref[0, at]
    inverse = inverse_ref[here]
    cross = 0.0
    for h in range(heads):
        scores = own_ref[h, at]
        for m in firsts if h < half else ():
            scores = scores + m[h, at].astype(F32)
        for m in () if h < half else seconds:
            scores = scores + m[pl.ds(pl.multiple_of((h - half) * rows + low, count), count)].astype(F32)
        prob = e_ref[h, here].astype(F32) * scale[:, h : h + 1]
        grad = prob * (scores - total[:, h : h + 1])
        cross = cross + grad * logit_ref[h, here]
        scratch[pl.ds(h, count, stride=BACK_SLOTS), :] = grad * inverse
    factor = inverse * inverse * cross * (1.0 / width)
    rest = [*split3(factor * mean_ref[here]), factor]
    rest += [jnp.zeros_like(factor)] * (BACK_SLOTS - heads - len(rest))
    for t, part in enumerate(rest):
        scratch[pl.ds(heads + t, count, stride=BACK_SLOTS), :] = part
    groups = count // BACK_GROUP
    size = BACK_GROUP * BACK_SLOTS
    for group in range(groups):
        rows = slice(group * columns, (group + 1) * columns)
        tile = jnp.transpose(scratch[group * size : (group + 1) * size])
        turned[rows] = tile
        rounded[rows] = tile.astype(BF16)
    for g in range(0, BACK_GROUP, 2):
        product = dot(rounded[...], back_ref[:, g * width : (g + 2) * width])
        for group in range(groups):
            rows = slice(group * columns, (group + 1) * columns)
            for s in range(2):
                i = group * BACK_GROUP + g + s
                lane = (g + s) * BACK_SLOTS + heads + 3
                slope = turned[rows, lane : lane + 1] * x_ref[low + i].astype(F32)
                out_ref[i] = (product[rows, s * width : (s + 1) * width] - slope).astype(BF16)


def settle_kernel(out):
    out[...] = jnp.zeros_like(out)


def gather_kernel(one, other, total):
    at = slice(0, total.shape[0])
    total[...] = one[at].astype(F32) + other[at].astype(F32)


def fold_kernel(dims, sums, *refs):
    Z, R, C, rows, parts, width = dims
    messages, refs = refs[:Z], refs[Z:]
    early, shares = refs[:-R], refs[-R:]
    columns = shares[0].shape[0] // 2
    z, x, c = place_of(dims)
    for b, share in enumerate(shares):
        at = slice(b * columns, (b + 1) * columns)
        total = sum(m[at].astype(F32) for a, m in enumerate(messages) if a not in sums)
        share[0:columns] = sum((m[at] for m in early), total).astype(BF16)
        for part in range(parts):
            plane = ((x ^ b) * C + c) * parts + part
            for a, message in enumerate(messages):

                @pl.when(plane ^ z == a)
                def _():
                    share[columns + part * rows : columns + (part + 1) * rows] = message[R * columns :]


def last_kernel(dims, scaled_ref, inverse_ref, alive_ref, gain_ref, *refs):
    Z, R, C, rows, parts, width = dims
    shares, refs = refs[:R], refs[R:]
    update_ref, grad_ref, updates, through = refs
    channels, columns = grad_ref.shape[1:]
    x = place_of(dims)[1]
    for b, share in enumerate(shares):
        at = pl.multiple_of((x ^ b) * width, width)
        through[:, pl.ds(at, width)] = share[0:columns].astype(F32)
        updates[:, pl.ds(at, width)] = share[columns:].astype(F32)
    mean_matrix = averaging(channels)
    gain = gain_ref[0:1]
    for pair in range(grad_ref.shape[0] // 2):
        at = slice(pair * 2 * channels, (pair + 1) * 2 * channels)
        scaled = scaled_ref[:, at]
        grad = through[:, at] * gain
        grad = inverse_ref[:, at] * (
            grad - average(grad, mean_matrix) - scaled * average(grad * scaled, mean_matrix)
        )
        grad = jnp.transpose(grad).astype(BF16)
        update = jnp.transpose(updates[:, at] * alive_ref[:, at]).astype(BF16)
        for s in range(2):
            at = slice(s * channels, (s + 1) * channels)
            grad_ref[2 * pair + s] = grad[at]
            update_ref[2 * pair + s] = update[at]


def shards(
    Z, R, C,
    alignment_input, pair_features, update_cotangent, alignment_norm_gain, pair_norm_gain,
    value_matrix, gate_matrix, output_matrix, head_bias_matrix, sequence_mask, token_padding_mask,
):
    sequences, columns, channels = alignment_input.shape
    rows, _, pair_width = pair_features.shape
    heads = head_bias_matrix.shape[1]
    hidden = value_matrix.shape[1]
    depth = hidden // heads
    parts = columns // rows
    width = sequences // R * channels
    lanes = QUAD * channels
    step = QUAD * depth
    dims = (Z, R, C, rows, parts, width)
    slim = (Z, R, C, parts) == (4, 2, 2, 1)
    everyone = ("seq", "res", "sub")

    def exchange(value, dz=0, dx=0, dc=0):
        at = lambda z, x, c: (z * R + x) * C + c
        places = [(z, x, c) for z in range(Z) for x in range(R) for c in range(C)]
        return lax.ppermute(value, everyone, [(at(z, x, c), at(z ^ dz, x ^ dx, c ^ dc)) for z, x, c in places])

    in_hbm = lambda value: pltpu.with_memory_space_constraint(value, pltpu.HBM)

    gain = in_hbm(alignment_norm_gain.reshape(1, channels))
    by_channel = lambda value: jnp.swapaxes(value, 1, 2)
    alignment_turned = in_hbm(by_channel(alignment_input))
    token_row = in_hbm(token_padding_mask.reshape(1, columns))
    seq_mask = in_hbm(sequence_mask.reshape(1, sequences))
    share = shape((2 * columns, width), BF16)

    kept = shape((columns, sequences * channels), F32)
    scaled, inverse, alive, wide_gain, *held = call(
        functools.partial(first_kernel, dims),
        [kept] * 3 + [shape((8, 2 * channels), F32)] + [share] * R,
        "first",
        operands=(seq_mask, alignment_turned, in_hbm(by_channel(update_cotangent)), gain, token_row),
    )
    first_kept = held[0]
    held = [held[0]] + [exchange(m, dx=b) for b, m in enumerate(held) if b]
    tall = R * columns + (rows if slim else R * columns)

    def pack(after):
        return call(
            functools.partial(pack_kernel, dims, slim),
            [shape((tall, width), BF16)] * (2 if slim else 1),
            "pack",
            operands=held,
            after=after,
        )

    spread_value, spread_gate, spread_output, moments, squares, centers, back = call(
        functools.partial(weights_kernel, depth),
        [shape((lanes, hidden * QUAD), BF16)] * 3
        + [shape((GROUP * SLOTS, GROUP * pair_width), BF16)] * 2
        + [shape((heads, pair_width), F32), shape((BACK_GROUP * BACK_SLOTS, BACK_GROUP * pair_width), BF16)],
        "weights",
        operands=(
            in_hbm(value_matrix), in_hbm(gate_matrix), in_hbm(output_matrix.T), in_hbm(head_bias_matrix.T),
            in_hbm(pair_norm_gain.reshape(1, pair_width)),
        ),
    )

    block = rows // 4
    cuts = ((0, 2 * block), (2 * block, 2 * block))
    def pair(index, before=(), after=()):
        first, size = cuts[index]
        return call(
            functools.partial(pair_kernel, heads, block, first),
            [
                shape((heads, size, columns), BF16),
                shape((first + size, columns), BF16),
                shape((heads, size, columns), F32),
                shape((size, columns), F32),
                shape((size, columns), F32),
            ],
            "pair",
            operands=(pair_features, moments, squares, centers, token_row, *before),
            scratch=[pltpu.VMEM((size * heads, columns), F32)],
            after=after,
        )

    upper, stats, *upper_kept = pair(0, after=[first_kept])
    packed = pack(after=[stats])
    if slim:
        near, away = packed
        arrived = {0: near, 2: exchange(away, dz=2), 1: exchange(near, dz=1)}
    else:
        arrived, stride = {0: packed[0]}, Z // 2
        while stride:
            arrived |= {a ^ stride: exchange(m, dz=stride) for a, m in arrived.items()}
            stride //= 2
    lower, stats, *lower_kept = pair(1, before=[stats], after=packed[:1])
    forward = [(upper, *upper_kept), (lower, *lower_kept)]
    uppers = [upper] + [exchange(upper, dx=b) for b in range(1, R)]
    (lower,) = call(
        functools.partial(attach_kernel, heads),
        [shape((heads + rows // lower.shape[1], *lower.shape[1:]), BF16)],
        "attach",
        operands=(lower, stats, exchange(stats, dc=1)),
        after=uppers[1:],
    )
    lowers = [lower] + [exchange(lower, dx=b) for b in range(1, R)]
    exps = [e for pair_of in zip(uppers, lowers) for e in pair_of]
    phases = [(2,), (0,), (1,), (3,)] if slim else [tuple(range(Z))]
    prepared, unfinished, outgoing = {}, {}, {}

    def pick(phase, relays=0, after=()):
        return call(
            functools.partial(pick_kernel, dims, slim, len(phase)),
            [shape((len(phase), 2 * rows, width), BF16)] + [shape((tall, width), BF16)] * relays,
            "pick",
            after=after,
            operands=[arrived[a] for a in phase],
        )

    def prepare(phase, picked, after=()):
        n = len(phase)
        quads = n * width // lanes
        prepared[phase] = call(
            functools.partial(prepare_kernel, dims, heads),
            [
                shape((heads, R * columns, quads * step), BF16),
                shape((heads, rows, quads * step), BF16),
                shape((quads, rows, heads * step), F32),
                shape((quads, rows, heads * step), F32),
            ],
            "prepare",
            operands=(
                picked, exchange(picked, dc=1), *[arrived[a] for a in phase],
                spread_value, spread_gate, spread_output,
            ),
            scratch=[pltpu.VMEM((n, 2 * rows, width), BF16)],
            after=after,
        )

    def work(phase, after=()):
        n = len(phase)
        keep, send, partial = call(
            functools.partial(work_kernel, dims, heads),
            [
                shape((n, 2 * rows, width), F32),
                shape((n, 2 * rows, width), BF16),
                shape((n, R * columns, width), F32),
            ],
            "work",
            operands=(*prepared[phase], probs, spread_value, spread_gate, spread_output),
            scratch=[pltpu.VMEM((n * width // lanes, R * columns, heads * step), BF16)],
            after=after,
        )
        unfinished[phase] = keep, exchange(send, dc=1), partial

    def finish(phase, after=()):
        finished = call(
            functools.partial(finish_kernel, dims),
            [shape((R * columns + rows, width), BF16)] * len(phase),
            "finish",
            operands=unfinished[phase],
            after=after,
        )
        outgoing.update(zip(phase, finished))

    early_phases = phases[:3]
    first_picked, *relayed = pick(phases[0], relays=int(slim), after=[lower, *arrived.values()][:3 if slim else 1])
    prepare(phases[0], first_picked)
    if slim:
        arrived[3] = exchange(relayed[0], dz=1)
    for phase in early_phases[1:]:
        prepare(phase, *pick(phase, after=[first_picked]))
    probs, scales = call(
        functools.partial(probs_kernel, R, heads),
        [shape((heads, rows, R * columns), BF16), shape((R, rows, columns), F32)],
        "probs",
        operands=exps,
        after=[prepared[phase][1] for phase in early_phases[:2]],
    )

    work(phases[0])
    if slim:
        work((1,))
        finish((2,), after=[unfinished[(1,)][2]])
        (picked,) = pick((3,), after=[outgoing[2]])
        work((0,), after=[picked])
        prepare((3,), picked, after=[unfinished[(0,)][2]])
    else:
        finish(phases[0])

    own_scores, own_total, *scores = call(
        functools.partial(scores_kernel, R, heads, len(prepared)),
        [shape((heads, rows, columns), F32), shape((rows, columns), BF16)]
        + [
            shape((count, rows, columns), BF16)
            for _ in range(R - 1)
            for count in (first_heads(heads), heads - first_heads(heads))
        ],
        "scores",
        after=[],
        operands=(
            *[p[1] for p in prepared.values()], *[p[0] for p in prepared.values()], scales, *exps,
        ),
    )
    other_total = exchange(own_total, dc=1)
    received = []
    for b in range(1, R):
        upper, lower = scores[2 * b - 2 : 2 * b]
        (lower,) = call(
            functools.partial(attach_total_kernel, heads),
            [shape(((heads - first_heads(heads)) * rows + rows // 4, columns), BF16)],
            "attach",
            operands=(lower, own_total, other_total),
        )
        received += [exchange(upper, dx=b), exchange(lower, dx=b)]
    if slim:
        work((3,), after=[])
        finish((3,))
        finish((1,), after=[unfinished[(3,)][2]])
        finish((0,))
    received = [lower, *received]
    collected = [exchange(outgoing[a], dz=a) if a else outgoing[a] for a in range(Z)]

    def pair_back(index, into=None, after=()):
        first, part_rows = cuts[index]
        return call(
            functools.partial(pair_back_kernel, R, heads, first),
            [shape(pair_features.shape, BF16), shape((8, 128), F32)],
            "pair_back",
            operands=(pair_features, *forward[index], scales, own_scores, back, *received),
            scratch=[
                pltpu.VMEM((block * BACK_SLOTS, columns), F32),
                pltpu.VMEM((block // BACK_GROUP * columns, BACK_GROUP * BACK_SLOTS), F32),
                pltpu.VMEM((block // BACK_GROUP * columns, BACK_GROUP * BACK_SLOTS), BF16),
            ],
            grid=(part_rows // block,),
            out_specs=[
                pl.BlockSpec((block, columns, pair_width), lambda i: (first // block + i, 0, 0)),
                pl.BlockSpec((8, 128), lambda i: (0, 0)),
            ],
            into=into,
            after=after,
        )

    sums, early = (), []
    if slim:
        sums = (0, 2)
        early = call(
            gather_kernel,
            [shape((R * columns, width), F32)],
            "gather",
            operands=[collected[a] for a in sums],
        )
    settled = call(settle_kernel, [shape((8, 128), F32)], "settle", operands=[], after=received[1:])
    pair_gradient, done = pair_back(0, after=[*settled, *early])
    shares = call(
        functools.partial(fold_kernel, dims, sums),
        [share] * R,
        "fold",
        operands=(*collected, *early),
        after=[done],
    )
    pair_gradient, _ = pair_back(1, into=pair_gradient, after=[shares[0]])
    shares = [shares[0]] + [exchange(m, dx=b) for b, m in enumerate(shares) if b]
    alignment_update, alignment_gradient = call(
        functools.partial(last_kernel, dims),
        [shape(alignment_turned.shape, BF16)] * 2,
        "last",
        operands=(scaled, inverse, alive, wide_gain, *shares),
        scratch=[pltpu.VMEM((columns, R * width), F32)] * 2,
    )
    return by_channel(alignment_update), by_channel(alignment_gradient), pair_gradient


def solution(mesh):
    split = P(("groups", "seq"), ("res", "sub"), None)
    sizes = (mesh.shape["seq"], mesh.shape["res"], mesh.shape["sub"])
    return jax.shard_map(
        functools.partial(shards, *sizes),
        mesh=mesh,
        in_specs=(split, split, split, P(), P(), P(), P(), P(), P())
        + (P(("groups", "seq")), P(("groups", "res", "sub"))),
        out_specs=(split, split, split),
        check_vma=False,
    )
```

```python
import functools

import jax
import jax.numpy as jnp
from jax import lax
from jax.experimental import pallas as pl
from jax.experimental.pallas import tpu as pltpu
from jax.sharding import PartitionSpec as P

F32 = jnp.float32
BF16 = jnp.bfloat16
EPS = 1e-05
QUAD = 4
GROUP = 4
SLOTS = 32
BACK_SLOTS = 16
BACK_GROUP = 8
TOTAL_LANES = 32
COST = dict(first=1.5, pack=0.1, weights=1.3, pair=2.5, attach=0, pick=0, probs=0, prepare=0, work=0.0, scores=0.0, finish=0, pair_back=0, gather=5, settle=5, fold=0, last=0)
VMEM = 20 * 1024 * 1024


def dot(a, b):
    return jnp.dot(a, b, preferred_element_type=F32)


def dot_nt(a, b):
    return lax.dot_general(a, b, (((1,), (1,)), ((), ())), preferred_element_type=F32)


def dot_tn(a, b):
    return lax.dot_general(a, b, (((0,), (0,)), ((), ())), preferred_element_type=F32)


def iota(shape, dim):
    return lax.broadcasted_iota(jnp.int32, shape, dim)


def split3(value):
    high = value.astype(BF16).astype(F32)
    rest = value - high
    middle = rest.astype(BF16).astype(F32)
    return high, middle, rest - middle


def split2(value):
    high = value.astype(BF16)
    return high, (value - high.astype(F32)).astype(BF16)


def call(kernel, out_shape, name, operands, scratch=(), after=(), grid=None, out_specs=None, into=None):
    whole = pl.BlockSpec(memory_space=pltpu.VMEM)
    count = len(operands)
    body = lambda *refs: kernel(*refs[:count], *refs[count + len(after) :])
    extra = {} if grid is None else {"grid": grid}
    if into is not None:
        extra["input_output_aliases"] = {count + len(after): 0}
        after = [*after, into]
    return pl.pallas_call(
        body,
        out_shape=out_shape,
        in_specs=[whole] * count + [pl.BlockSpec(memory_space=pl.ANY)] * len(after),
        out_specs=out_specs or [whole] * len(out_shape),
        scratch_shapes=list(scratch),
        compiler_params=pltpu.CompilerParams(vmem_limit_bytes=VMEM),
        cost_estimate=pl.CostEstimate(flops=int(COST[name] * 3e9), bytes_accessed=0, transcendentals=0),
        name=name,
        **extra,
    )(*operands, *after)


def shape(dims, dtype):
    return jax.ShapeDtypeStruct(tuple(dims), dtype)


def spread(matrix, channels, depth):
    hidden = matrix.shape[1]
    wide = hidden * QUAD
    row, col = iota((hidden, wide), 0), iota((hidden, wide), 1)
    pick = (row // depth == col // (depth * QUAD)) & (row % depth == col % depth)
    placed = dot(matrix, pick.astype(F32).astype(BF16))
    tall = jnp.concatenate([placed] * QUAD, axis=0)
    row, col = iota(tall.shape, 0), iota(tall.shape, 1)
    return jnp.where(row // channels == (col // depth) % QUAD, tall, 0.0).astype(BF16)


def weights_kernel(
    depth, value_ref, gate_ref, output_ref, bias_ref, gain_ref,
    spread_value, spread_gate, spread_output, moments, squares, centers, back,
):
    channels = value_ref.shape[0]
    spread_value[...] = spread(value_ref[...], channels, depth)
    spread_gate[...] = spread(gate_ref[...], channels, depth)
    spread_output[...] = spread(output_ref[...], channels, depth)
    scaled = bias_ref[...].astype(F32) * gain_ref[...].astype(F32)
    heads, width = scaled.shape
    total = jnp.sum(scaled, axis=1, keepdims=True)
    centers[...] = jnp.broadcast_to(total, (heads, width))
    high, middle, low = split3(scaled)
    tail = (SLOTS - 3 * heads, width)
    row = iota(tail, 0)
    slots = jnp.concatenate([high, middle, low, jnp.where(row < 4, 1.0, 0.0)], axis=0)
    square_slots = jnp.concatenate(
        [jnp.zeros((3 * heads, width), F32), jnp.where(row >= 4, 1.0, 0.0)], axis=0
    )

    def diagonal(tile):
        copies = GROUP * SLOTS // tile.shape[0]
        tall = jnp.concatenate([tile] * copies, axis=0)
        full = jnp.concatenate([tall] * copies, axis=1)
        row, col = iota(full.shape, 0), iota(full.shape, 1)
        return jnp.where(row // tile.shape[0] == col // tile.shape[1], full, 0.0).astype(BF16)

    moments[...] = diagonal(slots)
    squares[...] = diagonal(square_slots)
    row = iota((BACK_SLOTS - heads, width), 0)
    back[...] = diagonal(
        jnp.concatenate([scaled - total * (1.0 / width), jnp.where(row < 3, 1.0, 0.0)], axis=0)
    )


def side_by_side(ref, pair, channels):
    both = jnp.concatenate([ref[2 * pair], ref[2 * pair + 1]], axis=0)
    return jnp.transpose(both.astype(F32))


def averaging(channels):
    row, col = iota((2 * channels, 2 * channels), 0), iota((2 * channels, 2 * channels), 1)
    return jnp.where(row // channels == col // channels, 1.0 / channels, 0.0).astype(BF16)


def average(value, mean_matrix):
    high, low = split2(value)
    return dot(high, mean_matrix) + dot(low, mean_matrix)


def normalized(value, mean_matrix):
    center = value - dot(value.astype(BF16), mean_matrix)
    inverse = lax.rsqrt(average(center * center, mean_matrix) + EPS)
    return center * inverse, inverse


def column(row_value, lanes):
    return jnp.transpose(jnp.broadcast_to(row_value, (lanes, row_value.shape[1])))


def place_of(dims):
    return lax.axis_index("seq"), lax.axis_index("res"), lax.axis_index("sub")


def rows_place(dims):
    Z, R, C, rows, parts, width = dims
    z, x, c = place_of(dims)
    block = z // parts
    return c == lax.rem(block, C), x ^ (block // C), lax.rem(z, parts)


def first_kernel(dims, seq_mask_ref, x_ref, u_ref, gain_ref, token_ref, scaled_out, inverse_out, alive_out, gain_out, *shares):
    Z, R, C, rows, parts, width = dims
    channels, columns = x_ref.shape[1:]
    mean_matrix = averaging(channels)
    live = column(token_ref[...].astype(F32), 2 * channels)
    seq_mask = seq_mask_ref[...].astype(F32)
    gain = jnp.concatenate([gain_ref[...].astype(F32)] * 2, axis=1)
    second_half = iota((1, 2 * channels), 1) >= channels
    normed, masked = [], []
    for pair in range(x_ref.shape[0] // 2):
        at = slice(pair * 2 * channels, (pair + 1) * 2 * channels)
        scaled, inverse = normalized(side_by_side(x_ref, pair, channels), mean_matrix)
        scaled_out[:, at] = scaled
        inverse_out[:, at] = inverse
        normed.append((scaled * gain).astype(BF16))
        keep = jnp.where(
            second_half, seq_mask[:, 2 * pair + 1 : 2 * pair + 2], seq_mask[:, 2 * pair : 2 * pair + 1]
        )
        alive = keep * live
        alive_out[:, at] = alive
        masked.append((side_by_side(u_ref, pair, channels) * alive).astype(BF16))
    gain_out[...] = jnp.broadcast_to(gain, gain_out.shape)
    both = jnp.concatenate(
        [jnp.concatenate(normed, axis=1), jnp.concatenate(masked, axis=1)], axis=0
    )
    x = place_of(dims)[1]
    for b, share in enumerate(shares):
        for group in range(R):

            @pl.when(x ^ b == group)
            def _():
                share[...] = both[:, group * width : (group + 1) * width]


def pack_kernel(dims, slim, *refs):
    Z, R, C, rows, parts, width = dims
    held, messages = refs[:R], refs[R:]
    columns = held[0].shape[0] // 2
    for message in messages:
        for b in range(R):
            message[b * columns : (b + 1) * columns] = held[b][0:columns]
    if slim:
        near = rows_place(dims)[1]
        for far, message in enumerate(messages):
            for b in range(R):

                @pl.when(near ^ far == b)
                def _():
                    message[R * columns :] = held[b][columns:]
    else:
        for b in range(R):
            messages[0][(R + b) * columns : (R + b + 1) * columns] = held[b][columns:]


def pick_kernel(dims, slim, count, *refs):
    Z, R, C, rows, parts, width = dims
    messages, picked, relayed = refs[:count], refs[count], refs[count + 1 :]
    for source, target in zip(messages, relayed):
        target[...] = source[...]
    columns = messages[0].shape[0] // (R + 1 if slim else 2 * R)
    _, block, part = rows_place(dims)
    at = pl.multiple_of(block * columns + part * rows, rows)
    for n, message in enumerate(messages):
        picked[n, 0:rows] = message[pl.ds(at, rows)]
        picked[n, rows : 2 * rows] = message[R * columns :] if slim else message[pl.ds(R * columns + at, rows)]


def pair_kernel(heads, block, first, x_ref, moments, squares, centers, token_ref, *refs):
    before, refs = refs[:-6], refs[-6:]
    e_ref, stat_ref, logit_ref, mean_ref, inverse_ref, scratch = refs
    rows, columns, width = e_ref.shape[1], *x_ref.shape[1:]
    groups = block // GROUP
    padding = 1000000000.0 * (token_ref[...].astype(F32) - 1.0)
    lane = iota((rows, columns), 1)

    def step(index, carry):
        low = pl.multiple_of(index * block, block)
        x = x_ref[pl.ds(first + low, block)].reshape(groups, GROUP, columns, width)
        parts, highs, lows = [], [], []
        for g in range(GROUP):
            part = x[:, g].reshape(groups * columns, width)
            value = part.astype(F32)
            high, rest = split2(value * value)
            parts.append(part)
            highs.append(high)
            lows.append(rest)
        product = dot_nt(
            jnp.concatenate(parts + highs + lows, axis=1),
            jnp.concatenate([moments[...], squares[...], squares[...]], axis=1),
        )
        center = centers[...]
        for group in range(groups):
            turned = jnp.transpose(product[group * columns : (group + 1) * columns])
            for g in range(GROUP):
                i = group * GROUP + g
                base = g * SLOTS
                raw = (
                    turned[base : base + heads]
                    + turned[base + heads : base + 2 * heads]
                    + turned[base + 2 * heads : base + 3 * heads]
                )
                total = turned[base + 3 * heads : base + 3 * heads + 1]
                square = turned[base + 3 * heads + 4 : base + 3 * heads + 5]
                mean = total * (1.0 / width)
                upper = total.astype(BF16).astype(F32)
                lower = total - upper
                spread_sum = (square - upper * upper * (1.0 / width)) - (
                    2.0 * upper * lower + lower * lower
                ) * (1.0 / width)
                inverse = lax.rsqrt(jnp.maximum(spread_sum, 0.0) * (1.0 / width) + EPS)
                scratch[pl.ds(pl.multiple_of((low + i) * heads, heads), heads)] = inverse * (raw - mean * center)
                mean_ref[pl.ds(low + i, 1)] = mean
                inverse_ref[pl.ds(low + i, 1)] = inverse
        return carry

    lax.fori_loop(0, rows // block, step, 0, unroll=True)
    stats = jnp.zeros((rows, columns), F32)
    ones = jnp.ones((columns, columns), BF16)
    for h in range(heads):
        logit = scratch[pl.ds(h, rows, stride=heads), :]
        logit_ref[h] = logit
        logit = logit + padding
        peak = jnp.max(logit, axis=1, keepdims=True)
        e = jnp.exp(logit - peak).astype(BF16)
        e_ref[h] = e
        stats = jnp.where(lane == h, peak, stats)
        stats = jnp.where(lane == 3 * heads + h, dot(e, ones), stats)
    high, middle, rest = split3(stats)
    stats = high + pltpu.roll(middle, heads, 1) + pltpu.roll(rest, 2 * heads, 1)
    stat_ref[first:] = stats.astype(BF16)
    for ref in before:
        stat_ref[0:first] = ref[...]


def thirds(value, heads):
    lane = iota(value.shape, 1)
    high, middle, low = split3(jnp.where(lane < heads, value, 0.0))
    return high + pltpu.roll(middle, heads, 1) + pltpu.roll(low, 2 * heads, 1)


def joined_thirds(stats, heads):
    lanes = stats.shape[1]
    return (
        stats
        + pltpu.roll(stats, lanes - heads, 1)
        + pltpu.roll(stats, lanes - 2 * heads, 1)
    )


def attach_kernel(heads, e_ref, own_ref, other_ref, message):
    size = e_ref.shape[1]
    message[0:heads] = e_ref[...]
    both = own_ref[...].astype(F32) + pltpu.roll(other_ref[...].astype(F32), own_ref.shape[1] // 2, 1)
    for n in range(own_ref.shape[0] // size):
        message[heads + n] = both[n * size : (n + 1) * size].astype(BF16)


def attached(message, heads, rows):
    parts = [message[heads + n] for n in range(rows // message.shape[1])]
    both = jnp.concatenate(parts, axis=0).astype(F32)
    return [both, pltpu.roll(both, both.shape[1] // 2, 1)]


def probs_kernel(R, heads, *refs):
    exps, (probs, scales) = refs[: 2 * R], refs[2 * R :]
    rows, columns = scales.shape[1:]
    exps = [exps[2 * b : 2 * b + 2] for b in range(R)]
    stats = [[joined_thirds(s, heads) for s in attached(lower, heads, rows)] for _, lower in exps]
    near = [pair[0] for pair in stats]
    everything = near + [pair[1] for pair in stats]
    peak = functools.reduce(jnp.maximum, everything)
    total = 0.0
    for s in everything:
        total = total + jnp.exp(s - peak) * pltpu.roll(s, s.shape[1] - 3 * heads, 1)
    for b in range(R):
        scale = jnp.exp(near[b] - peak) / total
        scales[b] = scale
        for h in range(heads):
            low = 0
            for e in exps[b]:
                at = slice(low, low + e.shape[1])
                low += e.shape[1]
                weight = e[h].astype(F32) * scale[at, h : h + 1]
                probs[h, at, b * columns : (b + 1) * columns] = weight.astype(BF16)


def quad(refs, q, rows, lanes):
    per = max(lanes // refs[0].shape[-1], 1)
    return jnp.concatenate([refs[q * per + g][rows] for g in range(per)], axis=1)


def prepare_kernel(dims, heads, mine, other, *refs):
    Z, R, C, rows, parts, width = dims
    n = mine.shape[0]
    messages, refs = refs[:n], refs[n:]
    value_ref, gate_ref, output_ref, values, mixed_grad, gates, grads, gathered = refs
    columns = values.shape[1] // R
    lanes, step = value_ref.shape[0], value_ref.shape[1] // heads
    here, _, _ = rows_place(dims)

    @pl.when(here)
    def _():
        gathered[...] = mine[...]

    @pl.when(jnp.logical_not(here))
    def _():
        gathered[...] = other[...]

    planes = [gathered.at[a] for a in range(n)]
    for q in range(n * width // lanes):
        at = slice(q * step, (q + 1) * step)
        gate = jax.nn.sigmoid(dot(quad(planes, q, slice(0, rows), lanes), gate_ref[...]))
        grad = dot(quad(planes, q, slice(rows, 2 * rows), lanes), output_ref[...])
        product = (gate * grad).astype(BF16)
        gates[q] = gate
        grads[q] = grad
        tokens = dot(quad(messages, q, slice(0, R * columns), lanes), value_ref[...]).astype(BF16)
        for h in range(heads):
            mixed_grad[h, :, at] = product[:, h * step : (h + 1) * step]
            values[h, :, at] = tokens[:, h * step : (h + 1) * step]


def work_kernel(dims, heads, values, mixed_grad, gates, grads, probs, value_ref, gate_ref, output_ref, *refs):
    Z, R, C, rows, parts, width = dims
    keep, send, partial, turned = refs
    n = partial.shape[0]
    step = value_ref.shape[1] // heads
    quads = gates.shape[0]
    per = n // quads
    for h in range(heads):
        sums = dot_tn(probs[h], mixed_grad[h]).astype(BF16)
        for q in range(quads):
            turned[q, :, h * step : (h + 1) * step] = sums[:, q * step : (q + 1) * step]
    for q in range(quads):
        sums = dot_nt(turned[q], value_ref[...])
        for g in range(per):
            partial[q * per + g] = sums[:, g * width : (g + 1) * width]
    for q in range(quads):
        at = slice(q * step, (q + 1) * step)
        gate, grad = gates[q], grads[q]
        mixed = jnp.concatenate([dot(probs[h], values[h, :, at]) for h in range(heads)], axis=1)
        gated = mixed * gate
        gate_grad = (grad * gated * (1.0 - gate)).astype(BF16)
        update = dot_nt(gated.astype(BF16), output_ref[...])
        through = dot_nt(gate_grad, gate_ref[...])
        for g in range(per):
            for low, value in ((0, update), (rows, through)):
                value = value[:, g * width : (g + 1) * width]
                keep[q * per + g, low : low + rows] = value
                send[q * per + g, low : low + rows] = value.astype(BF16)


def finish_kernel(dims, keep, received, partial, *messages):
    Z, R, C, rows, parts, width = dims
    n, tall, _ = partial.shape
    here, block, part = rows_place(dims)
    at = pl.multiple_of(block * (tall // R) + part * rows, rows)
    for a, message in enumerate(messages):
        message[0:tall] = partial[a].astype(BF16)

        @pl.when(here)
        def _():
            both = keep[a] + received[a].astype(F32)
            message[tall:] = both[0:rows].astype(BF16)
            message[pl.ds(at, rows)] = (partial[a, pl.ds(at, rows)] + both[rows:]).astype(BF16)


def first_heads(heads):
    return heads * 6 // 8


def scores_kernel(R, heads, count, *refs):
    mixed_grads, refs = refs[:count], refs[count:]
    values, refs = refs[:count], refs[count:]
    scales, *refs = refs
    exps, refs = refs[: 2 * R], refs[2 * R :]
    own_scores, total_ref, *messages = refs
    half = first_heads(heads)
    rows, columns = total_ref.shape
    lane = iota((rows, columns), 1)
    sums = jnp.zeros((rows, columns), F32)
    for h in range(heads):
        scores = dot_nt(
            jnp.concatenate([g[h] for g in mixed_grads], axis=1),
            jnp.concatenate([v[h] for v in values], axis=1),
        )
        total = 0.0
        for b in range(R):
            part = scores[:, b * columns : (b + 1) * columns]
            if b == 0:
                own_scores[h] = part
            else:
                part = part.astype(BF16)
                messages[2 * b - 2 + h // half][h % half] = part
                part = part.astype(F32)
            weight = jnp.concatenate([e[h] for e in exps[2 * b : 2 * b + 2]], axis=0)
            weight = weight.astype(F32) * scales[b][:, h : h + 1]
            total = total + jnp.sum(weight * part, axis=1, keepdims=True)
        for t, part in enumerate(split3(total)):
            sums = jnp.where(lane == t * heads + h, part, sums)
    total_ref[...] = sums.astype(BF16)


def attach_total_kernel(heads, scores_ref, own_ref, other_ref, message):
    count, rows, columns = scores_ref.shape
    for h in range(count):
        message[h * rows : (h + 1) * rows] = scores_ref[h]
    total = sum(joined_thirds(ref[...].astype(F32), heads) for ref in (own_ref, other_ref))
    total = thirds(total, heads)
    packed, size = 0.0, message.shape[0] - count * rows
    for n in range(rows // size):
        part = total[n * size : (n + 1) * size]
        packed = packed + (pltpu.roll(part, n * TOTAL_LANES, 1) if n else part)
    message[count * rows :] = packed.astype(BF16)


def pair_back_kernel(R, heads, first, x_ref, e_ref, logit_ref, mean_ref, inverse_ref, scale_ref, own_ref, back_ref, *refs):
    own_total, received, refs = refs[0], refs[1 : 2 * R - 1], refs[2 * R - 1 :]
    firsts, seconds, half = received[::2], received[1::2], first_heads(heads)
    out_ref, done_ref, scratch, turned, rounded = refs
    count, columns, width = out_ref.shape
    here = pl.ds(pl.multiple_of(pl.program_id(0) * count, count), count)
    low = pl.multiple_of(first + pl.program_id(0) * count, count)
    at = pl.ds(low, count)
    done_ref[...] = jnp.zeros_like(done_ref)
    rows = own_ref.shape[1]
    total = sum(m[(heads - half) * rows :].astype(F32) for m in (own_total, *seconds))
    lanes = total.shape[1]
    total = pltpu.roll(total, lax.rem(lanes - low // count * TOTAL_LANES, lanes), 1)
    total = joined_thirds(total, heads)
    scale = scale_ref[0, at]
    inverse = inverse_ref[here]
    cross = 0.0
    for h in range(heads):
        scores = own_ref[h, at]
        for m in firsts if h < half else ():
            scores = scores + m[h, at].astype(F32)
        for m in () if h < half else seconds:
            scores = scores + m[pl.ds(pl.multiple_of((h - half) * rows + low, count), count)].astype(F32)
        prob = e_ref[h, here].astype(F32) * scale[:, h : h + 1]
        grad = prob * (scores - total[:, h : h + 1])
        cross = cross + grad * logit_ref[h, here]
        scratch[pl.ds(h, count, stride=BACK_SLOTS), :] = grad * inverse
    factor = inverse * inverse * cross * (1.0 / width)
    rest = [*split3(factor * mean_ref[here]), factor]
    rest += [jnp.zeros_like(factor)] * (BACK_SLOTS - heads - len(rest))
    for t, part in enumerate(rest):
        scratch[pl.ds(heads + t, count, stride=BACK_SLOTS), :] = part
    groups = count // BACK_GROUP
    size = BACK_GROUP * BACK_SLOTS
    for group in range(groups):
        rows = slice(group * columns, (group + 1) * columns)
        tile = jnp.transpose(scratch[group * size : (group + 1) * size])
        turned[rows] = tile
        rounded[rows] = tile.astype(BF16)
    for g in range(0, BACK_GROUP, 2):
        product = dot(rounded[...], back_ref[:, g * width : (g + 2) * width])
        for group in range(groups):
            rows = slice(group * columns, (group + 1) * columns)
            for s in range(2):
                i = group * BACK_GROUP + g + s
                lane = (g + s) * BACK_SLOTS + heads + 3
                slope = turned[rows, lane : lane + 1] * x_ref[low + i].astype(F32)
                out_ref[i] = (product[rows, s * width : (s + 1) * width] - slope).astype(BF16)


def settle_kernel(out):
    out[...] = jnp.zeros_like(out)


def gather_kernel(one, other, total):
    at = slice(0, total.shape[0])
    total[...] = one[at].astype(F32) + other[at].astype(F32)


def fold_kernel(dims, sums, *refs):
    Z, R, C, rows, parts, width = dims
    messages, refs = refs[:Z], refs[Z:]
    early, shares = refs[:-R], refs[-R:]
    columns = shares[0].shape[0] // 2
    z, x, c = place_of(dims)
    for b, share in enumerate(shares):
        at = slice(b * columns, (b + 1) * columns)
        total = sum(m[at].astype(F32) for a, m in enumerate(messages) if a not in sums)
        share[0:columns] = sum((m[at] for m in early), total).astype(BF16)
        for part in range(parts):
            plane = ((x ^ b) * C + c) * parts + part
            for a, message in enumerate(messages):

                @pl.when(plane ^ z == a)
                def _():
                    share[columns + part * rows : columns + (part + 1) * rows] = message[R * columns :]


def last_kernel(dims, scaled_ref, inverse_ref, alive_ref, gain_ref, *refs):
    Z, R, C, rows, parts, width = dims
    shares, refs = refs[:R], refs[R:]
    update_ref, grad_ref, updates, through = refs
    channels, columns = grad_ref.shape[1:]
    x = place_of(dims)[1]
    for b, share in enumerate(shares):
        at = pl.multiple_of((x ^ b) * width, width)
        through[:, pl.ds(at, width)] = share[0:columns].astype(F32)
        updates[:, pl.ds(at, width)] = share[columns:].astype(F32)
    mean_matrix = averaging(channels)
    gain = gain_ref[0:1]
    for pair in range(grad_ref.shape[0] // 2):
        at = slice(pair * 2 * channels, (pair + 1) * 2 * channels)
        scaled = scaled_ref[:, at]
        grad = through[:, at] * gain
        grad = inverse_ref[:, at] * (
            grad - average(grad, mean_matrix) - scaled * average(grad * scaled, mean_matrix)
        )
        grad = jnp.transpose(grad).astype(BF16)
        update = jnp.transpose(updates[:, at] * alive_ref[:, at]).astype(BF16)
        for s in range(2):
            at = slice(s * channels, (s + 1) * channels)
            grad_ref[2 * pair + s] = grad[at]
            update_ref[2 * pair + s] = update[at]


def shards(
    Z, R, C,
    alignment_input, pair_features, update_cotangent, alignment_norm_gain, pair_norm_gain,
    value_matrix, gate_matrix, output_matrix, head_bias_matrix, sequence_mask, token_padding_mask,
):
    sequences, columns, channels = alignment_input.shape
    rows, _, pair_width = pair_features.shape
    heads = head_bias_matrix.shape[1]
    hidden = value_matrix.shape[1]
    depth = hidden // heads
    parts = columns // rows
    width = sequences // R * channels
    lanes = QUAD * channels
    step = QUAD * depth
    dims = (Z, R, C, rows, parts, width)
    slim = (Z, R, C, parts) == (4, 2, 2, 1)
    everyone = ("seq", "res", "sub")

    def exchange(value, dz=0, dx=0, dc=0):
        at = lambda z, x, c: (z * R + x) * C + c
        places = [(z, x, c) for z in range(Z) for x in range(R) for c in range(C)]
        return lax.ppermute(value, everyone, [(at(z, x, c), at(z ^ dz, x ^ dx, c ^ dc)) for z, x, c in places])

    in_hbm = lambda value: pltpu.with_memory_space_constraint(value, pltpu.HBM)

    gain = in_hbm(alignment_norm_gain.reshape(1, channels))
    by_channel = lambda value: jnp.swapaxes(value, 1, 2)
    alignment_turned = in_hbm(by_channel(alignment_input))
    token_row = in_hbm(token_padding_mask.reshape(1, columns))
    seq_mask = in_hbm(sequence_mask.reshape(1, sequences))
    share = shape((2 * columns, width), BF16)

    kept = shape((columns, sequences * channels), F32)
    scaled, inverse, alive, wide_gain, *held = call(
        functools.partial(first_kernel, dims),
        [kept] * 3 + [shape((8, 2 * channels), F32)] + [share] * R,
        "first",
        operands=(seq_mask, alignment_turned, in_hbm(by_channel(update_cotangent)), gain, token_row),
    )
    first_kept = held[0]
    held = [held[0]] + [exchange(m, dx=b) for b, m in enumerate(held) if b]
    tall = R * columns + (rows if slim else R * columns)

    def pack(after):
        return call(
            functools.partial(pack_kernel, dims, slim),
            [shape((tall, width), BF16)] * (2 if slim else 1),
            "pack",
            operands=held,
            after=after,
        )

    spread_value, spread_gate, spread_output, moments, squares, centers, back = call(
        functools.partial(weights_kernel, depth),
        [shape((lanes, hidden * QUAD), BF16)] * 3
        + [shape((GROUP * SLOTS, GROUP * pair_width), BF16)] * 2
        + [shape((heads, pair_width), F32), shape((BACK_GROUP * BACK_SLOTS, BACK_GROUP * pair_width), BF16)],
        "weights",
        operands=(
            in_hbm(value_matrix), in_hbm(gate_matrix), in_hbm(output_matrix.T), in_hbm(head_bias_matrix.T),
            in_hbm(pair_norm_gain.reshape(1, pair_width)),
        ),
    )

    block = rows // 4
    cuts = ((0, 2 * block), (2 * block, 2 * block))
    def pair(index, before=(), after=()):
        first, size = cuts[index]
        return call(
            functools.partial(pair_kernel, heads, block, first),
            [
                shape((heads, size, columns), BF16),
                shape((first + size, columns), BF16),
                shape((heads, size, columns), F32),
                shape((size, columns), F32),
                shape((size, columns), F32),
            ],
            "pair",
            operands=(pair_features, moments, squares, centers, token_row, *before),
            scratch=[pltpu.VMEM((size * heads, columns), F32)],
            after=after,
        )

    upper, stats, *upper_kept = pair(0, after=[first_kept])
    packed = pack(after=[stats])
    if slim:
        near, away = packed
        arrived = {0: near, 2: exchange(away, dz=2), 1: exchange(near, dz=1)}
    else:
        arrived, stride = {0: packed[0]}, Z // 2
        while stride:
            arrived |= {a ^ stride: exchange(m, dz=stride) for a, m in arrived.items()}
            stride //= 2
    lower, stats, *lower_kept = pair(1, before=[stats], after=packed[:1])
    forward = [(upper, *upper_kept), (lower, *lower_kept)]
    uppers = [upper] + [exchange(upper, dx=b) for b in range(1, R)]
    (lower,) = call(
        functools.partial(attach_kernel, heads),
        [shape((heads + rows // lower.shape[1], *lower.shape[1:]), BF16)],
        "attach",
        operands=(lower, stats, exchange(stats, dc=1)),
        after=uppers[1:],
    )
    lowers = [lower] + [exchange(lower, dx=b) for b in range(1, R)]
    exps = [e for pair_of in zip(uppers, lowers) for e in pair_of]
    phases = [(2,), (0,), (1,), (3,)] if slim else [tuple(range(Z))]
    prepared, unfinished, outgoing = {}, {}, {}

    def pick(phase, relays=0, after=()):
        return call(
            functools.partial(pick_kernel, dims, slim, len(phase)),
            [shape((len(phase), 2 * rows, width), BF16)] + [shape((tall, width), BF16)] * relays,
            "pick",
            after=after,
            operands=[arrived[a] for a in phase],
        )

    def prepare(phase, picked, after=()):
        n = len(phase)
        quads = n * width // lanes
        prepared[phase] = call(
            functools.partial(prepare_kernel, dims, heads),
            [
                shape((heads, R * columns, quads * step), BF16),
                shape((heads, rows, quads * step), BF16),
                shape((quads, rows, heads * step), F32),
                shape((quads, rows, heads * step), F32),
            ],
            "prepare",
            operands=(
                picked, exchange(picked, dc=1), *[arrived[a] for a in phase],
                spread_value, spread_gate, spread_output,
            ),
            scratch=[pltpu.VMEM((n, 2 * rows, width), BF16)],
            after=after,
        )

    def work(phase, after=()):
        n = len(phase)
        keep, send, partial = call(
            functools.partial(work_kernel, dims, heads),
            [
                shape((n, 2 * rows, width), F32),
                shape((n, 2 * rows, width), BF16),
                shape((n, R * columns, width), F32),
            ],
            "work",
            operands=(*prepared[phase], probs, spread_value, spread_gate, spread_output),
            scratch=[pltpu.VMEM((n * width // lanes, R * columns, heads * step), BF16)],
            after=after,
        )
        unfinished[phase] = keep, exchange(send, dc=1), partial

    def finish(phase, after=()):
        finished = call(
            functools.partial(finish_kernel, dims),
            [shape((R * columns + rows, width), BF16)] * len(phase),
            "finish",
            operands=unfinished[phase],
            after=after,
        )
        outgoing.update(zip(phase, finished))

    early_phases = phases[:3]
    first_picked, *relayed = pick(phases[0], relays=int(slim), after=[lower, *arrived.values()][:3 if slim else 1])
    prepare(phases[0], first_picked)
    if slim:
        arrived[3] = exchange(relayed[0], dz=1)
    for phase in early_phases[1:]:
        prepare(phase, *pick(phase, after=[first_picked]))
    probs, scales = call(
        functools.partial(probs_kernel, R, heads),
        [shape((heads, rows, R * columns), BF16), shape((R, rows, columns), F32)],
        "probs",
        operands=exps,
        after=[prepared[phase][1] for phase in early_phases[:2]],
    )

    work(phases[0])
    if slim:
        work((1,))
        finish((2,), after=[unfinished[(1,)][2]])
        (picked,) = pick((3,), after=[outgoing[2]])
        work((0,), after=[picked])
        prepare((3,), picked, after=[unfinished[(0,)][2]])
    else:
        finish(phases[0])

    own_scores, own_total, *scores = call(
        functools.partial(scores_kernel, R, heads, len(prepared)),
        [shape((heads, rows, columns), F32), shape((rows, columns), BF16)]
        + [
            shape((count, rows, columns), BF16)
            for _ in range(R - 1)
            for count in (first_heads(heads), heads - first_heads(heads))
        ],
        "scores",
        after=[],
        operands=(
            *[p[1] for p in prepared.values()], *[p[0] for p in prepared.values()], scales, *exps,
        ),
    )
    other_total = exchange(own_total, dc=1)
    received = []
    for b in range(1, R):
        upper, lower = scores[2 * b - 2 : 2 * b]
        (lower,) = call(
            functools.partial(attach_total_kernel, heads),
            [shape(((heads - first_heads(heads)) * rows + rows // 4, columns), BF16)],
            "attach",
            operands=(lower, own_total, other_total),
        )
        received += [exchange(upper, dx=b), exchange(lower, dx=b)]
    if slim:
        work((3,), after=[])
        finish((3,))
        finish((1,), after=[unfinished[(3,)][2]])
        finish((0,))
    received = [lower, *received]
    collected = [exchange(outgoing[a], dz=a) if a else outgoing[a] for a in range(Z)]

    def pair_back(index, into=None, after=()):
        first, part_rows = cuts[index]
        return call(
            functools.partial(pair_back_kernel, R, heads, first),
            [shape(pair_features.shape, BF16), shape((8, 128), F32)],
            "pair_back",
            operands=(pair_features, *forward[index], scales, own_scores, back, *received),
            scratch=[
                pltpu.VMEM((block * BACK_SLOTS, columns), F32),
                pltpu.VMEM((block // BACK_GROUP * columns, BACK_GROUP * BACK_SLOTS), F32),
                pltpu.VMEM((block // BACK_GROUP * columns, BACK_GROUP * BACK_SLOTS), BF16),
            ],
            grid=(part_rows // block,),
            out_specs=[
                pl.BlockSpec((block, columns, pair_width), lambda i: (first // block + i, 0, 0)),
                pl.BlockSpec((8, 128), lambda i: (0, 0)),
            ],
            into=into,
            after=after,
        )

    sums, early = (), []
    if slim:
        sums = (0, 2)
        early = call(
            gather_kernel,
            [shape((R * columns, width), F32)],
            "gather",
            operands=[collected[a] for a in sums],
        )
    settled = call(settle_kernel, [shape((8, 128), F32)], "settle", operands=[], after=received[1:])
    pair_gradient, done = pair_back(0, after=[*settled, *early])
    shares = call(
        functools.partial(fold_kernel, dims, sums),
        [share] * R,
        "fold",
        operands=(*collected, *early),
        after=[done],
    )
    pair_gradient, _ = pair_back(1, into=pair_gradient, after=[shares[0]])
    shares = [shares[0]] + [exchange(m, dx=b) for b, m in enumerate(shares) if b]
    alignment_update, alignment_gradient = call(
        functools.partial(last_kernel, dims),
        [shape(alignment_turned.shape, BF16)] * 2,
        "last",
        operands=(scaled, inverse, alive, wide_gain, *shares),
        scratch=[pltpu.VMEM((columns, R * width), F32)] * 2,
    )
    return by_channel(alignment_update), by_channel(alignment_gradient), pair_gradient


def solution(mesh):
    split = P(("groups", "seq"), ("res", "sub"), None)
    sizes = (mesh.shape["seq"], mesh.shape["res"], mesh.shape["sub"])
    return jax.shard_map(
        functools.partial(shards, *sizes),
        mesh=mesh,
        in_specs=(split, split, split, P(), P(), P(), P(), P(), P())
        + (P(("groups", "seq")), P(("groups", "res", "sub"))),
        out_specs=(split, split, split),
        check_vma=False,
    )
```
